128 devices in a mesh: roll: 16 (over z, y_hi, core), kvh: 8 (over y_lo, x).
Axes of the slice: x: 4, y: 4 (y_hi: 2, y_lo: 2; y = y_hi * 2 + y_lo), z: 4, core: 2. Of those that a mesh axis runs over, the one named last changes fastest.
Arguments:
- out_grad: bfloat16 [16, 256, 5120], P('roll', 'kvh'), may hold values from -48 to 48
- out_weight: bfloat16 [8, 5, 128, 5120], P('kvh'), may hold values from -0.078125 to 0.078125
- queries: bfloat16 [16, 256, 8, 5, 128], P('roll', None, 'kvh'), may hold values from -16 to 16
- keys_new: bfloat16 [16, 256, 8, 128], P('roll', None, 'kvh'), may hold values from -16 to 16
- values_new: bfloat16 [16, 256, 8, 128], P('roll', None, 'kvh'), may hold values from -6 to 6
- keys_prompt: bfloat16 [4096, 8, 128], P('roll', 'kvh'), may hold values from -6 to 6
- values_prompt: bfloat16 [4096, 8, 128], P('roll', 'kvh'), may hold values from -6 to 6
- offsets: int32 [16], P('roll'), may hold values from 0 to 3840
Outputs:
- grad_queries: bfloat16 [16, 256, 8, 5, 128], P('roll', None, 'kvh')
- grad_keys_new: bfloat16 [16, 256, 8, 128], P('roll', None, 'kvh')
- grad_values_new: bfloat16 [16, 256, 8, 128], P('roll', None, 'kvh')
- grad_keys_prompt: bfloat16 [4096, 8, 128], P('roll', 'kvh')
- grad_values_prompt: bfloat16 [4096, 8, 128], P('roll', 'kvh')
The draws below stay inside these ranges and needn't reach their ends.
Inputs may be any that keep to these rules, and one draw needn't show every extreme that they name: `offsets`: each slice lies inside a response of 4096 tokens.
All inputs are finite; a program needn't handle non-finite values.
Results may differ from the reference program's by a relative error of at most 0.015.
The reference program's roundings to bfloat16 on the way (of `attn_grad`, `query_rot`, `key_rot`, `attn_probs` and `score_grad`) count: a program that leaves them out, or rounds other values in their place, can miss the bound.
Values may be sent and summed in bfloat16 or wider, within the bound.
A program may use at most 64 MiB of HBM per device.

```python
import jax
import jax.numpy as jnp
from jax import lax

D = 5120
HD = 128
QG = 5
KVH = 8
ROLLOUTS = 16
SEQ = 256
PROMPT = 4096
RESP = 4096


def draw_queries(key, part):
    full_shape = (ROLLOUTS, SEQ, KVH, QG, HD)
    noise_key = jax.random.fold_in(key, 17)
    bulk_values = jnp.clip(2.0 * jax.random.normal(noise_key, full_shape, jnp.float32), -12.0, 12.0)
    return bulk_values.astype(jnp.bfloat16)


def draw_keys_new(key, part):
    full_shape = (ROLLOUTS, SEQ, KVH, HD)
    noise_key = jax.random.fold_in(key, 29)
    bulk_values = jnp.clip(jax.random.normal(noise_key, full_shape, jnp.float32), -6.0, 6.0)
    return bulk_values.astype(jnp.bfloat16)


def with_ends(result, rng, low, top_value):
    extent = result.shape
    index_at = [jax.random.randint(jax.random.fold_in(rng, axis), (), 0, extent[axis]) for axis in range(len(extent))]
    result = result.at[tuple(index_at)].set(low)
    longest = extent.index(max(extent))
    index_at[longest] = (index_at[longest] + 1) % extent[longest]
    return result.at[tuple(index_at)].set(top_value)


def shard_levels(stream_key, dims, cuts, low, high):
    level, own = 1.0, jax.random.fold_in(stream_key, 6)
    for axis_at, blocks in cuts:
        draws = jnp.exp(jax.random.uniform(jax.random.fold_in(own, axis_at), (blocks,), jnp.float32, low / len(cuts), high / len(cuts)))
        level = level * jnp.repeat(draws, dims[axis_at] // blocks).reshape([-1 if axis == axis_at else 1 for axis in range(len(dims))])
    return level


def centred(own_key, extent, spread, reach, cuts=(), held_as=jnp.bfloat16):
    array = spread * jax.random.normal(own_key, extent, jnp.float32)
    if cuts:
        array = array * shard_levels(own_key, extent, cuts, -0.22, 0.18)
    return jnp.clip(array, -reach, reach).astype(held_as)


def setup_inputs(seed: int = 0) -> dict:
    key_list = jax.random.split(jax.random.key(seed), 9)
    out_grad = centred(key_list[0], (ROLLOUTS, SEQ, D), 8.0, 48.0, ((0, 16), (1, 8)))
    out_weight = centred(key_list[1], (KVH, QG, HD, D), D ** -0.5, 0.078125, ((0, 8),))
    queries = draw_queries(jax.random.fold_in(key_list[8], 71), 0)
    keys_new = draw_keys_new(jax.random.fold_in(key_list[8], 71), 0)
    values_new = centred(key_list[4], (ROLLOUTS, SEQ, KVH, HD), 1.0, 6.0, ((0, 16), (2, 8)))
    keys_prompt = centred(key_list[5], (PROMPT, KVH, HD), 1.0, 6.0, ((0, 16), (1, 8)))
    values_prompt = centred(key_list[6], (PROMPT, KVH, HD), 1.0, 6.0, ((0, 16), (1, 8)))
    offsets = with_ends(jax.random.randint(key_list[7], (ROLLOUTS,), 0, RESP - SEQ + 1), jax.random.fold_in(key_list[7], 1), 0, RESP - SEQ).astype(jnp.int32)
    return {"out_grad": out_grad, "out_weight": out_weight, "queries": queries, "keys_new": keys_new, "values_new": values_new, "keys_prompt": keys_prompt, "values_prompt": values_prompt, "offsets": offsets}


theta_base = 1000000.0


def rotation(positions, head_width):
    half_width = head_width // 2
    frequency = jnp.power(theta_base, -(jnp.arange(half_width, dtype=jnp.float32) / half_width))
    angles = positions.astype(jnp.float32)[:, None] * frequency[None, :]
    return jnp.cos(angles), jnp.sin(angles)


def rotate(vectors, cos_part, sin_part, direction):
    half_width = vectors.shape[-1] // 2
    front_half = vectors[..., :half_width]
    back_half = vectors[..., half_width:]
    return jnp.concatenate([front_half * cos_part - direction * back_half * sin_part, back_half * cos_part + direction * front_half * sin_part], axis=-1)


def one_pair(query_head, key_new, value_new, key_prompt, value_prompt, grad_head, cos_part, sin_part):
    seq_len, group_size, head_width = query_head.shape
    prompt_len = key_prompt.shape[0]
    score_scale = head_width ** -0.5
    query_rot = rotate(query_head.astype(jnp.float32), cos_part[:, None, :], sin_part[:, None, :], 1.0).astype(jnp.bfloat16)
    key_rot = rotate(key_new.astype(jnp.float32), cos_part, sin_part, 1.0).astype(jnp.bfloat16)
    all_keys = jnp.concatenate([key_prompt, key_rot], axis=0)
    all_values = jnp.concatenate([value_prompt, value_new], axis=0)
    query_rows = query_rot.reshape(seq_len * group_size, head_width)
    grad_rows = grad_head.reshape(seq_len * group_size, head_width)
    scores = jnp.dot(query_rows, all_keys.T, preferred_element_type=jnp.float32) * score_scale
    column = jnp.arange(prompt_len + seq_len)[None, :]
    row_pos = (jnp.arange(seq_len * group_size) // group_size)[:, None]
    allowed = (column < prompt_len) | (column - prompt_len <= row_pos)
    scores = jnp.where(allowed, scores, -jnp.inf)
    row_max = jnp.max(scores, axis=1, keepdims=True)
    log_total = row_max + jnp.log(jnp.sum(jnp.exp(scores - row_max), axis=1, keepdims=True))
    attn_probs = jnp.exp(scores - log_total).astype(jnp.bfloat16)
    output = jnp.dot(attn_probs, all_values, preferred_element_type=jnp.float32)
    row_delta = jnp.sum(grad_rows.astype(jnp.float32) * output, axis=1, keepdims=True)
    prob_grad = jnp.dot(grad_rows, all_values.T, preferred_element_type=jnp.float32)
    score_grad = (attn_probs.astype(jnp.float32) * (prob_grad - row_delta) * score_scale).astype(jnp.bfloat16)
    query_grad = jnp.dot(score_grad, all_keys, preferred_element_type=jnp.float32).reshape(seq_len, group_size, head_width)
    query_grad = rotate(query_grad, cos_part[:, None, :], sin_part[:, None, :], -1.0).astype(jnp.bfloat16)
    key_grad = jnp.dot(score_grad.T, query_rows, preferred_element_type=jnp.float32)
    value_grad = jnp.dot(attn_probs.T, grad_rows, preferred_element_type=jnp.float32)
    key_new_grad = rotate(key_grad[prompt_len:], cos_part, sin_part, -1.0).astype(jnp.bfloat16)
    return query_grad, key_new_grad, value_grad[prompt_len:].astype(jnp.bfloat16), key_grad[:prompt_len], value_grad[:prompt_len]


def reference(out_grad, out_weight, queries, keys_new, values_new, keys_prompt, values_prompt, offsets):
    attn_grad = jnp.einsum("rsc,ghdc->rsghd", out_grad.astype(jnp.float32), out_weight.astype(jnp.float32)).astype(jnp.bfloat16)

    def roll_step(totals, slices):
        query_roll, key_roll, value_roll, grad_roll, first_pos = slices
        positions = PROMPT + first_pos + jnp.arange(SEQ, dtype=jnp.int32)
        cos_part, sin_part = rotation(positions, HD)

        def head_step(pieces):
            return one_pair(pieces[0], pieces[1], pieces[2], pieces[3], pieces[4], pieces[5], cos_part, sin_part)

        stacked = (jnp.moveaxis(query_roll, 1, 0), jnp.moveaxis(key_roll, 1, 0), jnp.moveaxis(value_roll, 1, 0), jnp.moveaxis(keys_prompt, 1, 0), jnp.moveaxis(values_prompt, 1, 0), jnp.moveaxis(grad_roll, 1, 0))
        query_grad, key_grad, value_grad, prompt_key, prompt_value = lax.map(head_step, stacked)
        totals = (totals[0] + jnp.moveaxis(prompt_key, 0, 1), totals[1] + jnp.moveaxis(prompt_value, 0, 1))
        return totals, (jnp.moveaxis(query_grad, 0, 1), jnp.moveaxis(key_grad, 0, 1), jnp.moveaxis(value_grad, 0, 1))

    zero_sums = jnp.zeros((PROMPT, KVH, HD), jnp.float32)
    sums, grads = lax.scan(roll_step, (zero_sums, zero_sums), (queries, keys_new, values_new, attn_grad, offsets))
    return grads[0], grads[1], grads[2], sums[0].astype(jnp.bfloat16), sums[1].astype(jnp.bfloat16)
```

```python
import functools
import math

import jax
import jax.numpy as jnp
import numpy as np
from jax import lax
from jax.experimental import pallas as pl
from jax.experimental.pallas import tpu as pltpu
from jax.sharding import PartitionSpec as P

MESH = pl.DeviceIdType.MESH
f32 = jnp.float32
bf16 = jnp.bfloat16

HEADS = 5
SEQ = 256
HD = 128
ROWS = HEADS * SEQ
HALF = ROWS // 2
BLK = 256
WIDTH = 5120
PROMPT = 4096
CHUNK = 32
SCALE = HD ** -0.5
SCALE2 = SCALE * math.log2(math.e)
PAIRS = 8


def dot(a, b):
    return lax.dot_general(a, b, (((1,), (0,)), ((), ())), preferred_element_type=f32)


def dot_nt(a, b):
    return lax.dot_general(a, b, (((1,), (1,)), ((), ())), preferred_element_type=f32)


def kernel(
    og_hbm, w_hbm, q_hbm, kn_hbm, vn_hbm, kp_hbm, vp_hbm, off_ref, freq_ref,
    dq_ref, dkn_ref, dvn_ref, dkp_ref, dvp_ref,
    w_v, do_v, kb, vb, q_v, kn_v, qt, qp, dot_t, dop, s_v, p_v, o_t, dq_t, m_v, l_v, delta_v,
    cos_v, sin_v, ds_v, ag_v, csend, crecv, zs, zr,
    lsem, ksend, vsend, kfw, vfw, krecv, vrecv, dsend, drecv, cs_sem, cr_sem, zs_sem, zr_sem,
):
    roll = lax.axis_index("roll")
    kvh = lax.axis_index("kvh")
    zz, yh, cc = roll // 4, (roll // 2) % 2, roll % 2
    yl, xx = kvh // 4, kvh % 4

    def dev(dz=0, dyh=0, dc=0, dyl=0, dx=0):
        r = (((zz + dz) % 4) * 2 + (yh + dyh) % 2) * 2 + (cc + dc) % 2
        k = ((yl + dyl) % 2) * 4 + (xx + dx) % 4
        return (r, k)

    core, yhp = dev(dc=1), dev(dyh=1)
    zp, zm, z2 = dev(dz=1), dev(dz=3), dev(dz=2)
    ylp, xp, xm = dev(dyl=1), dev(dx=1), dev(dx=3)

    barrier = pltpu.get_barrier_semaphore()
    for d in (core, yhp, zp, zm, z2, ylp, xp, xm):
        pl.semaphore_signal(barrier, 1, device_id=d, device_id_type=MESH)

    local = [
        pltpu.make_async_copy(kp_hbm, kb.at[15], lsem.at[0]),
        pltpu.make_async_copy(vp_hbm, vb.at[15], lsem.at[1]),
        pltpu.make_async_copy(q_hbm, q_v, lsem.at[2]),
        pltpu.make_async_copy(kn_hbm, kn_v, lsem.at[3]),
        pltpu.make_async_copy(vn_hbm, vb.at[16], lsem.at[4]),
        pltpu.make_async_copy(og_hbm, do_v.at[pl.ds(0, CHUNK)], lsem.at[5]),
        pltpu.make_async_copy(w_hbm, w_v, lsem.at[6]),
    ]
    for c in local:
        c.start()

    pl.semaphore_wait(barrier, 8)

    def remote(src, dst, ssem, rsem, d):
        return pltpu.make_async_remote_copy(
            src_ref=src, dst_ref=dst, send_sem=ssem, recv_sem=rsem, device_id=d, device_id_type=MESH
        )

    first_hops = ((13, yhp), (11, zp), (9, zm), (3, z2), (14, core))
    relay_hops = ((7, zp), (5, zm), (1, z2))

    def kv_own(src, buf, ssem, rsem):
        return [remote(src, buf.at[s], ssem.at[i], rsem.at[s], d) for i, (s, d) in enumerate(first_hops)]

    def kv_relay(buf, ssem, rsem):
        return [
            remote(buf.at[13], buf.at[s], ssem.at[5 + i], rsem.at[s], d) for i, (s, d) in enumerate(relay_hops)
        ]

    def kv_forward(buf, fsem, rsem, n):
        return remote(buf.at[2 * n + 1], buf.at[2 * n], fsem.at[n], rsem.at[2 * n], core)

    def kv_arrived(buf, rsem, ssem, s):
        remote(buf.at[s], buf.at[s], ssem.at[0], rsem.at[s], core).wait_recv()

    for c in kv_own(kp_hbm, kb, ksend, krecv):
        c.start()
    for c in kv_own(vp_hbm, vb, vsend, vrecv):
        c.start()

    def rows(slot, lo=0, size=CHUNK):
        return do_v.at[pl.ds(slot * CHUNK + lo, size)]

    do_own = [
        remote(og_hbm, rows(1), dsend.at[0], drecv.at[0], ylp),
        remote(og_hbm, rows(3), dsend.at[1], drecv.at[1], xp),
        remote(og_hbm, rows(2), dsend.at[2], drecv.at[2], xm),
    ]
    do_relay = [
        remote(rows(3, 0, 16), rows(4, 0, 16), dsend.at[3], drecv.at[3], xp),
        remote(rows(2, 16, 16), rows(4, 16, 16), dsend.at[4], drecv.at[4], xm),
        remote(rows(1), rows(6), dsend.at[5], drecv.at[5], xp),
        remote(rows(1), rows(5), dsend.at[6], drecv.at[6], xm),
        remote(rows(4, 0, 16), rows(7, 0, 16), dsend.at[7], drecv.at[7], ylp),
        remote(rows(4, 16, 16), rows(7, 16, 16), dsend.at[8], drecv.at[8], ylp),
    ]
    for c in do_own:
        c.start()

    def kof(dyl, dx):
        return ((yl + dyl) % 2) * 4 + (xx + dx) % 4

    chunks = [kof(0, 0), kof(1, 0), kof(0, 1), kof(0, 3), kof(0, 2), kof(1, 1), kof(1, 3), kof(1, 2)]

    pos = (off_ref[0] + PROMPT + lax.broadcasted_iota(jnp.int32, (SEQ, HD), 0)).astype(f32)
    angle = pos * freq_ref[...]
    cos_v[...] = jnp.cos(angle)
    lane = lax.broadcasted_iota(jnp.int32, (SEQ, HD), 1)
    sin_a = jnp.sin(angle)
    sin_v[...] = jnp.where(lane < HD // 2, -sin_a, sin_a)

    for i in (2, 3, 4):
        local[i].wait()
    kn = kn_v[...].astype(f32)
    kb[16] = (kn * cos_v[...] + pltpu.roll(kn, HD // 2, 1) * sin_v[...]).astype(bf16)
    for p in range(2):
        for h in range(HEADS):
            parts = []
            for j in range(4):
                k = chunks[4 * p + j]
                x = q_v[pl.ds(pl.multiple_of(h * SEQ + k * CHUNK, CHUNK), CHUNK), :].astype(f32)
                at = pl.ds(pl.multiple_of(k * CHUNK, CHUNK), CHUNK)
                parts.append((x * cos_v[at, :] + pltpu.roll(x, HD // 2, 1) * sin_v[at, :]))
            tile = jnp.concatenate(parts, axis=0)
            qt[:, pl.ds((p * HEADS + h) * HD, HD)] = tile.T.astype(bf16)

    tl = lax.broadcasted_iota(jnp.int32, (1, HD), 1)

    def tokens(p):
        which = tl // CHUNK
        base = jnp.where(
            which == 0,
            chunks[4 * p],
            jnp.where(which == 1, chunks[4 * p + 1], jnp.where(which == 2, chunks[4 * p + 2], chunks[4 * p + 3])),
        )
        return base * CHUNK + tl % CHUNK

    key_at = lax.broadcasted_iota(jnp.int32, (BLK, HD), 0)
    for p in range(2):
        allowed = key_at <= tokens(p)
        for h in range(HEADS):
            at = pl.ds((p * HEADS + h) * HD, HD)
            s = jnp.where(allowed, dot(kb[16], qt[:, at]), -1e30)
            s_v[16, :, at] = s
            m_v[:, at] = jnp.max(s, axis=0, keepdims=True)

    local[0].wait()

    def scores_of(slot):
        kblk = kb[slot]
        for c in range(ROWS // 256):
            at = pl.ds(c * 256, 256)
            s = dot(kblk, qt[:, at])
            s_v[slot, :, at] = s
            m_v[:, at] = jnp.maximum(m_v[:, at], jnp.max(s, axis=0, keepdims=True))

    def score_step(i, carry):
        n = PAIRS - 1 - i

        @pl.when(n < PAIRS - 1)
        def _():
            kv_arrived(kb, krecv, ksend, 2 * n + 1)
            kv_forward(kb, kfw, krecv, n).start()

        @pl.when(n == PAIRS - 2)
        def _():
            for c in kv_relay(kb, ksend, krecv):
                c.start()

        scores_of(2 * n + 1)
        kv_arrived(kb, krecv, ksend, 2 * n)
        scores_of(2 * n)
        return carry

    lax.fori_loop(0, PAIRS, score_step, 0)

    do_own[1].wait_recv()
    do_relay[0].start()
    do_own[2].wait_recv()
    do_relay[1].start()
    do_own[0].wait_recv()
    do_relay[2].start()
    do_relay[3].start()

    def output_of(slot, first=False):
        vt = vb[slot].astype(f32).T.astype(bf16)
        for c in range(ROWS // 256):
            at = pl.ds(c * 256, 256)
            e = jnp.exp2(s_v[slot, :, at] * SCALE2 - m_v[:, at] * SCALE2)
            total = jnp.sum(e, axis=0, keepdims=True)
            eb = e.astype(bf16)
            p_v[slot, :, at] = eb
            o = dot(vt, eb)
            if first:
                l_v[:, at] = total
                o_t[:, at] = o
            else:
                l_v[:, at] += total
                o_t[:, at] += o

    output_of(16, True)
    local[1].wait()

    def output_step(i, carry):
        n = PAIRS - 1 - i

        @pl.when(n < PAIRS - 1)
        def _():
            kv_arrived(vb, vrecv, vsend, 2 * n + 1)
            kv_forward(vb, vfw, vrecv, n).start()

        @pl.when(n == PAIRS - 2)
        def _():
            for c in kv_relay(vb, vsend, vrecv):
                c.start()

        @pl.when(n == 1)
        def _():
            do_relay[0].wait_recv()
            do_relay[4].start()
            do_relay[1].wait_recv()
            do_relay[5].start()

        output_of(2 * n + 1)
        kv_arrived(vb, vrecv, vsend, 2 * n)
        output_of(2 * n)
        return carry

    lax.fori_loop(0, PAIRS, output_step, 0)

    for t in range(ROWS // HD):
        at = pl.ds(t * HD, HD)
        inv = 1.0 / l_v[:, at]
        l_v[:, at] = inv
        o_t[:, at] *= inv
        qp[at, :] = (qt[:, at].astype(f32) * (inv * SCALE)).T.astype(bf16)

    dq_t[...] = jnp.zeros_like(dq_t)

    def start_part(p):
        ag_v[...] = jnp.zeros_like(ag_v)

        def ag_step(i, carry):
            at = pl.ds(pl.multiple_of(i * 1024, 1024), 1024)
            ag_v[...] += dot_nt(w_v[:, at], do_v[p * HD:(p + 1) * HD, at])
            return carry

        lax.fori_loop(0, WIDTH // 1024, ag_step, 0)
        for h in range(HEADS):
            at = pl.ds((p * HEADS + h) * HD, HD)
            g = ag_v[h * HD:(h + 1) * HD, :].astype(bf16)
            dot_t[:, at] = g
            gf = g.astype(f32)
            delta_v[:, at] = jnp.sum(gf * o_t[:, at], axis=0, keepdims=True)
            dop[at, :] = (gf * l_v[:, at]).T.astype(bf16)

    def grads_of(p, slot):
        vblk = vb[slot]
        for c, size in ((0, 256), (256, 256), (512, 128)):
            at = pl.ds(p * HALF + c, size)
            dp = dot(vblk, dot_t[:, at])
            ds_v[:, c:c + size] = (p_v[slot, :, at].astype(f32) * (dp - delta_v[:, at])).astype(bf16)
        part = pl.ds(p * HALF, HALF)
        kt = kb[slot].astype(f32).T.astype(bf16)
        dq_t[:, part] += dot(kt, ds_v[...])
        dk = dot(ds_v[...], qp[part, :])
        dv = dot(p_v[slot, :, part], dop[part, :])
        return dk, dv

    local[5].wait()
    local[6].wait()
    start_part(0)

    def part_a(i, carry):
        dk, dv = grads_of(0, i)
        s_v[i, :, 0:HD] = dk
        s_v[i, :, HD:2 * HD] = dv
        return carry

    lax.fori_loop(0, 17, part_a, 0)

    for i in (2, 3, 4, 5):
        do_relay[i].wait_recv()
    start_part(1)

    def core_copy(n):
        return remote(csend.at[n], crecv.at[n], cs_sem.at[n], cr_sem.at[n], core)

    z_dest = (zm, zp, zp, zm, zp, zm, yhp)

    def z_copy(j):
        return remote(zs.at[j], zr.at[j], zs_sem.at[j], zr_sem.at[j], z_dest[j])

    def part_b(n, carry):
        dk, dv = grads_of(1, 2 * n)
        csend[n, :, 0:HD] = (dk + s_v[2 * n, :, 0:HD]).astype(bf16)
        csend[n, :, HD:2 * HD] = (dv + s_v[2 * n, :, HD:2 * HD]).astype(bf16)
        core_copy(n).start()
        dk, dv = grads_of(1, 2 * n + 1)
        s_v[2 * n + 1, :, 0:HD] += dk
        s_v[2 * n + 1, :, HD:2 * HD] += dv
        core_copy(n).wait_recv()
        total = s_v[2 * n + 1, :, 0:2 * HD] + crecv[n].astype(f32)
        s_v[2 * n + 1, :, 0:2 * HD] = total

        for j, extras in ((3, (0,)), (4, (1,)), (6, (2, 3))):
            @pl.when(n == j)
            def _():
                for e in extras:
                    z_copy(e).wait_recv()
                    s_v[2 * n + 1, :, 0:2 * HD] += zr[e].astype(f32)

        for j in range(7):
            @pl.when(n == j)
            def _():
                zs[j] = s_v[2 * n + 1, :, 0:2 * HD].astype(bf16)
                z_copy(j).start()
        return carry

    lax.fori_loop(0, PAIRS, part_b, 0)

    dk, dv = grads_of(1, 16)
    dk = dk + s_v[16, :, 0:HD]
    dvn_ref[...] = (dv + s_v[16, :, HD:2 * HD]).astype(bf16)
    dkn_ref[...] = (dk * cos_v[...] - pltpu.roll(dk, HD // 2, 1) * sin_v[...]).astype(bf16)

    for p in range(2):
        for h in range(HEADS):
            at = pl.ds((p * HEADS + h) * HD, HD)
            g = (dq_t[:, at] * (l_v[:, at] * SCALE)).T
            for j in range(4):
                k = chunks[4 * p + j]
                x = g[j * CHUNK:(j + 1) * CHUNK, :]
                ta = pl.ds(pl.multiple_of(k * CHUNK, CHUNK), CHUNK)
                y = x * cos_v[ta, :] - pltpu.roll(x, HD // 2, 1) * sin_v[ta, :]
                dq_ref[pl.ds(pl.multiple_of(h * SEQ + k * CHUNK, CHUNK), CHUNK), :] = y.astype(bf16)

    total = s_v[15, :, 0:2 * HD]
    for e in (4, 5, 6):
        z_copy(e).wait_recv()
        total = total + zr[e].astype(f32)
    dkp_ref[...] = total[:, 0:HD].astype(bf16)
    dvp_ref[...] = total[:, HD:2 * HD].astype(bf16)

    for src, buf, ssem, fsem, rsem in ((kp_hbm, kb, ksend, kfw, krecv), (vp_hbm, vb, vsend, vfw, vrecv)):
        for c in kv_own(src, buf, ssem, rsem) + kv_relay(buf, ssem, rsem):
            c.wait_send()
        for n in range(PAIRS - 1):
            kv_forward(buf, fsem, rsem, n).wait_send()
    for c in do_own + do_relay:
        c.wait_send()
    for n in range(PAIRS):
        core_copy(n).wait_send()
    for j in range(7):
        z_copy(j).wait_send()


def local(out_grad, out_weight, queries, keys_new, values_new, keys_prompt, values_prompt, offsets):
    half = HD // 2
    frequency = np.power(np.float32(1000000.0), -(np.arange(half, dtype=np.float32) / half)).astype(np.float32)
    frequency = jnp.asarray(np.concatenate([frequency, frequency])[None, :])
    q = jnp.transpose(queries[0, :, 0], (1, 0, 2)).reshape(ROWS, HD)
    any_spec = pl.BlockSpec(memory_space=pl.ANY)
    vmem = pl.BlockSpec(memory_space=pltpu.VMEM)
    dma = pltpu.SemaphoreType.DMA
    dq, dkn, dvn, dkp, dvp = pl.pallas_call(
        kernel,
        out_shape=(
            jax.ShapeDtypeStruct((ROWS, HD), bf16),
            jax.ShapeDtypeStruct((SEQ, HD), bf16),
            jax.ShapeDtypeStruct((SEQ, HD), bf16),
            jax.ShapeDtypeStruct((BLK, HD), bf16),
            jax.ShapeDtypeStruct((BLK, HD), bf16),
        ),
        in_specs=[any_spec] * 7 + [pl.BlockSpec(memory_space=pltpu.SMEM), vmem],
        out_specs=(vmem,) * 5,
        scratch_shapes=[
            pltpu.VMEM((HEADS * HD, WIDTH), bf16),
            pltpu.VMEM((SEQ, WIDTH), bf16),
            pltpu.VMEM((17, BLK, HD), bf16),
            pltpu.VMEM((17, BLK, HD), bf16),
            pltpu.VMEM((ROWS, HD), bf16),
            pltpu.VMEM((SEQ, HD), bf16),
            pltpu.VMEM((HD, ROWS), bf16),
            pltpu.VMEM((ROWS, HD), bf16),
            pltpu.VMEM((HD, ROWS), bf16),
            pltpu.VMEM((ROWS, HD), bf16),
            pltpu.VMEM((17, BLK, ROWS), f32),
            pltpu.VMEM((17, BLK, ROWS), bf16),
            pltpu.VMEM((HD, ROWS), f32),
            pltpu.VMEM((HD, ROWS), f32),
            pltpu.VMEM((1, ROWS), f32),
            pltpu.VMEM((1, ROWS), f32),
            pltpu.VMEM((1, ROWS), f32),
            pltpu.VMEM((SEQ, HD), f32),
            pltpu.VMEM((SEQ, HD), f32),
            pltpu.VMEM((BLK, HALF), bf16),
            pltpu.VMEM((HEADS * HD, HD), f32),
            pltpu.VMEM((PAIRS, BLK, 2 * HD), bf16),
            pltpu.VMEM((PAIRS, BLK, 2 * HD), bf16),
            pltpu.VMEM((7, BLK, 2 * HD), bf16),
            pltpu.VMEM((7, BLK, 2 * HD), bf16),
            dma((7,)),
            dma((8,)),
            dma((8,)),
            dma((7,)),
            dma((7,)),
            dma((16,)),
            dma((16,)),
            dma((9,)),
            dma((9,)),
            dma((8,)),
            dma((8,)),
            dma((7,)),
            dma((7,)),
        ],
        compiler_params=pltpu.CompilerParams(
            collective_id=0, has_side_effects=True, vmem_limit_bytes=60 * 1024 * 1024
        ),
        name="attention_backward",
    )(
        out_grad[0],
        out_weight.reshape(HEADS * HD, WIDTH),
        q,
        keys_new[0, :, 0],
        values_new[0, :, 0],
        keys_prompt[:, 0],
        values_prompt[:, 0],
        offsets,
        frequency,
    )
    grad_queries = jnp.transpose(dq.reshape(HEADS, SEQ, HD), (1, 0, 2))[None, :, None]
    return (
        grad_queries,
        dkn[None, :, None],
        dvn[None, :, None],
        dkp[:, None],
        dvp[:, None],
    )


def solution(mesh):
    placed = (
        P("roll", "kvh", None),
        P("kvh", None, None, None),
        P("roll", None, "kvh", None, None),
        P("roll", None, "kvh", None),
        P("roll", None, "kvh", None),
        P("roll", "kvh", None),
        P("roll", "kvh", None),
        P("roll"),
    )
    return jax.shard_map(
        local,
        mesh=mesh,
        in_specs=placed,
        out_specs=(
            P("roll", None, "kvh", None, None),
            P("roll", None, "kvh", None),
            P("roll", None, "kvh", None),
            P("roll", "kvh", None),
            P("roll", "kvh", None),
        ),
        check_vma=False,
    )
```

```python
import functools
import math

import jax
import jax.numpy as jnp
import numpy as np
from jax import lax
from jax.experimental import pallas as pl
from jax.experimental.pallas import tpu as pltpu
from jax.sharding import PartitionSpec as P

MESH = pl.DeviceIdType.MESH
f32 = jnp.float32
bf16 = jnp.bfloat16

HEADS = 5
SEQ = 256
HD = 128
ROWS = HEADS * SEQ
HALF = ROWS // 2
BLK = 256
WIDTH = 5120
PROMPT = 4096
CHUNK = 32
SCALE = HD ** -0.5
SCALE2 = SCALE * math.log2(math.e)
PAIRS = 8
PAIR = 2 * BLK
OWN = slice(16 * BLK, 17 * BLK)


def dot(a, b):
    return lax.dot_general(a, b, (((1,), (0,)), ((), ())), preferred_element_type=f32)


def dot_nt(a, b):
    return lax.dot_general(a, b, (((1,), (1,)), ((), ())), preferred_element_type=f32)


def kernel(
    og_hbm, w_hbm, q_hbm, kn_hbm, vn_hbm, kp_hbm, vp_hbm, off_ref, freq_ref,
    dq_ref, dkn_ref, dvn_ref, dkp_ref, dvp_ref,
    w_v, do_v, kb, vb, kt_v, q_v, kn_v, qt, qp, dot_t, dop, s_v, p_v, o_t, dq_t, m_v, l_v, delta_v,
    cos_v, sin_v, ds_v, ag_v, csend, crecv, zs, zr,
    lsem, ksend, vsend, kfw, vfw, krecv, vrecv, dsend, drecv, cs_sem, cr_sem, zs_sem, zr_sem,
):
    roll = lax.axis_index("roll")
    kvh = lax.axis_index("kvh")
    zz, yh, cc = roll // 4, (roll // 2) % 2, roll % 2
    yl, xx = kvh // 4, kvh % 4

    def dev(dz=0, dyh=0, dc=0, dyl=0, dx=0):
        r = (((zz + dz) % 4) * 2 + (yh + dyh) % 2) * 2 + (cc + dc) % 2
        k = ((yl + dyl) % 2) * 4 + (xx + dx) % 4
        return (r, k)

    core, yhp = dev(dc=1), dev(dyh=1)
    zp, zm, z2 = dev(dz=1), dev(dz=3), dev(dz=2)
    ylp, xp, xm = dev(dyl=1), dev(dx=1), dev(dx=3)

    barrier = pltpu.get_barrier_semaphore()
    for d in (core, yhp, zp, zm, z2, ylp, xp, xm):
        pl.semaphore_signal(barrier, 1, device_id=d, device_id_type=MESH)

    local = [
        pltpu.make_async_copy(kp_hbm, kb.at[pl.ds(15 * BLK, BLK)], lsem.at[0]),
        pltpu.make_async_copy(vp_hbm, vb.at[pl.ds(15 * BLK, BLK)], lsem.at[1]),
        pltpu.make_async_copy(q_hbm, q_v, lsem.at[2]),
        pltpu.make_async_copy(kn_hbm, kn_v, lsem.at[3]),
        pltpu.make_async_copy(vn_hbm, vb.at[pl.ds(16 * BLK, BLK)], lsem.at[4]),
        pltpu.make_async_copy(og_hbm, do_v.at[pl.ds(0, CHUNK)], lsem.at[5]),
        pltpu.make_async_copy(w_hbm, w_v, lsem.at[6]),
    ]
    for c in local:
        c.start()

    pos = (off_ref[0] + PROMPT + lax.broadcasted_iota(jnp.int32, (SEQ, HD), 0)).astype(f32)
    angle = pos * freq_ref[...]
    cos_v[...] = jnp.cos(angle)
    lane = lax.broadcasted_iota(jnp.int32, (SEQ, HD), 1)
    sin_a = jnp.sin(angle)
    sin_v[...] = jnp.where(lane < HD // 2, -sin_a, sin_a)

    pl.semaphore_wait(barrier, 8)

    def blk(buf, slot):
        return buf.at[pl.ds(slot * BLK, BLK)]

    def remote(src, dst, ssem, rsem, d):
        return pltpu.make_async_remote_copy(
            src_ref=src, dst_ref=dst, send_sem=ssem, recv_sem=rsem, device_id=d, device_id_type=MESH
        )

    first_hops = ((13, yhp), (9, zp), (11, zm), (5, z2), (14, core))
    relay_hops = ((7, zp), (3, zm), (1, z2))

    def kv_own(src, buf, ssem, rsem):
        return [remote(src, blk(buf, s), ssem.at[i], rsem.at[s], d) for i, (s, d) in enumerate(first_hops)]

    def kv_relay(buf, ssem, rsem):
        return [
            remote(blk(buf, 13), blk(buf, s), ssem.at[5 + i], rsem.at[s], d) for i, (s, d) in enumerate(relay_hops)
        ]

    def kv_forward(buf, fsem, rsem, n):
        return remote(blk(buf, 2 * n + 1), blk(buf, 2 * n), fsem.at[n], rsem.at[2 * n], core)

    def kv_arrived(buf, rsem, ssem, s):
        remote(blk(buf, s), blk(buf, s), ssem.at[0], rsem.at[s], core).wait_recv()

    for c in kv_own(kp_hbm, kb, ksend, krecv):
        c.start()
    for c in kv_own(vp_hbm, vb, vsend, vrecv):
        c.start()

    def rows(slot, lo=0, size=CHUNK):
        return do_v.at[pl.ds(slot * CHUNK + lo, size)]

    do_own = [
        remote(og_hbm, rows(1), dsend.at[0], drecv.at[0], ylp),
        remote(og_hbm, rows(3), dsend.at[1], drecv.at[1], xp),
        remote(og_hbm, rows(2), dsend.at[2], drecv.at[2], xm),
    ]
    do_relay = [
        remote(rows(3, 0, 16), rows(4, 0, 16), dsend.at[3], drecv.at[3], xp),
        remote(rows(2, 16, 16), rows(4, 16, 16), dsend.at[4], drecv.at[4], xm),
        remote(rows(1), rows(6), dsend.at[5], drecv.at[5], xp),
        remote(rows(1), rows(5), dsend.at[6], drecv.at[6], xm),
        remote(rows(4, 0, 16), rows(7, 0, 16), dsend.at[7], drecv.at[7], ylp),
        remote(rows(4, 16, 16), rows(7, 16, 16), dsend.at[8], drecv.at[8], ylp),
    ]
    for c in do_own:
        c.start()

    def kof(dyl, dx):
        return ((yl + dyl) % 2) * 4 + (xx + dx) % 4

    chunks = [kof(0, 0), kof(1, 0), kof(0, 1), kof(0, 3), kof(0, 2), kof(1, 1), kof(1, 3), kof(1, 2)]

    for i in (2, 3, 4):
        local[i].wait()
    kn = kn_v[...].astype(f32)
    kb[OWN, :] = (kn * cos_v[...] + pltpu.roll(kn, HD // 2, 1) * sin_v[...]).astype(bf16)
    for p in range(2):
        for h in range(HEADS):
            parts = []
            for j in range(4):
                k = chunks[4 * p + j]
                x = q_v[pl.ds(pl.multiple_of(h * SEQ + k * CHUNK, CHUNK), CHUNK), :].astype(f32)
                at = pl.ds(pl.multiple_of(k * CHUNK, CHUNK), CHUNK)
                parts.append((x * cos_v[at, :] + pltpu.roll(x, HD // 2, 1) * sin_v[at, :]))
            tile = jnp.concatenate(parts, axis=0)
            qt[:, pl.ds((p * HEADS + h) * HD, HD)] = tile.T.astype(bf16)

    tl = lax.broadcasted_iota(jnp.int32, (1, HD), 1)

    def tokens(p):
        which = tl // CHUNK
        base = jnp.where(
            which == 0,
            chunks[4 * p],
            jnp.where(which == 1, chunks[4 * p + 1], jnp.where(which == 2, chunks[4 * p + 2], chunks[4 * p + 3])),
        )
        return base * CHUNK + tl % CHUNK

    key_at = lax.broadcasted_iota(jnp.int32, (BLK, HD), 0)
    kt_v[:, OWN] = kb[OWN, :].T
    for p in range(2):
        allowed = key_at <= tokens(p)
        for h in range(HEADS):
            at = pl.ds((p * HEADS + h) * HD, HD)
            s = jnp.where(allowed, dot(kb[OWN, :], qt[:, at]), -1e30)
            s_v[OWN, at] = s
            m_v[:, at] = jnp.max(s, axis=0, keepdims=True)

    local[0].wait()

    def pair_at(n):
        return pl.multiple_of(n * PAIR, PAIR)

    def scores_of(n):
        here = pl.ds(pair_at(n), PAIR)
        kblk = kb[here, :]
        kt_v[:, here] = kblk.T
        for c in range(ROWS // 256):
            at = pl.ds(c * 256, 256)
            s = dot(kblk, qt[:, at])
            s_v[here, at] = s
            m_v[:, at] = jnp.maximum(m_v[:, at], jnp.max(s, axis=0, keepdims=True))

    def gather_order(i):
        return PAIRS - 1 - i - (i == 4).astype(jnp.int32) + (i == 5).astype(jnp.int32)

    def score_step(i, carry):
        n = gather_order(i)

        @pl.when(i > 0)
        def _():
            kv_arrived(kb, krecv, ksend, 2 * n + 1)
            kv_forward(kb, kfw, krecv, n).start()

        @pl.when(i == 1)
        def _():
            for c in kv_relay(kb, ksend, krecv):
                c.start()
            kv_arrived(vb, vrecv, vsend, 13)
            for c in kv_relay(vb, vsend, vrecv):
                c.start()

        @pl.when(i == 5)
        def _():
            do_own[1].wait_recv()
            do_relay[0].start()
            do_own[2].wait_recv()
            do_relay[1].start()
            do_own[0].wait_recv()
            do_relay[2].start()
            do_relay[3].start()

        kv_arrived(kb, krecv, ksend, 2 * n)
        scores_of(n)
        return carry

    lax.fori_loop(0, PAIRS, score_step, 0)

    def output_of(at_row, size, first=False):
        here = pl.ds(at_row, size)
        vt = vb[here, :].T
        for c in range(ROWS // 256):
            at = pl.ds(c * 256, 256)
            e = jnp.exp2(s_v[here, at] * SCALE2 - m_v[:, at] * SCALE2)
            total = jnp.sum(e, axis=0, keepdims=True)
            eb = e.astype(bf16)
            p_v[here, at] = eb
            o = dot(vt, eb)
            if first:
                l_v[:, at] = total
                o_t[:, at] = o
            else:
                l_v[:, at] += total
                o_t[:, at] += o

    output_of(16 * BLK, BLK, True)
    local[1].wait()

    def output_step(i, carry):
        n = gather_order(i)

        @pl.when(i == 1)
        def _():
            kv_forward(vb, vfw, vrecv, n).start()

        @pl.when(i > 1)
        def _():
            kv_arrived(vb, vrecv, vsend, 2 * n + 1)
            kv_forward(vb, vfw, vrecv, n).start()

        @pl.when(i == 1)
        def _():
            do_relay[0].wait_recv()
            do_relay[4].start()
            do_relay[1].wait_recv()
            do_relay[5].start()

        kv_arrived(vb, vrecv, vsend, 2 * n)
        output_of(pair_at(n), PAIR)
        return carry

    lax.fori_loop(0, PAIRS, output_step, 0)

    for t in range(ROWS // HD):
        at = pl.ds(t * HD, HD)
        inv = 1.0 / l_v[:, at]
        l_v[:, at] = inv
        o_t[:, at] *= inv
        qp[at, :] = (qt[:, at].astype(f32) * (inv * SCALE)).T.astype(bf16)

    dq_t[...] = jnp.zeros_like(dq_t)

    def start_part(p):
        ag_v[...] = jnp.zeros_like(ag_v)

        def ag_step(i, carry):
            at = pl.ds(pl.multiple_of(i * 1024, 1024), 1024)
            ag_v[...] += dot_nt(w_v[:, at], do_v[p * HD:(p + 1) * HD, at])
            return carry

        lax.fori_loop(0, WIDTH // 1024, ag_step, 0)
        for h in range(HEADS):
            at = pl.ds((p * HEADS + h) * HD, HD)
            g = ag_v[h * HD:(h + 1) * HD, :].astype(bf16)
            dot_t[:, at] = g
            gf = g.astype(f32)
            delta_v[:, at] = jnp.sum(gf * o_t[:, at], axis=0, keepdims=True)
            dop[at, :] = (gf * l_v[:, at]).T.astype(bf16)

    def grads_of(p, at_row, size):
        here = pl.ds(at_row, size)
        vblk = vb[here, :]
        for c, width in ((0, 256), (256, 256), (512, 128)):
            at = pl.ds(p * HALF + c, width)
            dp = dot(vblk, dot_t[:, at])
            ds_v[0:size, c:c + width] = (p_v[here, at].astype(f32) * (dp - delta_v[:, at])).astype(bf16)
        part = pl.ds(p * HALF, HALF)
        dq_t[:, part] += dot(kt_v[:, here], ds_v[0:size, :])
        dk = dot(ds_v[0:size, :], qp[part, :])
        dv = dot(p_v[here, part], dop[part, :])
        return dk, dv

    local[5].wait()
    local[6].wait()
    start_part(0)

    def part_a(n, carry):
        here = pl.ds(pair_at(n), PAIR)
        dk, dv = grads_of(0, pair_at(n), PAIR)
        s_v[here, 0:HD] = dk
        s_v[here, HD:2 * HD] = dv
        return carry

    lax.fori_loop(0, PAIRS, part_a, 0)
    dk, dv = grads_of(0, 16 * BLK, BLK)
    s_v[OWN, 0:HD] = dk
    s_v[OWN, HD:2 * HD] = dv

    for i in (2, 3, 4, 5):
        do_relay[i].wait_recv()
    start_part(1)

    def core_copy(n):
        return remote(csend.at[n], crecv.at[n], cs_sem.at[n], cr_sem.at[n], core)

    z_dest = (zm, zp, zp, zm, zm, zp, yhp)

    def z_copy(j):
        return remote(zs.at[j], zr.at[j], zs_sem.at[j], zr_sem.at[j], z_dest[j])

    def own_half(n):
        return pl.ds(pl.multiple_of(n * PAIR + BLK, BLK), BLK)

    def finish(n, j, extras):
        total = s_v[own_half(n), 0:2 * HD] + crecv[n].astype(f32)
        for e in extras:
            z_copy(e).wait_recv()
            total = total + zr[e].astype(f32)
        if j < 7:
            zs[j] = total.astype(bf16)
            z_copy(j).start()
        else:
            dkp_ref[...] = total[:, 0:HD].astype(bf16)
            dvp_ref[...] = total[:, HD:2 * HD].astype(bf16)

    extras_of = ((), (), (), (0,), (), (2,), (1, 3), (4, 5, 6))

    def part_b(n, carry):
        dk, dv = grads_of(1, pair_at(n), PAIR)
        there = pl.ds(pair_at(n), BLK)
        csend[n, :, 0:HD] = (dk[0:BLK] + s_v[there, 0:HD]).astype(bf16)
        csend[n, :, HD:2 * HD] = (dv[0:BLK] + s_v[there, HD:2 * HD]).astype(bf16)
        core_copy(n).start()
        s_v[own_half(n), 0:HD] += dk[BLK:]
        s_v[own_half(n), HD:2 * HD] += dv[BLK:]

        for j in range(7):
            @pl.when(n == j + 1)
            def _():
                core_copy(j).wait_recv()
                finish(j, j, extras_of[j])
        return carry

    lax.fori_loop(0, PAIRS, part_b, 0)

    dk, dv = grads_of(1, 16 * BLK, BLK)
    dk = dk + s_v[OWN, 0:HD]
    dvn_ref[...] = (dv + s_v[OWN, HD:2 * HD]).astype(bf16)
    dkn_ref[...] = (dk * cos_v[...] - pltpu.roll(dk, HD // 2, 1) * sin_v[...]).astype(bf16)

    for p in range(2):
        for h in range(HEADS):
            at = pl.ds((p * HEADS + h) * HD, HD)
            g = (dq_t[:, at] * (l_v[:, at] * SCALE)).T
            for j in range(4):
                k = chunks[4 * p + j]
                x = g[j * CHUNK:(j + 1) * CHUNK, :]
                ta = pl.ds(pl.multiple_of(k * CHUNK, CHUNK), CHUNK)
                y = x * cos_v[ta, :] - pltpu.roll(x, HD // 2, 1) * sin_v[ta, :]
                dq_ref[pl.ds(pl.multiple_of(h * SEQ + k * CHUNK, CHUNK), CHUNK), :] = y.astype(bf16)

    core_copy(7).wait_recv()
    finish(7, 7, extras_of[7])

    for src, buf, ssem, fsem, rsem in ((kp_hbm, kb, ksend, kfw, krecv), (vp_hbm, vb, vsend, vfw, vrecv)):
        for c in kv_own(src, buf, ssem, rsem) + kv_relay(buf, ssem, rsem):
            c.wait_send()
        for n in range(PAIRS - 1):
            kv_forward(buf, fsem, rsem, n).wait_send()
    for c in do_own + do_relay:
        c.wait_send()
    for n in range(PAIRS):
        core_copy(n).wait_send()
    for j in range(7):
        z_copy(j).wait_send()


def hand_over(*refs):
    sources, results, sems = refs[:5], refs[5:10], refs[10]
    copies = [pltpu.make_async_copy(a, b, sems.at[i]) for i, (a, b) in enumerate(zip(sources, results))]
    for c in copies:
        c.start()
    for c in copies:
        c.wait()


def local(out_grad, out_weight, queries, keys_new, values_new, keys_prompt, values_prompt, offsets):
    half = HD // 2
    frequency = np.power(np.float32(1000000.0), -(np.arange(half, dtype=np.float32) / half)).astype(np.float32)
    frequency = jnp.asarray(np.concatenate([frequency, frequency])[None, :])
    q = jnp.transpose(queries[0, :, 0], (1, 0, 2)).reshape(ROWS, HD)
    any_spec = pl.BlockSpec(memory_space=pl.ANY)
    vmem = pl.BlockSpec(memory_space=pltpu.VMEM)
    dma = pltpu.SemaphoreType.DMA
    grads = pl.pallas_call(
        kernel,
        out_shape=(
            jax.ShapeDtypeStruct((ROWS, HD), bf16),
            jax.ShapeDtypeStruct((SEQ, HD), bf16),
            jax.ShapeDtypeStruct((SEQ, HD), bf16),
            jax.ShapeDtypeStruct((BLK, HD), bf16),
            jax.ShapeDtypeStruct((BLK, HD), bf16),
        ),
        in_specs=[any_spec] * 7 + [pl.BlockSpec(memory_space=pltpu.SMEM), vmem],
        out_specs=(vmem,) * 5,
        scratch_shapes=[
            pltpu.VMEM((HEADS * HD, WIDTH), bf16),
            pltpu.VMEM((SEQ, WIDTH), bf16),
            pltpu.VMEM((17 * BLK, HD), bf16),
            pltpu.VMEM((17 * BLK, HD), bf16),
            pltpu.VMEM((HD, 17 * BLK), bf16),
            pltpu.VMEM((ROWS, HD), bf16),
            pltpu.VMEM((SEQ, HD), bf16),
            pltpu.VMEM((HD, ROWS), bf16),
            pltpu.VMEM((ROWS, HD), bf16),
            pltpu.VMEM((HD, ROWS), bf16),
            pltpu.VMEM((ROWS, HD), bf16),
            pltpu.VMEM((17 * BLK, ROWS), f32),
            pltpu.VMEM((17 * BLK, ROWS), bf16),
            pltpu.VMEM((HD, ROWS), f32),
            pltpu.VMEM((HD, ROWS), f32),
            pltpu.VMEM((1, ROWS), f32),
            pltpu.VMEM((1, ROWS), f32),
            pltpu.VMEM((1, ROWS), f32),
            pltpu.VMEM((SEQ, HD), f32),
            pltpu.VMEM((SEQ, HD), f32),
            pltpu.VMEM((PAIR, HALF), bf16),
            pltpu.VMEM((HEADS * HD, HD), f32),
            pltpu.VMEM((PAIRS, BLK, 2 * HD), bf16),
            pltpu.VMEM((PAIRS, BLK, 2 * HD), bf16),
            pltpu.VMEM((7, BLK, 2 * HD), bf16),
            pltpu.VMEM((7, BLK, 2 * HD), bf16),
            dma((7,)),
            dma((8,)),
            dma((8,)),
            dma((7,)),
            dma((7,)),
            dma((16,)),
            dma((16,)),
            dma((9,)),
            dma((9,)),
            dma((8,)),
            dma((8,)),
            dma((7,)),
            dma((7,)),
        ],
        compiler_params=pltpu.CompilerParams(
            collective_id=0, has_side_effects=True, vmem_limit_bytes=60 * 1024 * 1024
        ),
        name="attention_backward",
    )(
        out_grad[0],
        out_weight.reshape(HEADS * HD, WIDTH),
        q,
        keys_new[0, :, 0],
        values_new[0, :, 0],
        keys_prompt[:, 0],
        values_prompt[:, 0],
        offsets,
        frequency,
    )
    dq, dkn, dvn, dkp, dvp = pl.pallas_call(
        hand_over,
        out_shape=tuple(jax.ShapeDtypeStruct(g.shape, g.dtype) for g in grads),
        in_specs=[any_spec] * 5,
        out_specs=(any_spec,) * 5,
        scratch_shapes=[dma((5,))],
        name="hand_over",
    )(*grads)
    grad_queries = jnp.transpose(dq.reshape(HEADS, SEQ, HD), (1, 0, 2))[None, :, None]
    return (
        grad_queries,
        dkn[None, :, None],
        dvn[None, :, None],
        dkp[:, None],
        dvp[:, None],
    )


def solution(mesh):
    placed = (
        P("roll", "kvh", None),
        P("kvh", None, None, None),
        P("roll", None, "kvh", None, None),
        P("roll", None, "kvh", None),
        P("roll", None, "kvh", None),
        P("roll", "kvh", None),
        P("roll", "kvh", None),
        P("roll"),
    )
    return jax.shard_map(
        local,
        mesh=mesh,
        in_specs=placed,
        out_specs=(
            P("roll", None, "kvh", None, None),
            P("roll", None, "kvh", None),
            P("roll", None, "kvh", None),
            P("roll", "kvh", None),
            P("roll", "kvh", None),
        ),
        check_vma=False,
    )
```

```python
import functools
import math

import jax
import jax.numpy as jnp
import numpy as np
from jax import lax
from jax.experimental import pallas as pl
from jax.experimental.pallas import tpu as pltpu
from jax.sharding import PartitionSpec as P

MESH = pl.DeviceIdType.MESH
f32 = jnp.float32
bf16 = jnp.bfloat16

HEADS = 5
SEQ = 256
HD = 128
ROWS = HEADS * SEQ
BLK = 256
WIDTH = 5120
PROMPT = 4096
CHUNK = 32
SCALE = HD ** -0.5
SCALE2 = SCALE * math.log2(math.e)
PAIRS = 8
PAIR = 2 * BLK
OWN = slice(16 * BLK, 17 * BLK)


def dot(a, b):
    return lax.dot_general(a, b, (((1,), (0,)), ((), ())), preferred_element_type=f32)


def dot_nt(a, b):
    return lax.dot_general(a, b, (((1,), (1,)), ((), ())), preferred_element_type=f32)


def kernel(
    og_hbm, w_hbm, q_hbm, kn_hbm, vn_hbm, kp_hbm, vp_hbm, off_ref, freq_ref,
    dq_ref, dkn_ref, dvn_ref, dkp_ref, dvp_ref,
    w_v, do_v, kb, vb, kt_v, q_v, kn_v, qt, qp, dot_t, dop, s_v, p_v, o_t, dq_t, m_v, l_v, delta_v,
    cos_v, sin_v, ds_v, ag_v, csend, crecv, zs, zr,
    lsem, ksend, vsend, kfw, vfw, krecv, vrecv, dsend, drecv, cs_sem, cr_sem, zs_sem, zr_sem,
):
    roll = lax.axis_index("roll")
    kvh = lax.axis_index("kvh")
    zz, yh, cc = roll // 4, (roll // 2) % 2, roll % 2
    yl, xx = kvh // 4, kvh % 4

    def dev(dz=0, dyh=0, dc=0, dyl=0, dx=0):
        r = (((zz + dz) % 4) * 2 + (yh + dyh) % 2) * 2 + (cc + dc) % 2
        k = ((yl + dyl) % 2) * 4 + (xx + dx) % 4
        return (r, k)

    core, yhp = dev(dc=1), dev(dyh=1)
    zp, zm = dev(dz=1), dev(dz=3)
    ylp, xp, xm = dev(dyl=1), dev(dx=1), dev(dx=3)

    barrier = pltpu.get_barrier_semaphore()
    for d in (core, yhp, zp, zm, ylp, xp, xm):
        pl.semaphore_signal(barrier, 1, device_id=d, device_id_type=MESH)

    local = [
        pltpu.make_async_copy(kp_hbm, kb.at[pl.ds(15 * BLK, BLK)], lsem.at[0]),
        pltpu.make_async_copy(vp_hbm, vb.at[pl.ds(15 * BLK, BLK)], lsem.at[1]),
        pltpu.make_async_copy(q_hbm, q_v, lsem.at[2]),
        pltpu.make_async_copy(kn_hbm, kn_v, lsem.at[3]),
        pltpu.make_async_copy(vn_hbm, vb.at[pl.ds(16 * BLK, BLK)], lsem.at[4]),
        pltpu.make_async_copy(og_hbm, do_v.at[pl.ds(0, CHUNK)], lsem.at[5]),
        pltpu.make_async_copy(w_hbm, w_v, lsem.at[6]),
    ]
    for c in local:
        c.start()

    pos = (off_ref[0] + PROMPT + lax.broadcasted_iota(jnp.int32, (SEQ, HD), 0)).astype(f32)
    angle = pos * freq_ref[...]
    cos_v[...] = jnp.cos(angle)
    lane = lax.broadcasted_iota(jnp.int32, (SEQ, HD), 1)
    sin_a = jnp.sin(angle)
    sin_v[...] = jnp.where(lane < HD // 2, -sin_a, sin_a)

    pl.semaphore_wait(barrier, 7)

    def remote(src, dst, ssem, rsem, d):
        return pltpu.make_async_remote_copy(
            src_ref=src, dst_ref=dst, send_sem=ssem, recv_sem=rsem, device_id=d, device_id_type=MESH
        )

    def blk(buf, slot, lo=0, size=BLK):
        return buf.at[pl.ds(slot * BLK + lo, size)]

    class Spread:
        def __init__(self, src, buf, send, recv, fsend):
            self.src, self.buf, self.send, self.recv, self.fsend = src, buf, send, recv, fsend
            mid = BLK // 2
            self.near = [self.hop(src, 13, 0, yhp), self.hop(src, 14, 1, core)]
            self.along = [self.hop(src, 9, 2, zp), self.hop(src, 11, 3, zm)]
            self.relay = [self.hop(blk(buf, 13), 7, 4, zp), self.hop(blk(buf, 13), 3, 5, zm)]
            self.far = {
                9: remote(blk(buf, 9, 0, mid), blk(buf, 5, 0, mid), send.at[6], recv.at[5], zp),
                11: remote(blk(buf, 11, mid, mid), blk(buf, 5, mid, mid), send.at[7], recv.at[16], zm),
                7: remote(blk(buf, 7, 0, mid), blk(buf, 1, 0, mid), send.at[8], recv.at[1], zp),
                3: remote(blk(buf, 3, mid, mid), blk(buf, 1, mid, mid), send.at[9], recv.at[17], zm),
            }

        def hop(self, src, slot, i, d):
            return remote(src, blk(self.buf, slot), self.send.at[i], self.recv.at[slot], d)

        def forward(self, n):
            return remote(
                blk(self.buf, 2 * n + 1), blk(self.buf, 2 * n), self.fsend.at[n], self.recv.at[2 * n], core
            )

        def arrived(self, slot):
            if slot == 5:
                self.far[9].wait_recv()
                self.far[11].wait_recv()
            elif slot == 1:
                self.far[7].wait_recv()
                self.far[3].wait_recv()
            else:
                self.hop(blk(self.buf, slot), slot, 0, core).wait_recv()

        def wait_send(self):
            for c in self.near + self.along + self.relay + list(self.far.values()):
                c.wait_send()
            for n in range(PAIRS - 1):
                self.forward(n).wait_send()

    keys = Spread(kp_hbm, kb, ksend, krecv, kfw)
    vals = Spread(vp_hbm, vb, vsend, vrecv, vfw)
    for c in keys.near[:1] + keys.along + vals.near[:1] + keys.near[1:] + vals.near[1:]:
        c.start()

    def rows(slot, lo=0, size=CHUNK):
        return do_v.at[pl.ds(slot * CHUNK + lo, size)]

    do_own = [
        remote(og_hbm, rows(1), dsend.at[0], drecv.at[0], ylp),
        remote(og_hbm, rows(3), dsend.at[1], drecv.at[1], xp),
        remote(og_hbm, rows(2), dsend.at[2], drecv.at[2], xm),
    ]
    do_relay = [
        remote(rows(3, 0, 16), rows(4, 0, 16), dsend.at[3], drecv.at[3], xp),
        remote(rows(2, 16, 16), rows(4, 16, 16), dsend.at[4], drecv.at[4], xm),
        remote(rows(1), rows(6), dsend.at[5], drecv.at[5], xp),
        remote(rows(1), rows(5), dsend.at[6], drecv.at[6], xm),
        remote(rows(4, 0, 16), rows(7, 0, 16), dsend.at[7], drecv.at[7], ylp),
        remote(rows(4, 16, 16), rows(7, 16, 16), dsend.at[8], drecv.at[8], ylp),
    ]
    for c in do_own:
        c.start()

    def kof(dyl, dx):
        return ((yl + dyl) % 2) * 4 + (xx + dx) % 4

    chunks = [kof(0, 0), kof(1, 0), kof(0, 1), kof(0, 3), kof(0, 2), kof(1, 1), kof(1, 3), kof(1, 2)]

    for i in (2, 3, 4):
        local[i].wait()
    kn = kn_v[...].astype(f32)
    kb[OWN, :] = (kn * cos_v[...] + pltpu.roll(kn, HD // 2, 1) * sin_v[...]).astype(bf16)
    for p in range(2):
        for h in range(HEADS):
            parts = []
            for j in range(4):
                k = chunks[4 * p + j]
                x = q_v[pl.ds(pl.multiple_of(h * SEQ + k * CHUNK, CHUNK), CHUNK), :].astype(f32)
                at = pl.ds(pl.multiple_of(k * CHUNK, CHUNK), CHUNK)
                parts.append((x * cos_v[at, :] + pltpu.roll(x, HD // 2, 1) * sin_v[at, :]))
            tile = jnp.concatenate(parts, axis=0)
            qt[:, pl.ds((p * HEADS + h) * HD, HD)] = tile.T.astype(bf16)

    tl = lax.broadcasted_iota(jnp.int32, (1, HD), 1)

    def tokens(p):
        which = tl // CHUNK
        base = jnp.where(
            which == 0,
            chunks[4 * p],
            jnp.where(which == 1, chunks[4 * p + 1], jnp.where(which == 2, chunks[4 * p + 2], chunks[4 * p + 3])),
        )
        return base * CHUNK + tl % CHUNK

    key_at = lax.broadcasted_iota(jnp.int32, (BLK, HD), 0)
    kt_v[:, OWN] = kb[OWN, :].T
    for p in range(2):
        allowed = key_at <= tokens(p)
        for h in range(HEADS):
            at = pl.ds((p * HEADS + h) * HD, HD)
            s = jnp.where(allowed, dot(kb[OWN, :], qt[:, at]), -1e30)
            s_v[OWN, at] = s
            m_v[:, at] = jnp.max(s, axis=0, keepdims=True)

    local[0].wait()

    def pair_at(n):
        return pl.multiple_of(n * PAIR, PAIR)

    def scores_of(n):
        here = pl.ds(pair_at(n), PAIR)
        kblk = kb[here, :]
        kt_v[:, here] = kblk.T
        for c in range(ROWS // 256):
            at = pl.ds(c * 256, 256)
            s = dot(kblk, qt[:, at])
            s_v[here, at] = s
            m_v[:, at] = jnp.maximum(m_v[:, at], jnp.max(s, axis=0, keepdims=True))

    def gather_order(i):
        return PAIRS - 1 - i - (i == 5).astype(jnp.int32) + (i == 6).astype(jnp.int32)

    ORDER = (7, 6, 5, 4, 3, 1, 2, 0)

    def take(x, i):
        for j in range(1, PAIRS):
            @pl.when(i == j)
            def _():
                slot = 2 * ORDER[j] + 1
                x.arrived(slot)
                if slot == 13:
                    for c in x.relay:
                        c.start()
                if slot in x.far:
                    x.far[slot].start()
                x.forward(ORDER[j]).start()

    def score_step(i, carry):
        n = gather_order(i)
        take(keys, i)

        @pl.when(i == 3)
        def _():
            for c in vals.along:
                c.start()
            vals.arrived(13)
            for c in vals.relay:
                c.start()

        keys.forward(n).wait_recv()
        scores_of(n)
        return carry

    lax.fori_loop(0, PAIRS, score_step, 0)

    def output_of(at_row, size, first=False):
        here = pl.ds(at_row, size)
        vt = vb[here, :].T
        for c in range(ROWS // 256):
            at = pl.ds(c * 256, 256)
            e = jnp.exp2(s_v[here, at] * SCALE2 - m_v[:, at] * SCALE2)
            total = jnp.sum(e, axis=0, keepdims=True)
            eb = e.astype(bf16)
            p_v[here, at] = eb
            o = dot(vt, eb)
            if first:
                l_v[:, at] = total
                o_t[:, at] = o
            else:
                l_v[:, at] += total
                o_t[:, at] += o

    output_of(16 * BLK, BLK, True)
    local[1].wait()

    def take_values(i):
        for j in range(1, PAIRS):
            @pl.when(i == j)
            def _():
                slot = 2 * ORDER[j] + 1
                if slot not in (13, 11, 9):
                    vals.arrived(slot)
                    if slot in vals.far:
                        vals.far[slot].start()
                    vals.forward(ORDER[j]).start()

    def output_step(i, carry):
        n = gather_order(i)

        @pl.when(i == 0)
        def _():
            vals.forward(6).start()
            for slot in (11, 9):
                vals.arrived(slot)
                vals.far[slot].start()
                vals.forward(slot // 2).start()

        @pl.when(i == 3)
        def _():
            do_own[1].wait_recv()
            do_relay[0].start()
            do_own[2].wait_recv()
            do_relay[1].start()
            do_own[0].wait_recv()
            do_relay[2].start()
            do_relay[3].start()

        take_values(i)
        vals.forward(n).wait_recv()
        output_of(pair_at(n), PAIR)
        return carry

    lax.fori_loop(0, PAIRS, output_step, 0)

    do_relay[0].wait_recv()
    do_relay[4].start()
    do_relay[1].wait_recv()
    do_relay[5].start()

    for t in range(ROWS // HD):
        at = pl.ds(t * HD, HD)
        inv = 1.0 / l_v[:, at]
        l_v[:, at] = inv
        o_t[:, at] *= inv
        qp[at, :] = (qt[:, at].astype(f32) * (inv * SCALE)).T.astype(bf16)

    dq_t[...] = jnp.zeros_like(dq_t)

    def start_part(p):
        ag_v[...] = jnp.zeros_like(ag_v)

        def ag_step(i, carry):
            at = pl.ds(pl.multiple_of(i * 1024, 1024), 1024)
            ag_v[...] += dot_nt(w_v[:, at], do_v[p * HD:(p + 1) * HD, at])
            return carry

        lax.fori_loop(0, WIDTH // 1024, ag_step, 0)
        for h in range(HEADS):
            at = pl.ds((p * HEADS + h) * HD, HD)
            g = ag_v[h * HD:(h + 1) * HD, :].astype(bf16)
            dot_t[:, at] = g
            gf = g.astype(f32)
            delta_v[:, at] = jnp.sum(gf * o_t[:, at], axis=0, keepdims=True)
            dop[at, :] = (gf * l_v[:, at]).T.astype(bf16)

    def grads_of(at_row, size):
        here = pl.ds(at_row, size)
        vblk = vb[here, :]
        for c in range(ROWS // 256):
            at = pl.ds(c * 256, 256)
            dp = dot(vblk, dot_t[:, at])
            ds_v[0:size, at] = (p_v[here, at].astype(f32) * (dp - delta_v[:, at])).astype(bf16)
        dq_t[...] += dot(kt_v[:, here], ds_v[0:size, :])
        dk = dot(ds_v[0:size, :], qp[...])
        dv = dot(p_v[here, :], dop[...])
        return dk, dv

    local[5].wait()
    local[6].wait()
    start_part(0)
    for i in (2, 3, 4, 5):
        do_relay[i].wait_recv()
    start_part(1)

    def core_copy(n):
        return remote(csend.at[n], crecv.at[n], cs_sem.at[n], cr_sem.at[n], core)

    z_dest = (zm, zp, zp, zm, zm, zp, yhp)

    def z_copy(j):
        return remote(zs.at[j], zr.at[j], zs_sem.at[j], zr_sem.at[j], z_dest[j])

    def own_half(n):
        return pl.ds(pl.multiple_of(n * PAIR + BLK, BLK), BLK)

    def finish(n, j, extras):
        total = s_v[own_half(n), 0:2 * HD] + crecv[n].astype(f32)
        for e in extras:
            z_copy(e).wait_recv()
            total = total + zr[e].astype(f32)
        if j < 7:
            zs[j] = total.astype(bf16)
            z_copy(j).start()
        else:
            dkp_ref[...] = total[:, 0:HD].astype(bf16)
            dvp_ref[...] = total[:, HD:2 * HD].astype(bf16)

    extras_of = ((), (), (), (0,), (), (2,), (1, 3), (4, 5, 6))

    def pair_grads(n):
        dk, dv = grads_of(pair_at(n), PAIR)
        csend[n, :, 0:HD] = dk[0:BLK].astype(bf16)
        csend[n, :, HD:2 * HD] = dv[0:BLK].astype(bf16)
        core_copy(n).start()
        s_v[own_half(n), 0:HD] = dk[BLK:]
        s_v[own_half(n), HD:2 * HD] = dv[BLK:]

    def grad_step(n, carry):
        pair_grads(n)

        @pl.when(n == PAIRS - 2)
        def _():
            dk, dv = grads_of(16 * BLK, BLK)
            dvn_ref[...] = dv.astype(bf16)
            dkn_ref[...] = (dk * cos_v[...] - pltpu.roll(dk, HD // 2, 1) * sin_v[...]).astype(bf16)
            core_copy(6).wait_recv()

        for j in range(6):
            @pl.when(n == j + 1)
            def _():
                core_copy(j).wait_recv()
                finish(j, j, extras_of[j])

        @pl.when(n == PAIRS - 2)
        def _():
            finish(6, 6, extras_of[6])
        return carry

    lax.fori_loop(0, PAIRS, grad_step, 0)

    for p in range(2):
        for h in range(HEADS):
            at = pl.ds((p * HEADS + h) * HD, HD)
            g = (dq_t[:, at] * (l_v[:, at] * SCALE)).T
            for j in range(4):
                k = chunks[4 * p + j]
                x = g[j * CHUNK:(j + 1) * CHUNK, :]
                ta = pl.ds(pl.multiple_of(k * CHUNK, CHUNK), CHUNK)
                y = x * cos_v[ta, :] - pltpu.roll(x, HD // 2, 1) * sin_v[ta, :]
                dq_ref[pl.ds(pl.multiple_of(h * SEQ + k * CHUNK, CHUNK), CHUNK), :] = y.astype(bf16)

    core_copy(7).wait_recv()
    finish(7, 7, extras_of[7])

    keys.wait_send()
    vals.wait_send()
    for c in do_own + do_relay:
        c.wait_send()
    for n in range(PAIRS):
        core_copy(n).wait_send()
    for j in range(7):
        z_copy(j).wait_send()


def hand_over(*refs):
    for source, result in zip(refs[:5], refs[5:]):
        result[...] = source[...]


def local(out_grad, out_weight, queries, keys_new, values_new, keys_prompt, values_prompt, offsets):
    half = HD // 2
    frequency = np.power(np.float32(1000000.0), -(np.arange(half, dtype=np.float32) / half)).astype(np.float32)
    frequency = jnp.asarray(np.concatenate([frequency, frequency])[None, :])
    q = jnp.transpose(queries[0, :, 0], (1, 0, 2)).reshape(ROWS, HD)
    any_spec = pl.BlockSpec(memory_space=pl.ANY)
    vmem = pl.BlockSpec(memory_space=pltpu.VMEM)
    dma = pltpu.SemaphoreType.DMA
    grads = pl.pallas_call(
        kernel,
        out_shape=(
            jax.ShapeDtypeStruct((ROWS, HD), bf16),
            jax.ShapeDtypeStruct((SEQ, HD), bf16),
            jax.ShapeDtypeStruct((SEQ, HD), bf16),
            jax.ShapeDtypeStruct((BLK, HD), bf16),
            jax.ShapeDtypeStruct((BLK, HD), bf16),
        ),
        in_specs=[any_spec] * 7 + [pl.BlockSpec(memory_space=pltpu.SMEM), vmem],
        out_specs=(vmem,) * 5,
        scratch_shapes=[
            pltpu.VMEM((HEADS * HD, WIDTH), bf16),
            pltpu.VMEM((SEQ, WIDTH), bf16),
            pltpu.VMEM((17 * BLK, HD), bf16),
            pltpu.VMEM((17 * BLK, HD), bf16),
            pltpu.VMEM((HD, 17 * BLK), bf16),
            pltpu.VMEM((ROWS, HD), bf16),
            pltpu.VMEM((SEQ, HD), bf16),
            pltpu.VMEM((HD, ROWS), bf16),
            pltpu.VMEM((ROWS, HD), bf16),
            pltpu.VMEM((HD, ROWS), bf16),
            pltpu.VMEM((ROWS, HD), bf16),
            pltpu.VMEM((17 * BLK, ROWS), f32),
            pltpu.VMEM((17 * BLK, ROWS), bf16),
            pltpu.VMEM((HD, ROWS), f32),
            pltpu.VMEM((HD, ROWS), f32),
            pltpu.VMEM((1, ROWS), f32),
            pltpu.VMEM((1, ROWS), f32),
            pltpu.VMEM((1, ROWS), f32),
            pltpu.VMEM((SEQ, HD), f32),
            pltpu.VMEM((SEQ, HD), f32),
            pltpu.VMEM((PAIR, ROWS), bf16),
            pltpu.VMEM((HEADS * HD, HD), f32),
            pltpu.VMEM((PAIRS, BLK, 2 * HD), bf16),
            pltpu.VMEM((PAIRS, BLK, 2 * HD), bf16),
            pltpu.VMEM((7, BLK, 2 * HD), bf16),
            pltpu.VMEM((7, BLK, 2 * HD), bf16),
            dma((7,)),
            dma((10,)),
            dma((10,)),
            dma((7,)),
            dma((7,)),
            dma((18,)),
            dma((18,)),
            dma((9,)),
            dma((9,)),
            dma((8,)),
            dma((8,)),
            dma((7,)),
            dma((7,)),
        ],
        compiler_params=pltpu.CompilerParams(
            collective_id=0, has_side_effects=True, vmem_limit_bytes=60 * 1024 * 1024
        ),
        name="attention_backward",
    )(
        out_grad[0],
        out_weight.reshape(HEADS * HD, WIDTH),
        q,
        keys_new[0, :, 0],
        values_new[0, :, 0],
        keys_prompt[:, 0],
        values_prompt[:, 0],
        offsets,
        frequency,
    )
    dq, dkn, dvn, dkp, dvp = pl.pallas_call(
        hand_over,
        out_shape=tuple(jax.ShapeDtypeStruct(g.shape, g.dtype) for g in grads),
        in_specs=[vmem] * 5,
        out_specs=(vmem,) * 5,
        name="hand_over",
    )(*grads)
    grad_queries = jnp.transpose(dq.reshape(HEADS, SEQ, HD), (1, 0, 2))[None, :, None]
    return (
        grad_queries,
        dkn[None, :, None],
        dvn[None, :, None],
        dkp[:, None],
        dvp[:, None],
    )


def solution(mesh):
    placed = (
        P("roll", "kvh", None),
        P("kvh", None, None, None),
        P("roll", None, "kvh", None, None),
        P("roll", None, "kvh", None),
        P("roll", None, "kvh", None),
        P("roll", "kvh", None),
        P("roll", "kvh", None),
        P("roll"),
    )
    return jax.shard_map(
        local,
        mesh=mesh,
        in_specs=placed,
        out_specs=(
            P("roll", None, "kvh", None, None),
            P("roll", None, "kvh", None),
            P("roll", None, "kvh", None),
            P("roll", "kvh", None),
            P("roll", "kvh", None),
        ),
        check_vma=False,
    )
```

```python
import functools
import math

import jax
import jax.numpy as jnp
import numpy as np
from jax import lax
from jax.experimental import pallas as pl
from jax.experimental.pallas import tpu as pltpu
from jax.sharding import PartitionSpec as P

MESH = pl.DeviceIdType.MESH
f32 = jnp.float32
bf16 = jnp.bfloat16

HEADS = 5
SEQ = 256
HD = 128
ROWS = HEADS * SEQ
BLK = 256
WIDTH = 5120
PROMPT = 4096
CHUNK = 32
SCALE = HD ** -0.5
SCALE2 = SCALE * math.log2(math.e)
PAIRS = 8
PAIR = 2 * BLK
OWN = slice(16 * BLK, 17 * BLK)


def dot(a, b):
    return lax.dot_general(a, b, (((1,), (0,)), ((), ())), preferred_element_type=f32)


def dot_nt(a, b):
    return lax.dot_general(a, b, (((1,), (1,)), ((), ())), preferred_element_type=f32)


def kernel(
    og_hbm, w_hbm, q_hbm, kn_hbm, vn_hbm, kp_hbm, vp_hbm, off_ref, freq_ref,
    dq_ref, dkn_ref, dvn_ref, dkp_ref, dvp_ref,
    w_v, do_v, kb, vb, kt_v, q_v, kn_v, qt, qp, dot_t, dop, s_v, p_v, o_t, dq_t, m_v, l_v, delta_v,
    cos_v, sin_v, ag_v, csend, crecv, zs, zr,
    lsem, ksend, vsend, kfw, vfw, krecv, vrecv, dsend, drecv, cs_sem, cr_sem, zs_sem, zr_sem,
):
    roll = lax.axis_index("roll")
    kvh = lax.axis_index("kvh")
    zz, yh, cc = roll // 4, (roll // 2) % 2, roll % 2
    yl, xx = kvh // 4, kvh % 4

    def dev(dz=0, dyh=0, dc=0, dyl=0, dx=0):
        r = (((zz + dz) % 4) * 2 + (yh + dyh) % 2) * 2 + (cc + dc) % 2
        k = ((yl + dyl) % 2) * 4 + (xx + dx) % 4
        return (r, k)

    core, yhp = dev(dc=1), dev(dyh=1)
    zp, zm, z2 = dev(dz=1), dev(dz=3), dev(dz=2)
    ylp, xp, xm = dev(dyl=1), dev(dx=1), dev(dx=3)

    barrier = pltpu.get_barrier_semaphore()
    for d in (core, yhp, zp, zm, z2, ylp, xp, xm):
        pl.semaphore_signal(barrier, 1, device_id=d, device_id_type=MESH)

    local = [
        pltpu.make_async_copy(kp_hbm, kb.at[pl.ds(15 * BLK, BLK)], lsem.at[0]),
        pltpu.make_async_copy(vp_hbm, vb.at[pl.ds(15 * BLK, BLK)], lsem.at[1]),
        pltpu.make_async_copy(q_hbm, q_v, lsem.at[2]),
        pltpu.make_async_copy(kn_hbm, kn_v, lsem.at[3]),
        pltpu.make_async_copy(vn_hbm, vb.at[pl.ds(16 * BLK, BLK)], lsem.at[4]),
        pltpu.make_async_copy(og_hbm, do_v.at[pl.ds(0, CHUNK)], lsem.at[5]),
        pltpu.make_async_copy(w_hbm, w_v, lsem.at[6]),
    ]
    for c in local:
        c.start()

    pos = (off_ref[0] + PROMPT + lax.broadcasted_iota(jnp.int32, (SEQ, HD), 0)).astype(f32)
    angle = pos * freq_ref[...]
    cos_v[...] = jnp.cos(angle)
    lane = lax.broadcasted_iota(jnp.int32, (SEQ, HD), 1)
    sin_a = jnp.sin(angle)
    sin_v[...] = jnp.where(lane < HD // 2, -sin_a, sin_a)

    pl.semaphore_wait(barrier, 8)

    def remote(src, dst, ssem, rsem, d):
        return pltpu.make_async_remote_copy(
            src_ref=src, dst_ref=dst, send_sem=ssem, recv_sem=rsem, device_id=d, device_id_type=MESH
        )

    def blk(buf, slot):
        return buf.at[pl.ds(slot * BLK, BLK)]

    class Spread:
        def __init__(self, src, buf, send, recv, fsend):
            self.buf, self.send, self.recv, self.fsend = buf, send, recv, fsend
            self.own = [
                self.hop(src, s, i, d) for i, (s, d) in enumerate(((13, yhp), (11, zp), (9, zm), (7, z2), (14, core)))
            ]
            self.relay = [
                self.hop(blk(buf, 13), s, 5 + i, d) for i, (s, d) in enumerate(((5, zp), (3, zm), (1, z2)))
            ]

        def hop(self, src, slot, i, d):
            return remote(src, blk(self.buf, slot), self.send.at[i], self.recv.at[slot], d)

        def forward(self, n):
            return remote(
                blk(self.buf, 2 * n + 1), blk(self.buf, 2 * n), self.fsend.at[n], self.recv.at[2 * n], core
            )

        def take(self, n):
            slot = 2 * n + 1
            self.hop(blk(self.buf, slot), slot, 0, core).wait_recv()
            self.forward(n).start()

        def wait_send(self):
            for c in self.own + self.relay:
                c.wait_send()
            for n in range(PAIRS - 1):
                self.forward(n).wait_send()

    keys = Spread(kp_hbm, kb, ksend, krecv, kfw)
    vals = Spread(vp_hbm, vb, vsend, vrecv, vfw)
    for c in keys.own[:1] + vals.own[:1] + keys.own[1:] + vals.own[1:]:
        c.start()

    def rows(slot, lo=0, size=CHUNK):
        return do_v.at[pl.ds(slot * CHUNK + lo, size)]

    do_own = [
        remote(og_hbm, rows(1), dsend.at[0], drecv.at[0], ylp),
        remote(og_hbm.at[pl.ds(0, 16)], rows(3, 0, 16), dsend.at[1], drecv.at[1], xp),
        remote(og_hbm.at[pl.ds(16, 16)], rows(2, 16, 16), dsend.at[2], drecv.at[2], xm),
        remote(og_hbm.at[pl.ds(16, 16)], rows(3, 16, 16), dsend.at[9], drecv.at[9], xp),
        remote(og_hbm.at[pl.ds(0, 16)], rows(2, 0, 16), dsend.at[10], drecv.at[10], xm),
    ]
    do_relay = [
        remote(rows(3, 0, 16), rows(4, 0, 16), dsend.at[3], drecv.at[3], xp),
        remote(rows(2, 16, 16), rows(4, 16, 16), dsend.at[4], drecv.at[4], xm),
        remote(rows(1), rows(6), dsend.at[5], drecv.at[5], xp),
        remote(rows(1), rows(5), dsend.at[6], drecv.at[6], xm),
        remote(rows(4, 0, 16), rows(7, 0, 16), dsend.at[7], drecv.at[7], ylp),
        remote(rows(4, 16, 16), rows(7, 16, 16), dsend.at[8], drecv.at[8], ylp),
    ]
    for c in do_own:
        c.start()

    def kof(dyl, dx):
        return ((yl + dyl) % 2) * 4 + (xx + dx) % 4

    chunks = [kof(0, 0), kof(1, 0), kof(0, 1), kof(0, 3), kof(0, 2), kof(1, 1), kof(1, 3), kof(1, 2)]

    for i in (2, 3, 4):
        local[i].wait()
    kn = kn_v[...].astype(f32)
    kb[OWN, :] = (kn * cos_v[...] + pltpu.roll(kn, HD // 2, 1) * sin_v[...]).astype(bf16)
    for p in range(2):
        for h in range(HEADS):
            parts = []
            for j in range(4):
                k = chunks[4 * p + j]
                x = q_v[pl.ds(pl.multiple_of(h * SEQ + k * CHUNK, CHUNK), CHUNK), :].astype(f32)
                at = pl.ds(pl.multiple_of(k * CHUNK, CHUNK), CHUNK)
                parts.append((x * cos_v[at, :] + pltpu.roll(x, HD // 2, 1) * sin_v[at, :]))
            tile = jnp.concatenate(parts, axis=0)
            qt[:, pl.ds((p * HEADS + h) * HD, HD)] = tile.T.astype(bf16)

    tl = lax.broadcasted_iota(jnp.int32, (1, HD), 1)

    def tokens(p):
        which = tl // CHUNK
        base = jnp.where(
            which == 0,
            chunks[4 * p],
            jnp.where(which == 1, chunks[4 * p + 1], jnp.where(which == 2, chunks[4 * p + 2], chunks[4 * p + 3])),
        )
        return base * CHUNK + tl % CHUNK

    key_at = lax.broadcasted_iota(jnp.int32, (BLK, HD), 0)
    kt_v[:, OWN] = kb[OWN, :].T
    for p in range(2):
        allowed = key_at <= tokens(p)
        for h in range(HEADS):
            at = pl.ds((p * HEADS + h) * HD, HD)
            s = jnp.where(allowed, dot(kb[OWN, :], qt[:, at]), -1e30)
            s_v[OWN, at] = s
            m_v[:, at] = jnp.max(s, axis=0, keepdims=True)

    local[0].wait()

    def pair_at(n):
        return pl.multiple_of(n * PAIR, PAIR)

    def scores_of(n):
        here = pl.ds(pair_at(n), PAIR)
        kblk = kb[here, :]
        kt_v[:, here] = kblk.T
        for c in range(ROWS // 256):
            at = pl.ds(c * 256, 256)
            s = dot(kblk, qt[:, at])
            s_v[here, at] = s
            m_v[:, at] = jnp.maximum(m_v[:, at], jnp.max(s, axis=0, keepdims=True))

    def score_step(i, carry):
        n = PAIRS - 1 - i

        @pl.when(i == 1)
        def _():
            keys.take(6)
            for c in keys.relay:
                c.start()
            vals.take(6)
            for c in vals.relay:
                c.start()
            do_own[1].wait_recv()
            do_relay[0].start()
            do_own[2].wait_recv()
            do_relay[1].start()
            for j in (5, 4, 3):
                keys.take(j)

        for j, ahead in ((4, 2), (5, 1), (6, 0)):
            @pl.when(i == j)
            def _():
                keys.take(ahead)

        @pl.when(i == 6)
        def _():
            do_own[0].wait_recv()
            do_relay[2].start()
            do_relay[3].start()

        keys.forward(n).wait_recv()
        scores_of(n)
        return carry

    lax.fori_loop(0, PAIRS, score_step, 0)

    def output_of(at_row, size, first=False):
        here = pl.ds(at_row, size)
        vt = vb[here, :].T
        for c in range(ROWS // 256):
            at = pl.ds(c * 256, 256)
            e = jnp.exp2(s_v[here, at] * SCALE2 - m_v[:, at] * SCALE2)
            total = jnp.sum(e, axis=0, keepdims=True)
            eb = e.astype(bf16)
            p_v[here, at] = eb
            o = dot(vt, eb)
            if first:
                l_v[:, at] = total
                o_t[:, at] = o
            else:
                l_v[:, at] += total
                o_t[:, at] += o

    output_of(16 * BLK, BLK, True)
    local[1].wait()

    def output_step(i, carry):
        n = PAIRS - 1 - i

        @pl.when(i == 0)
        def _():
            for j in (5, 4, 3):
                vals.take(j)

        for j, ahead in ((3, 2), (4, 1), (5, 0)):
            @pl.when(i == j)
            def _():
                vals.take(ahead)

        @pl.when(i == 1)
        def _():
            do_relay[0].wait_recv()
            do_relay[4].start()
            do_relay[1].wait_recv()
            do_relay[5].start()

        vals.forward(n).wait_recv()
        output_of(pair_at(n), PAIR)
        return carry

    lax.fori_loop(0, PAIRS, output_step, 0)

    for t in range(ROWS // HD):
        at = pl.ds(t * HD, HD)
        inv = 1.0 / l_v[:, at]
        l_v[:, at] = inv
        o_t[:, at] *= inv
        qp[at, :] = (qt[:, at].astype(f32) * (inv * SCALE)).T.astype(bf16)

    def start_part(p):
        ag_v[...] = jnp.zeros_like(ag_v)

        def ag_step(i, carry):
            at = pl.ds(pl.multiple_of(i * 1024, 1024), 1024)
            ag_v[...] += dot_nt(w_v[:, at], do_v[p * HD:(p + 1) * HD, at])
            return carry

        lax.fori_loop(0, WIDTH // 1024, ag_step, 0)
        for h in range(HEADS):
            at = pl.ds((p * HEADS + h) * HD, HD)
            g = ag_v[h * HD:(h + 1) * HD, :].astype(bf16)
            dot_t[:, at] = g
            gf = g.astype(f32)
            delta_v[:, at] = jnp.sum(gf * o_t[:, at], axis=0, keepdims=True)
            dop[at, :] = (gf * l_v[:, at]).T.astype(bf16)

    def grads_of(at_row, size):
        here = pl.ds(at_row, size)
        vblk = vb[here, :]
        dv = dot(p_v[here, :], dop[...])
        for c in range(ROWS // 256):
            at = pl.ds(c * 256, 256)
            dp = dot(vblk, dot_t[:, at])
            p_v[here, at] = (p_v[here, at].astype(f32) * (dp - delta_v[:, at])).astype(bf16)
        dk = dot(p_v[here, :], qp[...])
        return dk, dv

    local[5].wait()
    local[6].wait()
    do_own[3].wait_recv()
    do_own[4].wait_recv()
    start_part(0)
    for i in (2, 3, 4, 5):
        do_relay[i].wait_recv()
    start_part(1)

    def core_copy(n):
        return remote(csend.at[n], crecv.at[n], cs_sem.at[n], cr_sem.at[n], core)

    z_dest = (z2, zp, zm, z2, zp, zm, yhp)

    def z_copy(j):
        return remote(zs.at[j], zr.at[j], zs_sem.at[j], zr_sem.at[j], z_dest[j])

    def own_half(n):
        return pl.ds(pl.multiple_of(n * PAIR + BLK, BLK), BLK)

    def finish(n, j, extras):
        total = s_v[own_half(n), 0:2 * HD] + crecv[n].astype(f32)
        for e in extras:
            z_copy(e).wait_recv()
            total = total + zr[e].astype(f32)
        if j < 7:
            zs[j] = total.astype(bf16)
            z_copy(j).start()
        else:
            dkp_ref[...] = total[:, 0:HD].astype(bf16)
            dvp_ref[...] = total[:, HD:2 * HD].astype(bf16)

    extras_of = ((), (), (), (), (), (), (0, 1, 2), (3, 4, 5, 6))

    def pair_grads(n):
        dk, dv = grads_of(pair_at(n), PAIR)
        csend[n, :, 0:HD] = dk[0:BLK].astype(bf16)
        csend[n, :, HD:2 * HD] = dv[0:BLK].astype(bf16)
        core_copy(n).start()
        s_v[own_half(n), 0:HD] = dk[BLK:]
        s_v[own_half(n), HD:2 * HD] = dv[BLK:]

    def grad_step(n, carry):
        pair_grads(n)

        for j in range(6):
            @pl.when(n == j + 1)
            def _():
                core_copy(j).wait_recv()
                finish(j, j, extras_of[j])

        return carry

    lax.fori_loop(0, PAIRS, grad_step, 0)

    dk, dv = grads_of(16 * BLK, BLK)
    dvn_ref[...] = dv.astype(bf16)
    dkn_ref[...] = (dk * cos_v[...] - pltpu.roll(dk, HD // 2, 1) * sin_v[...]).astype(bf16)
    core_copy(6).wait_recv()
    finish(6, 6, extras_of[6])

    def query_step(c, carry):
        at = pl.ds(pl.multiple_of(c * 256, 256), 256)
        dq_t[:, at] = dot(kt_v[...], p_v[:, at])
        return carry

    lax.fori_loop(0, ROWS // 256, query_step, 0)
    for p in range(2):
        for h in range(HEADS):
            at = pl.ds((p * HEADS + h) * HD, HD)
            g = (dq_t[:, at] * (l_v[:, at] * SCALE)).T
            for j in range(4):
                k = chunks[4 * p + j]
                x = g[j * CHUNK:(j + 1) * CHUNK, :]
                ta = pl.ds(pl.multiple_of(k * CHUNK, CHUNK), CHUNK)
                y = x * cos_v[ta, :] - pltpu.roll(x, HD // 2, 1) * sin_v[ta, :]
                dq_ref[pl.ds(pl.multiple_of(h * SEQ + k * CHUNK, CHUNK), CHUNK), :] = y.astype(bf16)

    core_copy(7).wait_recv()
    finish(7, 7, extras_of[7])

    keys.wait_send()
    vals.wait_send()
    for c in do_own + do_relay:
        c.wait_send()
    for n in range(PAIRS):
        core_copy(n).wait_send()
    for j in range(7):
        z_copy(j).wait_send()


def hand_over(*refs):
    for source, result in zip(refs[:5], refs[5:]):
        result[...] = source[...]


def local(out_grad, out_weight, queries, keys_new, values_new, keys_prompt, values_prompt, offsets):
    half = HD // 2
    frequency = np.power(np.float32(1000000.0), -(np.arange(half, dtype=np.float32) / half)).astype(np.float32)
    frequency = jnp.asarray(np.concatenate([frequency, frequency])[None, :])
    q = jnp.transpose(queries[0, :, 0], (1, 0, 2)).reshape(ROWS, HD)
    any_spec = pl.BlockSpec(memory_space=pl.ANY)
    vmem = pl.BlockSpec(memory_space=pltpu.VMEM)
    dma = pltpu.SemaphoreType.DMA
    grads = pl.pallas_call(
        kernel,
        out_shape=(
            jax.ShapeDtypeStruct((ROWS, HD), bf16),
            jax.ShapeDtypeStruct((SEQ, HD), bf16),
            jax.ShapeDtypeStruct((SEQ, HD), bf16),
            jax.ShapeDtypeStruct((BLK, HD), bf16),
            jax.ShapeDtypeStruct((BLK, HD), bf16),
        ),
        in_specs=[any_spec] * 7 + [pl.BlockSpec(memory_space=pltpu.SMEM), vmem],
        out_specs=(vmem,) * 5,
        scratch_shapes=[
            pltpu.VMEM((HEADS * HD, WIDTH), bf16),
            pltpu.VMEM((SEQ, WIDTH), bf16),
            pltpu.VMEM((17 * BLK, HD), bf16),
            pltpu.VMEM((17 * BLK, HD), bf16),
            pltpu.VMEM((HD, 17 * BLK), bf16),
            pltpu.VMEM((ROWS, HD), bf16),
            pltpu.VMEM((SEQ, HD), bf16),
            pltpu.VMEM((HD, ROWS), bf16),
            pltpu.VMEM((ROWS, HD), bf16),
            pltpu.VMEM((HD, ROWS), bf16),
            pltpu.VMEM((ROWS, HD), bf16),
            pltpu.VMEM((17 * BLK, ROWS), f32),
            pltpu.VMEM((17 * BLK, ROWS), bf16),
            pltpu.VMEM((HD, ROWS), f32),
            pltpu.VMEM((HD, ROWS), f32),
            pltpu.VMEM((1, ROWS), f32),
            pltpu.VMEM((1, ROWS), f32),
            pltpu.VMEM((1, ROWS), f32),
            pltpu.VMEM((SEQ, HD), f32),
            pltpu.VMEM((SEQ, HD), f32),
            pltpu.VMEM((HEADS * HD, HD), f32),
            pltpu.VMEM((PAIRS, BLK, 2 * HD), bf16),
            pltpu.VMEM((PAIRS, BLK, 2 * HD), bf16),
            pltpu.VMEM((7, BLK, 2 * HD), bf16),
            pltpu.VMEM((7, BLK, 2 * HD), bf16),
            dma((7,)),
            dma((8,)),
            dma((8,)),
            dma((7,)),
            dma((7,)),
            dma((16,)),
            dma((16,)),
            dma((11,)),
            dma((11,)),
            dma((8,)),
            dma((8,)),
            dma((7,)),
            dma((7,)),
        ],
        compiler_params=pltpu.CompilerParams(
            collective_id=0, has_side_effects=True, vmem_limit_bytes=60 * 1024 * 1024
        ),
        name="attention_backward",
    )(
        out_grad[0],
        out_weight.reshape(HEADS * HD, WIDTH),
        q,
        keys_new[0, :, 0],
        values_new[0, :, 0],
        keys_prompt[:, 0],
        values_prompt[:, 0],
        offsets,
        frequency,
    )
    dq, dkn, dvn, dkp, dvp = pl.pallas_call(
        hand_over,
        out_shape=tuple(jax.ShapeDtypeStruct(g.shape, g.dtype) for g in grads),
        in_specs=[vmem] * 5,
        out_specs=(vmem,) * 5,
        name="hand_over",
    )(*grads)
    grad_queries = jnp.transpose(dq.reshape(HEADS, SEQ, HD), (1, 0, 2))[None, :, None]
    return (
        grad_queries,
        dkn[None, :, None],
        dvn[None, :, None],
        dkp[:, None],
        dvp[:, None],
    )


def solution(mesh):
    placed = (
        P("roll", "kvh", None),
        P("kvh", None, None, None),
        P("roll", None, "kvh", None, None),
        P("roll", None, "kvh", None),
        P("roll", None, "kvh", None),
        P("roll", "kvh", None),
        P("roll", "kvh", None),
        P("roll"),
    )
    return jax.shard_map(
        local,
        mesh=mesh,
        in_specs=placed,
        out_specs=(
            P("roll", None, "kvh", None, None),
            P("roll", None, "kvh", None),
            P("roll", None, "kvh", None),
            P("roll", "kvh", None),
            P("roll", "kvh", None),
        ),
        check_vma=False,
    )
```

```python
import functools
import math

import jax
import jax.numpy as jnp
import numpy as np
from jax import lax
from jax.experimental import pallas as pl
from jax.experimental.pallas import tpu as pltpu
from jax.sharding import PartitionSpec as P

MESH = pl.DeviceIdType.MESH
f32 = jnp.float32
bf16 = jnp.bfloat16

HEADS = 5
SEQ = 256
HD = 128
ROWS = HEADS * SEQ
BLK = 256
WIDTH = 5120
PROMPT = 4096
CHUNK = 32
SCALE = HD ** -0.5
SCALE2 = SCALE * math.log2(math.e)
PAIRS = 8
PAIR = 2 * BLK
OWN = slice(16 * BLK, 17 * BLK)


def dot(a, b):
    return lax.dot_general(a, b, (((1,), (0,)), ((), ())), preferred_element_type=f32)


def dot_nt(a, b):
    return lax.dot_general(a, b, (((1,), (1,)), ((), ())), preferred_element_type=f32)


def kernel(
    og_hbm, w_hbm, q_hbm, kn_hbm, vn_hbm, kp_hbm, vp_hbm, off_ref, freq_ref,
    dq_ref, dkn_ref, dvn_ref, dkp_ref, dvp_ref,
    w_v, do_v, kb, vb, kt_v, q_v, kn_v, qt, qp, dot_t, dop, s_v, p_v, o_t, dq_t, m_v, l_v, delta_v,
    cos_v, sin_v, ds_v, ag_v, csend, crecv, zs, zr,
    lsem, ksend, vsend, kfw, vfw, krecv, vrecv, dsend, drecv, cs_sem, cr_sem, zs_sem, zr_sem,
):
    roll = lax.axis_index("roll")
    kvh = lax.axis_index("kvh")
    zz, yh, cc = roll // 4, (roll // 2) % 2, roll % 2
    yl, xx = kvh // 4, kvh % 4

    def dev(dz=0, dyh=0, dc=0, dyl=0, dx=0):
        r = (((zz + dz) % 4) * 2 + (yh + dyh) % 2) * 2 + (cc + dc) % 2
        k = ((yl + dyl) % 2) * 4 + (xx + dx) % 4
        return (r, k)

    core, yhp = dev(dc=1), dev(dyh=1)
    zp, zm, z2 = dev(dz=1), dev(dz=3), dev(dz=2)
    ylp, xp, xm = dev(dyl=1), dev(dx=1), dev(dx=3)

    barrier = pltpu.get_barrier_semaphore()
    for d in (core, yhp, zp, zm, z2, ylp, xp, xm):
        pl.semaphore_signal(barrier, 1, device_id=d, device_id_type=MESH)

    local = [
        pltpu.make_async_copy(kp_hbm, kb.at[pl.ds(15 * BLK, BLK)], lsem.at[0]),
        pltpu.make_async_copy(vp_hbm, vb.at[pl.ds(15 * BLK, BLK)], lsem.at[1]),
        pltpu.make_async_copy(q_hbm, q_v, lsem.at[2]),
        pltpu.make_async_copy(kn_hbm, kn_v, lsem.at[3]),
        pltpu.make_async_copy(vn_hbm, vb.at[pl.ds(16 * BLK, BLK)], lsem.at[4]),
        pltpu.make_async_copy(og_hbm, do_v.at[pl.ds(0, CHUNK)], lsem.at[5]),
        pltpu.make_async_copy(w_hbm, w_v, lsem.at[6]),
    ]
    for c in local:
        c.start()

    pos = (off_ref[0] + PROMPT + lax.broadcasted_iota(jnp.int32, (SEQ, HD), 0)).astype(f32)
    angle = pos * freq_ref[...]
    cos_v[...] = jnp.cos(angle)
    lane = lax.broadcasted_iota(jnp.int32, (SEQ, HD), 1)
    sin_a = jnp.sin(angle)
    sin_v[...] = jnp.where(lane < HD // 2, -sin_a, sin_a)

    pl.semaphore_wait(barrier, 8)

    def remote(src, dst, ssem, rsem, d):
        return pltpu.make_async_remote_copy(
            src_ref=src, dst_ref=dst, send_sem=ssem, recv_sem=rsem, device_id=d, device_id_type=MESH
        )

    def blk(buf, slot):
        return buf.at[pl.ds(slot * BLK, BLK)]

    class Spread:
        def __init__(self, src, buf, send, recv, fsend):
            self.buf, self.send, self.recv, self.fsend = buf, send, recv, fsend
            self.own = [
                self.hop(src, s, i, d) for i, (s, d) in enumerate(((13, yhp), (11, zp), (9, zm), (7, z2), (14, core)))
            ]
            self.relay = [
                self.hop(blk(buf, 13), s, 5 + i, d) for i, (s, d) in enumerate(((5, zp), (3, zm), (1, z2)))
            ]

        def hop(self, src, slot, i, d):
            return remote(src, blk(self.buf, slot), self.send.at[i], self.recv.at[slot], d)

        def forward(self, n):
            return remote(
                blk(self.buf, 2 * n + 1), blk(self.buf, 2 * n), self.fsend.at[n], self.recv.at[2 * n], core
            )

        def take(self, n):
            slot = 2 * n + 1
            self.hop(blk(self.buf, slot), slot, 0, core).wait_recv()
            self.forward(n).start()

        def wait_send(self):
            for c in self.own + self.relay:
                c.wait_send()
            for n in range(PAIRS - 1):
                self.forward(n).wait_send()

    keys = Spread(kp_hbm, kb, ksend, krecv, kfw)
    vals = Spread(vp_hbm, vb, vsend, vrecv, vfw)
    for c in keys.own[:1] + vals.own[:1] + keys.own[1:] + vals.own[1:]:
        c.start()

    mid = WIDTH // 2

    def rows(slot, lo=0, size=CHUNK, col=0, width=WIDTH):
        return do_v.at[pl.ds(slot * CHUNK + lo, size), pl.ds(col, width)]

    do_own = [
        remote(og_hbm, rows(1), dsend.at[0], drecv.at[0], ylp),
        remote(og_hbm.at[pl.ds(0, 16)], rows(3, 0, 16), dsend.at[1], drecv.at[1], xp),
        remote(og_hbm.at[pl.ds(16, 16)], rows(2, 16, 16), dsend.at[2], drecv.at[2], xm),
        remote(og_hbm.at[pl.ds(16, 16)], rows(3, 16, 16), dsend.at[9], drecv.at[9], xp),
        remote(og_hbm.at[pl.ds(0, 16)], rows(2, 0, 16), dsend.at[10], drecv.at[10], xm),
    ]
    do_relay = [
        remote(rows(3, 0, 16), rows(4, 0, 16), dsend.at[3], drecv.at[3], xp),
        remote(rows(2, 16, 16), rows(4, 16, 16), dsend.at[4], drecv.at[4], xm),
    ]
    pair_relay = [
        remote(rows(1, 0, CHUNK, col, mid), rows(slot, 0, CHUNK, col, mid), dsend.at[i], drecv.at[i], d)
        for i, col, slot, d in ((5, 0, 6, xp), (6, 0, 5, xm), (7, mid, 6, xp), (8, mid, 5, xm))
    ]
    last_relay = [
        remote(rows(4, lo, 16, col, mid), rows(7, lo, 16, col, mid), dsend.at[i], drecv.at[i], ylp)
        for i, col, lo in ((11, 0, 0), (12, 0, 16), (13, mid, 0), (14, mid, 16))
    ]
    for c in do_own:
        c.start()

    def kof(dyl, dx):
        return ((yl + dyl) % 2) * 4 + (xx + dx) % 4

    chunks = [kof(0, 0), kof(1, 0), kof(0, 1), kof(0, 3), kof(0, 2), kof(1, 1), kof(1, 3), kof(1, 2)]

    for i in (2, 3, 4):
        local[i].wait()
    kn = kn_v[...].astype(f32)
    kb[OWN, :] = (kn * cos_v[...] + pltpu.roll(kn, HD // 2, 1) * sin_v[...]).astype(bf16)
    for p in range(2):
        for h in range(HEADS):
            parts = []
            for j in range(4):
                k = chunks[4 * p + j]
                x = q_v[pl.ds(pl.multiple_of(h * SEQ + k * CHUNK, CHUNK), CHUNK), :].astype(f32)
                at = pl.ds(pl.multiple_of(k * CHUNK, CHUNK), CHUNK)
                parts.append((x * cos_v[at, :] + pltpu.roll(x, HD // 2, 1) * sin_v[at, :]))
            tile = jnp.concatenate(parts, axis=0)
            qt[:, pl.ds((p * HEADS + h) * HD, HD)] = tile.T.astype(bf16)

    tl = lax.broadcasted_iota(jnp.int32, (1, HD), 1)

    def tokens(p):
        which = tl // CHUNK
        base = jnp.where(
            which == 0,
            chunks[4 * p],
            jnp.where(which == 1, chunks[4 * p + 1], jnp.where(which == 2, chunks[4 * p + 2], chunks[4 * p + 3])),
        )
        return base * CHUNK + tl % CHUNK

    key_at = lax.broadcasted_iota(jnp.int32, (BLK, HD), 0)
    kt_v[:, OWN] = kb[OWN, :].T
    for p in range(2):
        allowed = key_at <= tokens(p)
        for h in range(HEADS):
            at = pl.ds((p * HEADS + h) * HD, HD)
            s = jnp.where(allowed, dot(kb[OWN, :], qt[:, at]), -1e30)
            s_v[OWN, at] = s
            m_v[:, at] = jnp.max(s, axis=0, keepdims=True)

    local[0].wait()

    def pair_at(n):
        return pl.multiple_of(n * PAIR, PAIR)

    def scores_of(n):
        here = pl.ds(pair_at(n), PAIR)
        kblk = kb[here, :]
        kt_v[:, here] = kblk.T
        for c in range(ROWS // 256):
            at = pl.ds(c * 256, 256)
            s = dot(kblk, qt[:, at])
            s_v[here, at] = s
            m_v[:, at] = jnp.maximum(m_v[:, at], jnp.max(s, axis=0, keepdims=True))

    def project(p, part):
        tokens_at = slice(p * HD, (p + 1) * HD)

        def step(i, carry):
            at = pl.ds(pl.multiple_of(part * mid + i * 1280, 1280), 1280)
            ag_v[p] += dot_nt(w_v[:, at], do_v[tokens_at, at])
            return carry

        lax.fori_loop(0, mid // 1280, step, 0)

    ag_v[...] = jnp.zeros_like(ag_v)

    def score_step(i, carry):
        n = PAIRS - 1 - i

        @pl.when(i == 1)
        def _():
            keys.take(6)
            for c in keys.relay:
                c.start()
            vals.take(6)
            for c in vals.relay:
                c.start()
            do_own[1].wait_recv()
            do_relay[0].start()
            do_own[2].wait_recv()
            do_relay[1].start()
            for j in (5, 4, 3):
                keys.take(j)

        for j, ahead in ((4, 2), (5, 1), (6, 0)):
            @pl.when(i == j)
            def _():
                keys.take(ahead)

        @pl.when(i == 6)
        def _():
            do_own[0].wait_recv()
            for c in pair_relay:
                c.start()
            do_own[3].wait_recv()
            do_own[4].wait_recv()
            local[5].wait()
            local[6].wait()
            project(0, 0)
            project(0, 1)

        keys.forward(n).wait_recv()
        scores_of(n)
        return carry

    lax.fori_loop(0, PAIRS, score_step, 0)

    def output_of(at_row, size, first=False):
        here = pl.ds(at_row, size)
        vt = vb[here, :].T
        for c in range(ROWS // 256):
            at = pl.ds(c * 256, 256)
            e = jnp.exp2(s_v[here, at] * SCALE2 - m_v[:, at] * SCALE2)
            total = jnp.sum(e, axis=0, keepdims=True)
            eb = e.astype(bf16)
            p_v[here, at] = eb
            o = dot(vt, eb)
            if first:
                l_v[:, at] = total
                o_t[:, at] = o
            else:
                l_v[:, at] += total
                o_t[:, at] += o

    output_of(16 * BLK, BLK, True)
    local[1].wait()

    def output_step(i, carry):
        n = PAIRS - 1 - i

        @pl.when(i == 0)
        def _():
            for j in (5, 4, 3):
                vals.take(j)

        for j, ahead in ((3, 2), (4, 1), (5, 0)):
            @pl.when(i == j)
            def _():
                vals.take(ahead)

        @pl.when(i == 1)
        def _():
            for c in do_relay:
                c.wait_recv()
            for c in last_relay:
                c.start()

        vals.forward(n).wait_recv()
        output_of(pair_at(n), PAIR)
        return carry

    lax.fori_loop(0, PAIRS, output_step, 0)

    for t in range(ROWS // HD):
        at = pl.ds(t * HD, HD)
        inv = 1.0 / l_v[:, at]
        l_v[:, at] = inv
        o_t[:, at] *= inv
        qp[at, :] = (qt[:, at].astype(f32) * (inv * SCALE)).T.astype(bf16)

    def row_terms(p):
        for h in range(HEADS):
            at = pl.ds((p * HEADS + h) * HD, HD)
            g = ag_v[p, h * HD:(h + 1) * HD, :].astype(bf16)
            dot_t[:, at] = g
            gf = g.astype(f32)
            delta_v[:, at] = jnp.sum(gf * o_t[:, at], axis=0, keepdims=True)
            dop[at, :] = (gf * l_v[:, at]).T.astype(bf16)

    def grads_of(at_row, size, ds, col):
        here = pl.ds(at_row, size)
        vblk = vb[here, :]
        for c in range(ROWS // 256):
            at = pl.ds(c * 256, 256)
            dp = dot(vblk, dot_t[:, at])
            ds[:, pl.ds(col + c * 256, 256)] = (p_v[here, at].astype(f32) * (dp - delta_v[:, at])).astype(bf16)
        dk = dot(ds[:, pl.ds(col, ROWS)], qp[...])
        dv = dot(p_v[here, :], dop[...])
        return dk, dv

    row_terms(0)
    for c in (pair_relay[0], pair_relay[1], last_relay[0], last_relay[1]):
        c.wait_recv()
    project(1, 0)
    for c in (pair_relay[2], pair_relay[3], last_relay[2], last_relay[3]):
        c.wait_recv()
    project(1, 1)
    row_terms(1)

    def core_copy(n):
        return remote(csend.at[n], crecv.at[n], cs_sem.at[n], cr_sem.at[n], core)

    z_dest = (z2, zp, zm, z2, zp, zm, yhp)

    def z_copy(j):
        return remote(zs.at[j], zr.at[j], zs_sem.at[j], zr_sem.at[j], z_dest[j])

    def own_half(n):
        return pl.ds(pl.multiple_of(n * PAIR + BLK, BLK), BLK)

    def finish(n, j, extras):
        total = s_v[own_half(n), 0:2 * HD] + crecv[n].astype(f32)
        for e in extras:
            z_copy(e).wait_recv()
            total = total + zr[e].astype(f32)
        if j < 7:
            zs[j] = total.astype(bf16)
            z_copy(j).start()
        else:
            dkp_ref[...] = total[:, 0:HD].astype(bf16)
            dvp_ref[...] = total[:, HD:2 * HD].astype(bf16)

    extras_of = ((), (), (), (), (), (), (0, 1, 2), (3, 4, 5, 6))

    def pair_grads(n, ds, col):
        dk, dv = grads_of(pair_at(n), PAIR, ds, col)
        csend[n, :, 0:HD] = dk[0:BLK].astype(bf16)
        csend[n, :, HD:2 * HD] = dv[0:BLK].astype(bf16)
        core_copy(n).start()
        s_v[own_half(n), 0:HD] = dk[BLK:]
        s_v[own_half(n), HD:2 * HD] = dv[BLK:]

        for j in range(6):
            @pl.when(n == j + 1)
            def _():
                core_copy(j).wait_recv()
                finish(j, j, extras_of[j])

    def first_step(n, carry):
        pair_grads(n, w_v.at[pl.ds(0, PAIR)], pl.multiple_of(n * ROWS, ROWS))
        return carry

    lax.fori_loop(0, PAIRS // 2, first_step, 0)

    def second_step(n, carry):
        pair_grads(n, ds_v.at[pl.ds(pl.multiple_of((n - PAIRS // 2) * PAIR, PAIR), PAIR)], 0)
        return carry

    lax.fori_loop(PAIRS // 2, PAIRS, second_step, 0)

    dk, dv = grads_of(16 * BLK, BLK, ds_v.at[pl.ds(8 * BLK, BLK)], 0)
    dvn_ref[...] = dv.astype(bf16)
    dkn_ref[...] = (dk * cos_v[...] - pltpu.roll(dk, HD // 2, 1) * sin_v[...]).astype(bf16)
    core_copy(6).wait_recv()
    finish(6, 6, extras_of[6])

    def query_step(c, carry):
        at = pl.ds(pl.multiple_of(c * 256, 256), 256)
        total = dot(kt_v[:, 8 * BLK:], ds_v[:, at])
        for n in range(PAIRS // 2):
            total += dot(
                kt_v[:, n * PAIR:(n + 1) * PAIR], w_v[0:PAIR, pl.ds(pl.multiple_of(n * ROWS + c * 256, 256), 256)]
            )
        dq_t[:, at] = total
        return carry

    lax.fori_loop(0, ROWS // 256, query_step, 0)
    for p in range(2):
        for h in range(HEADS):
            at = pl.ds((p * HEADS + h) * HD, HD)
            g = (dq_t[:, at] * (l_v[:, at] * SCALE)).T
            for j in range(4):
                k = chunks[4 * p + j]
                x = g[j * CHUNK:(j + 1) * CHUNK, :]
                ta = pl.ds(pl.multiple_of(k * CHUNK, CHUNK), CHUNK)
                y = x * cos_v[ta, :] - pltpu.roll(x, HD // 2, 1) * sin_v[ta, :]
                dq_ref[pl.ds(pl.multiple_of(h * SEQ + k * CHUNK, CHUNK), CHUNK), :] = y.astype(bf16)

    core_copy(7).wait_recv()
    finish(7, 7, extras_of[7])

    keys.wait_send()
    vals.wait_send()
    for c in do_own + do_relay + pair_relay + last_relay:
        c.wait_send()
    for n in range(PAIRS):
        core_copy(n).wait_send()
    for j in range(7):
        z_copy(j).wait_send()


def hand_over(*refs):
    for source, result in zip(refs[:5], refs[5:]):
        result[...] = source[...]


def local(out_grad, out_weight, queries, keys_new, values_new, keys_prompt, values_prompt, offsets):
    half = HD // 2
    frequency = np.power(np.float32(1000000.0), -(np.arange(half, dtype=np.float32) / half)).astype(np.float32)
    frequency = jnp.asarray(np.concatenate([frequency, frequency])[None, :])
    q = jnp.transpose(queries[0, :, 0], (1, 0, 2)).reshape(ROWS, HD)
    any_spec = pl.BlockSpec(memory_space=pl.ANY)
    vmem = pl.BlockSpec(memory_space=pltpu.VMEM)
    dma = pltpu.SemaphoreType.DMA
    grads = pl.pallas_call(
        kernel,
        out_shape=(
            jax.ShapeDtypeStruct((ROWS, HD), bf16),
            jax.ShapeDtypeStruct((SEQ, HD), bf16),
            jax.ShapeDtypeStruct((SEQ, HD), bf16),
            jax.ShapeDtypeStruct((BLK, HD), bf16),
            jax.ShapeDtypeStruct((BLK, HD), bf16),
        ),
        in_specs=[any_spec] * 7 + [pl.BlockSpec(memory_space=pltpu.SMEM), vmem],
        out_specs=(vmem,) * 5,
        scratch_shapes=[
            pltpu.VMEM((HEADS * HD, WIDTH), bf16),
            pltpu.VMEM((SEQ, WIDTH), bf16),
            pltpu.VMEM((17 * BLK, HD), bf16),
            pltpu.VMEM((17 * BLK, HD), bf16),
            pltpu.VMEM((HD, 17 * BLK), bf16),
            pltpu.VMEM((ROWS, HD), bf16),
            pltpu.VMEM((SEQ, HD), bf16),
            pltpu.VMEM((HD, ROWS), bf16),
            pltpu.VMEM((ROWS, HD), bf16),
            pltpu.VMEM((HD, ROWS), bf16),
            pltpu.VMEM((ROWS, HD), bf16),
            pltpu.VMEM((17 * BLK, ROWS), f32),
            pltpu.VMEM((17 * BLK, ROWS), bf16),
            pltpu.VMEM((HD, ROWS), f32),
            pltpu.VMEM((HD, ROWS), f32),
            pltpu.VMEM((1, ROWS), f32),
            pltpu.VMEM((1, ROWS), f32),
            pltpu.VMEM((1, ROWS), f32),
            pltpu.VMEM((SEQ, HD), f32),
            pltpu.VMEM((SEQ, HD), f32),
            pltpu.VMEM((9 * BLK, ROWS), bf16),
            pltpu.VMEM((2, HEADS * HD, HD), f32),
            pltpu.VMEM((PAIRS, BLK, 2 * HD), bf16),
            pltpu.VMEM((PAIRS, BLK, 2 * HD), bf16),
            pltpu.VMEM((7, BLK, 2 * HD), bf16),
            pltpu.VMEM((7, BLK, 2 * HD), bf16),
            dma((7,)),
            dma((8,)),
            dma((8,)),
            dma((7,)),
            dma((7,)),
            dma((16,)),
            dma((16,)),
            dma((15,)),
            dma((15,)),
            dma((8,)),
            dma((8,)),
            dma((7,)),
            dma((7,)),
        ],
        compiler_params=pltpu.CompilerParams(
            collective_id=0, has_side_effects=True, vmem_limit_bytes=60 * 1024 * 1024
        ),
        name="attention_backward",
    )(
        out_grad[0],
        out_weight.reshape(HEADS * HD, WIDTH),
        q,
        keys_new[0, :, 0],
        values_new[0, :, 0],
        keys_prompt[:, 0],
        values_prompt[:, 0],
        offsets,
        frequency,
    )
    dq, dkn, dvn, dkp, dvp = pl.pallas_call(
        hand_over,
        out_shape=tuple(jax.ShapeDtypeStruct(g.shape, g.dtype) for g in grads),
        in_specs=[vmem] * 5,
        out_specs=(vmem,) * 5,
        name="hand_over",
    )(*grads)
    grad_queries = jnp.transpose(dq.reshape(HEADS, SEQ, HD), (1, 0, 2))[None, :, None]
    return (
        grad_queries,
        dkn[None, :, None],
        dvn[None, :, None],
        dkp[:, None],
        dvp[:, None],
    )


def solution(mesh):
    placed = (
        P("roll", "kvh", None),
        P("kvh", None, None, None),
        P("roll", None, "kvh", None, None),
        P("roll", None, "kvh", None),
        P("roll", None, "kvh", None),
        P("roll", "kvh", None),
        P("roll", "kvh", None),
        P("roll"),
    )
    return jax.shard_map(
        local,
        mesh=mesh,
        in_specs=placed,
        out_specs=(
            P("roll", None, "kvh", None, None),
            P("roll", None, "kvh", None),
            P("roll", None, "kvh", None),
            P("roll", "kvh", None),
            P("roll", "kvh", None),
        ),
        check_vma=False,
    )
```

```python
import functools
import math

import jax
import jax.numpy as jnp
import numpy as np
from jax import lax
from jax.experimental import pallas as pl
from jax.experimental.pallas import tpu as pltpu
from jax.sharding import PartitionSpec as P

MESH = pl.DeviceIdType.MESH
f32 = jnp.float32
bf16 = jnp.bfloat16

HEADS = 5
SEQ = 256
HD = 128
ROWS = HEADS * SEQ
BLK = 256
WIDTH = 5120
PROMPT = 4096
CHUNK = 32
SCALE = HD ** -0.5
SCALE2 = SCALE * math.log2(math.e)
PAIRS = 8
PAIR = 2 * BLK
OWN = slice(16 * BLK, 17 * BLK)


def dot(a, b):
    return lax.dot_general(a, b, (((1,), (0,)), ((), ())), preferred_element_type=f32)


def dot_nt(a, b):
    return lax.dot_general(a, b, (((1,), (1,)), ((), ())), preferred_element_type=f32)


def kernel(
    og_hbm, w_hbm, q_hbm, kn_hbm, vn_hbm, kp_hbm, vp_hbm, off_ref, freq_ref,
    dq_ref, dkn_ref, dvn_ref, dkp_ref, dvp_ref,
    w_v, do_v, kb, vb, kt_v, q_v, kn_v, qt, qp, dot_t, dop, s_v, p_v, o_t, dq_t, m_v, l_v, delta_v,
    cos_v, sin_v, ds_v, ag_v, csend, crecv, zs, zr,
    lsem, ksend, vsend, kfw, vfw, krecv, vrecv, dsend, drecv, cs_sem, cr_sem, zs_sem, zr_sem,
):
    roll = lax.axis_index("roll")
    kvh = lax.axis_index("kvh")
    zz, yh, cc = roll // 4, (roll // 2) % 2, roll % 2
    yl, xx = kvh // 4, kvh % 4

    def dev(dz=0, dyh=0, dc=0, dyl=0, dx=0):
        r = (((zz + dz) % 4) * 2 + (yh + dyh) % 2) * 2 + (cc + dc) % 2
        k = ((yl + dyl) % 2) * 4 + (xx + dx) % 4
        return (r, k)

    core, yhp = dev(dc=1), dev(dyh=1)
    zp, zm, z2 = dev(dz=1), dev(dz=3), dev(dz=2)
    ylp, xp, xm = dev(dyl=1), dev(dx=1), dev(dx=3)

    barrier = pltpu.get_barrier_semaphore()
    for d in (core, yhp, zp, zm, z2, ylp, xp, xm):
        pl.semaphore_signal(barrier, 1, device_id=d, device_id_type=MESH)

    local = [
        pltpu.make_async_copy(kp_hbm, kb.at[pl.ds(15 * BLK, BLK)], lsem.at[0]),
        pltpu.make_async_copy(vp_hbm, vb.at[pl.ds(15 * BLK, BLK)], lsem.at[1]),
        pltpu.make_async_copy(q_hbm, q_v, lsem.at[2]),
        pltpu.make_async_copy(kn_hbm, kn_v, lsem.at[3]),
        pltpu.make_async_copy(vn_hbm, vb.at[pl.ds(16 * BLK, BLK)], lsem.at[4]),
        pltpu.make_async_copy(og_hbm, do_v.at[pl.ds(0, CHUNK)], lsem.at[5]),
        pltpu.make_async_copy(w_hbm, w_v, lsem.at[6]),
    ]
    for c in local:
        c.start()

    pos = (off_ref[0] + PROMPT + lax.broadcasted_iota(jnp.int32, (SEQ, HD), 0)).astype(f32)
    angle = pos * freq_ref[...]
    cos_v[...] = jnp.cos(angle)
    lane = lax.broadcasted_iota(jnp.int32, (SEQ, HD), 1)
    sin_a = jnp.sin(angle)
    sin_v[...] = jnp.where(lane < HD // 2, -sin_a, sin_a)

    pl.semaphore_wait(barrier, 8)

    def remote(src, dst, ssem, rsem, d):
        return pltpu.make_async_remote_copy(
            src_ref=src, dst_ref=dst, send_sem=ssem, recv_sem=rsem, device_id=d, device_id_type=MESH
        )

    def blk(buf, slot):
        return buf.at[pl.ds(slot * BLK, BLK)]

    class Spread:
        def __init__(self, src, buf, send, recv, fsend):
            self.buf, self.send, self.recv, self.fsend = buf, send, recv, fsend
            self.own = [
                self.hop(src, s, i, d) for i, (s, d) in enumerate(((13, yhp), (11, zp), (9, zm), (7, z2), (14, core)))
            ]
            self.relay = [
                self.hop(blk(buf, 13), s, 5 + i, d) for i, (s, d) in enumerate(((5, zp), (3, zm), (1, z2)))
            ]

        def hop(self, src, slot, i, d):
            return remote(src, blk(self.buf, slot), self.send.at[i], self.recv.at[slot], d)

        def forward(self, n):
            return remote(
                blk(self.buf, 2 * n + 1), blk(self.buf, 2 * n), self.fsend.at[n], self.recv.at[2 * n], core
            )

        def take(self, n):
            slot = 2 * n + 1
            self.hop(blk(self.buf, slot), slot, 0, core).wait_recv()
            self.forward(n).start()

        def wait_send(self):
            for c in self.own + self.relay:
                c.wait_send()
            for n in range(PAIRS - 1):
                self.forward(n).wait_send()

    keys = Spread(kp_hbm, kb, ksend, krecv, kfw)
    vals = Spread(vp_hbm, vb, vsend, vrecv, vfw)
    for c in keys.own[:1] + vals.own[:1] + keys.own[1:] + vals.own[1:]:
        c.start()

    mid = WIDTH // 2

    def rows(slot, lo=0, size=CHUNK, col=0, width=WIDTH):
        return do_v.at[pl.ds(slot * CHUNK + lo, size), pl.ds(col, width)]

    do_own = [
        remote(og_hbm, rows(1), dsend.at[0], drecv.at[0], ylp),
        remote(og_hbm.at[pl.ds(0, 16)], rows(3, 0, 16), dsend.at[1], drecv.at[1], xp),
        remote(og_hbm.at[pl.ds(16, 16)], rows(2, 16, 16), dsend.at[2], drecv.at[2], xm),
        remote(og_hbm.at[pl.ds(16, 16)], rows(3, 16, 16), dsend.at[9], drecv.at[9], xp),
        remote(og_hbm.at[pl.ds(0, 16)], rows(2, 0, 16), dsend.at[10], drecv.at[10], xm),
    ]
    do_relay = [
        remote(rows(3, 0, 16), rows(4, 0, 16), dsend.at[3], drecv.at[3], xp),
        remote(rows(2, 16, 16), rows(4, 16, 16), dsend.at[4], drecv.at[4], xm),
    ]
    pair_relay = [
        remote(rows(1, 0, CHUNK, col, mid), rows(slot, 0, CHUNK, col, mid), dsend.at[i], drecv.at[i], d)
        for i, col, slot, d in ((5, 0, 6, xp), (6, 0, 5, xm), (7, mid, 6, xp), (8, mid, 5, xm))
    ]
    last_relay = [
        remote(rows(4, lo, 16, col, mid), rows(7, lo, 16, col, mid), dsend.at[i], drecv.at[i], ylp)
        for i, col, lo in ((11, 0, 0), (12, 0, 16), (13, mid, 0), (14, mid, 16))
    ]
    for c in do_own:
        c.start()

    def kof(dyl, dx):
        return ((yl + dyl) % 2) * 4 + (xx + dx) % 4

    chunks = [kof(0, 0), kof(1, 0), kof(0, 1), kof(0, 3), kof(0, 2), kof(1, 1), kof(1, 3), kof(1, 2)]

    for i in (2, 3, 4):
        local[i].wait()
    kn = kn_v[...].astype(f32)
    kb[OWN, :] = (kn * cos_v[...] + pltpu.roll(kn, HD // 2, 1) * sin_v[...]).astype(bf16)
    for p in range(2):
        for h in range(HEADS):
            parts = []
            for j in range(4):
                k = chunks[4 * p + j]
                x = q_v[pl.ds(pl.multiple_of(h * SEQ + k * CHUNK, CHUNK), CHUNK), :].astype(f32)
                at = pl.ds(pl.multiple_of(k * CHUNK, CHUNK), CHUNK)
                parts.append((x * cos_v[at, :] + pltpu.roll(x, HD // 2, 1) * sin_v[at, :]))
            tile = jnp.concatenate(parts, axis=0)
            qt[:, pl.ds((p * HEADS + h) * HD, HD)] = tile.T.astype(bf16)

    tl = lax.broadcasted_iota(jnp.int32, (1, HD), 1)

    def tokens(p):
        which = tl // CHUNK
        base = jnp.where(
            which == 0,
            chunks[4 * p],
            jnp.where(which == 1, chunks[4 * p + 1], jnp.where(which == 2, chunks[4 * p + 2], chunks[4 * p + 3])),
        )
        return base * CHUNK + tl % CHUNK

    key_at = lax.broadcasted_iota(jnp.int32, (BLK, HD), 0)
    kt_v[:, OWN] = kb[OWN, :].T
    for p in range(2):
        allowed = key_at <= tokens(p)
        for h in range(HEADS):
            at = pl.ds((p * HEADS + h) * HD, HD)
            s = jnp.where(allowed, dot(kb[OWN, :], qt[:, at]), -1e30)
            s_v[OWN, at] = s
            m_v[:, at] = jnp.max(s, axis=0, keepdims=True)

    local[0].wait()

    def pair_at(n):
        return pl.multiple_of(n * PAIR, PAIR)

    def scores_of(n):
        here = pl.ds(pair_at(n), PAIR)
        kblk = kb[here, :]
        kt_v[:, here] = kblk.T
        for c in range(ROWS // 256):
            at = pl.ds(c * 256, 256)
            s = dot(kblk, qt[:, at])
            s_v[here, at] = s
            m_v[:, at] = jnp.maximum(m_v[:, at], jnp.max(s, axis=0, keepdims=True))

    def project(p, part):
        tokens_at = slice(p * HD, (p + 1) * HD)

        def step(i, carry):
            at = pl.ds(pl.multiple_of(part * mid + i * 1280, 1280), 1280)
            ag_v[p] += dot_nt(w_v[:, at], do_v[tokens_at, at])
            return carry

        lax.fori_loop(0, mid // 1280, step, 0)

    ag_v[...] = jnp.zeros_like(ag_v)

    def score_step(i, carry):
        n = PAIRS - 1 - i

        @pl.when(i == 1)
        def _():
            keys.take(6)
            for c in keys.relay:
                c.start()
            vals.take(6)
            for c in vals.relay:
                c.start()
            do_own[1].wait_recv()
            do_relay[0].start()
            do_own[2].wait_recv()
            do_relay[1].start()
            for j in (5, 4, 3):
                keys.take(j)

        for j, ahead in ((4, 2), (5, 1), (6, 0)):
            @pl.when(i == j)
            def _():
                keys.take(ahead)

        @pl.when(i == 6)
        def _():
            do_own[0].wait_recv()
            for c in pair_relay:
                c.start()
            do_own[3].wait_recv()
            do_own[4].wait_recv()
            local[5].wait()
            local[6].wait()
            project(0, 0)
            project(0, 1)

        keys.forward(n).wait_recv()
        scores_of(n)
        return carry

    lax.fori_loop(0, PAIRS, score_step, 0)

    def output_of(at_row, size, first=False):
        here = pl.ds(at_row, size)
        vt = vb[here, :].T
        for c in range(ROWS // 256):
            at = pl.ds(c * 256, 256)
            e = jnp.exp2(s_v[here, at] * SCALE2 - m_v[:, at] * SCALE2)
            total = jnp.sum(e, axis=0, keepdims=True)
            eb = e.astype(bf16)
            p_v[here, at] = eb
            o = dot(vt, eb)
            if first:
                l_v[:, at] = total
                o_t[:, at] = o
            else:
                l_v[:, at] += total
                o_t[:, at] += o

    output_of(16 * BLK, BLK, True)
    local[1].wait()

    def output_step(i, carry):
        n = PAIRS - 1 - i

        @pl.when(i == 0)
        def _():
            for j in (5, 4, 3):
                vals.take(j)

        for j, ahead in ((3, 2), (4, 1), (5, 0)):
            @pl.when(i == j)
            def _():
                vals.take(ahead)

        @pl.when(i == 1)
        def _():
            for c in do_relay:
                c.wait_recv()
            for c in last_relay:
                c.start()

        vals.forward(n).wait_recv()
        output_of(pair_at(n), PAIR)
        return carry

    lax.fori_loop(0, PAIRS, output_step, 0)

    for t in range(ROWS // HD):
        at = pl.ds(t * HD, HD)
        inv = 1.0 / l_v[:, at]
        l_v[:, at] = inv
        o_t[:, at] *= inv
        qp[at, :] = (qt[:, at].astype(f32) * (inv * SCALE)).T.astype(bf16)

    def row_terms(p):
        for h in range(HEADS):
            at = pl.ds((p * HEADS + h) * HD, HD)
            g = ag_v[p, h * HD:(h + 1) * HD, :].astype(bf16)
            dot_t[:, at] = g
            gf = g.astype(f32)
            delta_v[:, at] = jnp.sum(gf * o_t[:, at], axis=0, keepdims=True)
            dop[at, :] = (gf * l_v[:, at]).T.astype(bf16)

    def value_grads(at_row, size):
        return dot(p_v[pl.ds(at_row, size), :], dop[...])

    def key_grads(at_row, size, ds, col):
        here = pl.ds(at_row, size)
        vblk = vb[here, :]
        for c in range(ROWS // 256):
            at = pl.ds(c * 256, 256)
            dp = dot(vblk, dot_t[:, at])
            ds[:, pl.ds(col + c * 256, 256)] = (p_v[here, at].astype(f32) * (dp - delta_v[:, at])).astype(bf16)
        return dot(ds[:, pl.ds(col, ROWS)], qp[...])

    row_terms(0)
    for c in (pair_relay[0], pair_relay[1], last_relay[0], last_relay[1]):
        c.wait_recv()
    project(1, 0)
    for c in (pair_relay[2], pair_relay[3], last_relay[2], last_relay[3]):
        c.wait_recv()
    project(1, 1)
    row_terms(1)

    def own_half(n):
        return pl.ds(pl.multiple_of(n * PAIR + BLK, BLK), BLK)

    z_dest = (z2, zp, zm, z2, zp, zm, yhp)
    extras_of = ((), (), (), (), (), (), (0, 1, 2), (3, 4, 5, 6))

    class Sums:
        def __init__(self, kind, col, out):
            self.kind, self.col, self.out = kind, pl.ds(col, HD), out

        def core(self, n):
            k = self.kind
            return remote(csend.at[k, n], crecv.at[k, n], cs_sem.at[k, n], cr_sem.at[k, n], core)

        def z(self, j):
            k = self.kind
            return remote(zs.at[k, j], zr.at[k, j], zs_sem.at[k, j], zr_sem.at[k, j], z_dest[j])

        def give(self, n, grads):
            csend[self.kind, n] = grads[0:BLK].astype(bf16)
            self.core(n).start()
            s_v[own_half(n), self.col] = grads[BLK:]

        def finish(self, j):
            self.core(j).wait_recv()
            total = s_v[own_half(j), self.col] + crecv[self.kind, j].astype(f32)
            for e in extras_of[j]:
                self.z(e).wait_recv()
                total = total + zr[self.kind, e].astype(f32)
            if j < 7:
                zs[self.kind, j] = total.astype(bf16)
                self.z(j).start()
            else:
                self.out[...] = total.astype(bf16)

        def wait_send(self):
            for n in range(PAIRS):
                self.core(n).wait_send()
            for j in range(7):
                self.z(j).wait_send()

    key_sums = Sums(0, 0, dkp_ref)
    value_sums = Sums(1, HD, dvp_ref)

    def value_step(n, carry):
        value_sums.give(n, value_grads(pair_at(n), PAIR))
        for j in range(6):
            @pl.when(n == j + 2)
            def _():
                value_sums.finish(j)
        return carry

    lax.fori_loop(0, PAIRS, value_step, 0)

    def pair_grads(n, ds, col):
        key_sums.give(n, key_grads(pair_at(n), PAIR, ds, col))

        for j in range(6):
            @pl.when(n == j + 1)
            def _():
                key_sums.finish(j)

        @pl.when(n == 4)
        def _():
            value_sums.finish(6)

    def first_step(n, carry):
        pair_grads(n, w_v.at[pl.ds(0, PAIR)], pl.multiple_of(n * ROWS, ROWS))
        return carry

    lax.fori_loop(0, PAIRS // 2, first_step, 0)

    def second_step(n, carry):
        pair_grads(n, ds_v.at[pl.ds(pl.multiple_of((n - PAIRS // 2) * PAIR, PAIR), PAIR)], 0)
        return carry

    lax.fori_loop(PAIRS // 2, PAIRS, second_step, 0)

    dvn_ref[...] = value_grads(16 * BLK, BLK).astype(bf16)
    dk = key_grads(16 * BLK, BLK, ds_v.at[pl.ds(8 * BLK, BLK)], 0)
    dkn_ref[...] = (dk * cos_v[...] - pltpu.roll(dk, HD // 2, 1) * sin_v[...]).astype(bf16)
    key_sums.finish(6)

    def query_step(c, carry):
        at = pl.ds(pl.multiple_of(c * 256, 256), 256)
        total = dot(kt_v[:, 8 * BLK:], ds_v[:, at])
        for n in range(PAIRS // 2):
            total += dot(
                kt_v[:, n * PAIR:(n + 1) * PAIR], w_v[0:PAIR, pl.ds(pl.multiple_of(n * ROWS + c * 256, 256), 256)]
            )
        dq_t[:, at] = total
        return carry

    lax.fori_loop(0, ROWS // 256, query_step, 0)
    for p in range(2):
        for h in range(HEADS):
            at = pl.ds((p * HEADS + h) * HD, HD)
            g = (dq_t[:, at] * (l_v[:, at] * SCALE)).T
            for j in range(4):
                k = chunks[4 * p + j]
                x = g[j * CHUNK:(j + 1) * CHUNK, :]
                ta = pl.ds(pl.multiple_of(k * CHUNK, CHUNK), CHUNK)
                y = x * cos_v[ta, :] - pltpu.roll(x, HD // 2, 1) * sin_v[ta, :]
                dq_ref[pl.ds(pl.multiple_of(h * SEQ + k * CHUNK, CHUNK), CHUNK), :] = y.astype(bf16)

    value_sums.finish(7)
    key_sums.finish(7)

    keys.wait_send()
    vals.wait_send()
    for c in do_own + do_relay + pair_relay + last_relay:
        c.wait_send()
    key_sums.wait_send()
    value_sums.wait_send()


def hand_over(*refs):
    for source, result in zip(refs[:5], refs[5:]):
        result[...] = source[...]


def local(out_grad, out_weight, queries, keys_new, values_new, keys_prompt, values_prompt, offsets):
    half = HD // 2
    frequency = np.power(np.float32(1000000.0), -(np.arange(half, dtype=np.float32) / half)).astype(np.float32)
    frequency = jnp.asarray(np.concatenate([frequency, frequency])[None, :])
    q = jnp.transpose(queries[0, :, 0], (1, 0, 2)).reshape(ROWS, HD)
    any_spec = pl.BlockSpec(memory_space=pl.ANY)
    vmem = pl.BlockSpec(memory_space=pltpu.VMEM)
    dma = pltpu.SemaphoreType.DMA
    grads = pl.pallas_call(
        kernel,
        out_shape=(
            jax.ShapeDtypeStruct((ROWS, HD), bf16),
            jax.ShapeDtypeStruct((SEQ, HD), bf16),
            jax.ShapeDtypeStruct((SEQ, HD), bf16),
            jax.ShapeDtypeStruct((BLK, HD), bf16),
            jax.ShapeDtypeStruct((BLK, HD), bf16),
        ),
        in_specs=[any_spec] * 7 + [pl.BlockSpec(memory_space=pltpu.SMEM), vmem],
        out_specs=(vmem,) * 5,
        scratch_shapes=[
            pltpu.VMEM((HEADS * HD, WIDTH), bf16),
            pltpu.VMEM((SEQ, WIDTH), bf16),
            pltpu.VMEM((17 * BLK, HD), bf16),
            pltpu.VMEM((17 * BLK, HD), bf16),
            pltpu.VMEM((HD, 17 * BLK), bf16),
            pltpu.VMEM((ROWS, HD), bf16),
            pltpu.VMEM((SEQ, HD), bf16),
            pltpu.VMEM((HD, ROWS), bf16),
            pltpu.VMEM((ROWS, HD), bf16),
            pltpu.VMEM((HD, ROWS), bf16),
            pltpu.VMEM((ROWS, HD), bf16),
            pltpu.VMEM((17 * BLK, ROWS), f32),
            pltpu.VMEM((17 * BLK, ROWS), bf16),
            pltpu.VMEM((HD, ROWS), f32),
            pltpu.VMEM((HD, ROWS), f32),
            pltpu.VMEM((1, ROWS), f32),
            pltpu.VMEM((1, ROWS), f32),
            pltpu.VMEM((1, ROWS), f32),
            pltpu.VMEM((SEQ, HD), f32),
            pltpu.VMEM((SEQ, HD), f32),
            pltpu.VMEM((9 * BLK, ROWS), bf16),
            pltpu.VMEM((2, HEADS * HD, HD), f32),
            pltpu.VMEM((2, PAIRS, BLK, HD), bf16),
            pltpu.VMEM((2, PAIRS, BLK, HD), bf16),
            pltpu.VMEM((2, 7, BLK, HD), bf16),
            pltpu.VMEM((2, 7, BLK, HD), bf16),
            dma((7,)),
            dma((8,)),
            dma((8,)),
            dma((7,)),
            dma((7,)),
            dma((16,)),
            dma((16,)),
            dma((15,)),
            dma((15,)),
            dma((2, 8)),
            dma((2, 8)),
            dma((2, 7)),
            dma((2, 7)),
        ],
        compiler_params=pltpu.CompilerParams(
            collective_id=0, has_side_effects=True, vmem_limit_bytes=60 * 1024 * 1024
        ),
        name="attention_backward",
    )(
        out_grad[0],
        out_weight.reshape(HEADS * HD, WIDTH),
        q,
        keys_new[0, :, 0],
        values_new[0, :, 0],
        keys_prompt[:, 0],
        values_prompt[:, 0],
        offsets,
        frequency,
    )
    dq, dkn, dvn, dkp, dvp = pl.pallas_call(
        hand_over,
        out_shape=tuple(jax.ShapeDtypeStruct(g.shape, g.dtype) for g in grads),
        in_specs=[vmem] * 5,
        out_specs=(vmem,) * 5,
        name="hand_over",
    )(*grads)
    grad_queries = jnp.transpose(dq.reshape(HEADS, SEQ, HD), (1, 0, 2))[None, :, None]
    return (
        grad_queries,
        dkn[None, :, None],
        dvn[None, :, None],
        dkp[:, None],
        dvp[:, None],
    )


def solution(mesh):
    placed = (
        P("roll", "kvh", None),
        P("kvh", None, None, None),
        P("roll", None, "kvh", None, None),
        P("roll", None, "kvh", None),
        P("roll", None, "kvh", None),
        P("roll", "kvh", None),
        P("roll", "kvh", None),
        P("roll"),
    )
    return jax.shard_map(
        local,
        mesh=mesh,
        in_specs=placed,
        out_specs=(
            P("roll", None, "kvh", None, None),
            P("roll", None, "kvh", None),
            P("roll", None, "kvh", None),
            P("roll", "kvh", None),
            P("roll", "kvh", None),
        ),
        check_vma=False,
    )
```

```python
import functools
import math

import jax
import jax.numpy as jnp
import numpy as np
from jax import lax
from jax.experimental import pallas as pl
from jax.experimental.pallas import tpu as pltpu
from jax.sharding import PartitionSpec as P

MESH = pl.DeviceIdType.MESH
f32 = jnp.float32
bf16 = jnp.bfloat16

HEADS = 5
SEQ = 256
HD = 128
ROWS = HEADS * SEQ
BLK = 256
WIDTH = 5120
PROMPT = 4096
CHUNK = 32
SCALE = HD ** -0.5
SCALE2 = SCALE * math.log2(math.e)
PAIRS = 8
PAIR = 2 * BLK
OWN = slice(16 * BLK, 17 * BLK)


def dot(a, b):
    return lax.dot_general(a, b, (((1,), (0,)), ((), ())), preferred_element_type=f32)


def dot_nt(a, b):
    return lax.dot_general(a, b, (((1,), (1,)), ((), ())), preferred_element_type=f32)


def kernel(
    og_hbm, w_hbm, q_hbm, kn_hbm, vn_hbm, kp_hbm, vp_hbm, off_ref, freq_ref,
    dq_ref, dkn_ref, dvn_ref, dkp_ref, dvp_ref,
    w_v, do_v, kb, vb, kt_v, q_v, kn_v, qt, qp, dot_t, dop, s_v, p_v, o_t, dq_t, m_v, l_v, delta_v,
    cos_v, sin_v, ds_v, ag_v, csend, crecv, zs, zr,
    lsem, ksend, vsend, kfw, vfw, krecv, vrecv, dsend, drecv, cs_sem, cr_sem, zs_sem, zr_sem,
):
    roll = lax.axis_index("roll")
    kvh = lax.axis_index("kvh")
    zz, yh, cc = roll // 4, (roll // 2) % 2, roll % 2
    yl, xx = kvh // 4, kvh % 4

    def dev(dz=0, dyh=0, dc=0, dyl=0, dx=0):
        r = (((zz + dz) % 4) * 2 + (yh + dyh) % 2) * 2 + (cc + dc) % 2
        k = ((yl + dyl) % 2) * 4 + (xx + dx) % 4
        return (r, k)

    core, yhp = dev(dc=1), dev(dyh=1)
    zp, zm, z2 = dev(dz=1), dev(dz=3), dev(dz=2)
    ylp, xp, xm = dev(dyl=1), dev(dx=1), dev(dx=3)

    barrier = pltpu.get_barrier_semaphore()
    for d in (core, yhp, zp, zm, z2, ylp, xp, xm):
        pl.semaphore_signal(barrier, 1, device_id=d, device_id_type=MESH)

    local = [
        pltpu.make_async_copy(kp_hbm, kb.at[pl.ds(15 * BLK, BLK)], lsem.at[0]),
        pltpu.make_async_copy(vp_hbm, vb.at[pl.ds(15 * BLK, BLK)], lsem.at[1]),
        pltpu.make_async_copy(q_hbm, q_v, lsem.at[2]),
        pltpu.make_async_copy(kn_hbm, kn_v, lsem.at[3]),
        pltpu.make_async_copy(vn_hbm, vb.at[pl.ds(16 * BLK, BLK)], lsem.at[4]),
        pltpu.make_async_copy(og_hbm, do_v.at[pl.ds(0, CHUNK)], lsem.at[5]),
        pltpu.make_async_copy(w_hbm, w_v, lsem.at[6]),
    ]
    for c in local:
        c.start()

    pos = (off_ref[0] + PROMPT + lax.broadcasted_iota(jnp.int32, (SEQ, HD), 0)).astype(f32)
    angle = pos * freq_ref[...]
    cos_v[...] = jnp.cos(angle)
    lane = lax.broadcasted_iota(jnp.int32, (SEQ, HD), 1)
    sin_a = jnp.sin(angle)
    sin_v[...] = jnp.where(lane < HD // 2, -sin_a, sin_a)

    pl.semaphore_wait(barrier, 8)

    def remote(src, dst, ssem, rsem, d):
        return pltpu.make_async_remote_copy(
            src_ref=src, dst_ref=dst, send_sem=ssem, recv_sem=rsem, device_id=d, device_id_type=MESH
        )

    def blk(buf, slot):
        return buf.at[pl.ds(slot * BLK, BLK)]

    class Spread:
        def __init__(self, src, buf, send, recv, fsend):
            self.buf, self.send, self.recv, self.fsend = buf, send, recv, fsend
            self.own = [
                self.hop(src, s, i, d) for i, (s, d) in enumerate(((13, yhp), (11, zp), (9, zm), (7, z2), (14, core)))
            ]
            self.relay = [
                self.hop(blk(buf, 13), s, 5 + i, d) for i, (s, d) in enumerate(((5, zp), (3, zm), (1, z2)))
            ]

        def hop(self, src, slot, i, d):
            return remote(src, blk(self.buf, slot), self.send.at[i], self.recv.at[slot], d)

        def forward(self, n):
            return remote(
                blk(self.buf, 2 * n + 1), blk(self.buf, 2 * n), self.fsend.at[n], self.recv.at[2 * n], core
            )

        def take(self, n):
            slot = 2 * n + 1
            self.hop(blk(self.buf, slot), slot, 0, core).wait_recv()
            self.forward(n).start()

        def wait_send(self):
            for c in self.own + self.relay:
                c.wait_send()
            for n in range(PAIRS - 1):
                self.forward(n).wait_send()

    keys = Spread(kp_hbm, kb, ksend, krecv, kfw)
    vals = Spread(vp_hbm, vb, vsend, vrecv, vfw)
    for c in keys.own:
        c.start()

    mid = WIDTH // 2

    def rows(slot, lo=0, size=CHUNK, col=0, width=WIDTH):
        return do_v.at[pl.ds(slot * CHUNK + lo, size), pl.ds(col, width)]

    do_own = [
        remote(og_hbm, rows(1), dsend.at[0], drecv.at[0], ylp),
        remote(og_hbm.at[pl.ds(0, 16)], rows(3, 0, 16), dsend.at[1], drecv.at[1], xp),
        remote(og_hbm.at[pl.ds(16, 16)], rows(2, 16, 16), dsend.at[2], drecv.at[2], xm),
        remote(og_hbm.at[pl.ds(16, 16)], rows(3, 16, 16), dsend.at[9], drecv.at[9], xp),
        remote(og_hbm.at[pl.ds(0, 16)], rows(2, 0, 16), dsend.at[10], drecv.at[10], xm),
    ]
    do_relay = [
        remote(rows(3, 0, 16), rows(4, 0, 16), dsend.at[3], drecv.at[3], xp),
        remote(rows(2, 16, 16), rows(4, 16, 16), dsend.at[4], drecv.at[4], xm),
    ]
    pair_relay = [
        remote(rows(1, 0, CHUNK, col, mid), rows(slot, 0, CHUNK, col, mid), dsend.at[i], drecv.at[i], d)
        for i, col, slot, d in ((5, 0, 6, xp), (6, 0, 5, xm), (7, mid, 6, xp), (8, mid, 5, xm))
    ]
    last_relay = [
        remote(rows(4, lo, 16, col, mid), rows(7, lo, 16, col, mid), dsend.at[i], drecv.at[i], ylp)
        for i, col, lo in ((11, 0, 0), (12, 0, 16), (13, mid, 0), (14, mid, 16))
    ]
    for c in do_own[1:]:
        c.start()

    def kof(dyl, dx):
        return ((yl + dyl) % 2) * 4 + (xx + dx) % 4

    chunks = [kof(0, 0), kof(1, 0), kof(0, 1), kof(0, 3), kof(0, 2), kof(1, 1), kof(1, 3), kof(1, 2)]

    for i in (2, 3, 4):
        local[i].wait()
    kn = kn_v[...].astype(f32)
    kb[OWN, :] = (kn * cos_v[...] + pltpu.roll(kn, HD // 2, 1) * sin_v[...]).astype(bf16)
    for p in range(2):
        for h in range(HEADS):
            parts = []
            for j in range(4):
                k = chunks[4 * p + j]
                x = q_v[pl.ds(pl.multiple_of(h * SEQ + k * CHUNK, CHUNK), CHUNK), :].astype(f32)
                at = pl.ds(pl.multiple_of(k * CHUNK, CHUNK), CHUNK)
                parts.append((x * cos_v[at, :] + pltpu.roll(x, HD // 2, 1) * sin_v[at, :]))
            tile = jnp.concatenate(parts, axis=0)
            qt[:, pl.ds((p * HEADS + h) * HD, HD)] = tile.T.astype(bf16)

    for c in do_own[:1] + vals.own:
        c.start()

    tl = lax.broadcasted_iota(jnp.int32, (1, HD), 1)

    def tokens(p):
        which = tl // CHUNK
        base = jnp.where(
            which == 0,
            chunks[4 * p],
            jnp.where(which == 1, chunks[4 * p + 1], jnp.where(which == 2, chunks[4 * p + 2], chunks[4 * p + 3])),
        )
        return base * CHUNK + tl % CHUNK

    key_at = lax.broadcasted_iota(jnp.int32, (BLK, HD), 0)
    kt_v[:, OWN] = kb[OWN, :].T
    for p in range(2):
        allowed = key_at <= tokens(p)
        for h in range(HEADS):
            at = pl.ds((p * HEADS + h) * HD, HD)
            s = jnp.where(allowed, dot(kb[OWN, :], qt[:, at]), -1e30)
            s_v[OWN, at] = s
            m_v[:, at] = jnp.max(s, axis=0, keepdims=True)

    local[0].wait()

    def pair_at(n):
        return pl.multiple_of(n * PAIR, PAIR)

    def scores_of(n):
        here = pl.ds(pair_at(n), PAIR)
        kblk = kb[here, :]
        kt_v[:, here] = kblk.T
        for c in range(ROWS // 256):
            at = pl.ds(c * 256, 256)
            s = dot(kblk, qt[:, at])
            s_v[here, at] = s
            m_v[:, at] = jnp.maximum(m_v[:, at], jnp.max(s, axis=0, keepdims=True))

    def project(p, part):
        tokens_at = slice(p * HD, (p + 1) * HD)

        def step(i, carry):
            at = pl.ds(pl.multiple_of(part * mid + i * 1280, 1280), 1280)
            ag_v[p] += dot_nt(w_v[:, at], do_v[tokens_at, at])
            return carry

        lax.fori_loop(0, mid // 1280, step, 0)

    ag_v[...] = jnp.zeros_like(ag_v)

    def score_step(i, carry):
        n = PAIRS - 1 - i

        @pl.when(i == 1)
        def _():
            keys.take(6)
            for c in keys.relay:
                c.start()
            do_own[1].wait_recv()
            do_relay[0].start()
            do_own[2].wait_recv()
            do_relay[1].start()
            for j in (5, 4, 3):
                keys.take(j)

        @pl.when(i == 3)
        def _():
            vals.take(6)
            for c in vals.relay:
                c.start()

        @pl.when(i == 5)
        def _():
            do_own[0].wait_recv()
            for c in pair_relay:
                c.start()
            do_own[3].wait_recv()
            do_own[4].wait_recv()
            local[5].wait()
            local[6].wait()
            project(0, 0)
            project(0, 1)
            for c in do_relay:
                c.wait_recv()
            for c in last_relay:
                c.start()
            for j in (2, 1, 0):
                keys.take(j)

        @pl.when(i == 7)
        def _():
            for j in (5, 4, 3):
                vals.take(j)

        keys.forward(n).wait_recv()
        scores_of(n)
        return carry

    lax.fori_loop(0, PAIRS, score_step, 0)

    def output_of(at_row, size, first=False):
        here = pl.ds(at_row, size)
        vt = vb[here, :].T
        for c in range(ROWS // 256):
            at = pl.ds(c * 256, 256)
            e = jnp.exp2(s_v[here, at] * SCALE2 - m_v[:, at] * SCALE2)
            total = jnp.sum(e, axis=0, keepdims=True)
            eb = e.astype(bf16)
            p_v[here, at] = eb
            o = dot(vt, eb)
            if first:
                l_v[:, at] = total
                o_t[:, at] = o
            else:
                l_v[:, at] += total
                o_t[:, at] += o

    output_of(16 * BLK, BLK, True)
    local[1].wait()

    def output_step(i, carry):
        n = PAIRS - 1 - i

        for j, ahead in ((3, 2), (4, 1), (5, 0)):
            @pl.when(i == j)
            def _():
                vals.take(ahead)

        vals.forward(n).wait_recv()
        output_of(pair_at(n), PAIR)
        return carry

    lax.fori_loop(0, PAIRS, output_step, 0)

    for t in range(ROWS // HD):
        at = pl.ds(t * HD, HD)
        inv = 1.0 / l_v[:, at]
        l_v[:, at] = inv
        o_t[:, at] *= inv
        qp[at, :] = (qt[:, at].astype(f32) * (inv * SCALE)).T.astype(bf16)

    def row_terms(p):
        for h in range(HEADS):
            at = pl.ds((p * HEADS + h) * HD, HD)
            g = ag_v[p, h * HD:(h + 1) * HD, :].astype(bf16)
            dot_t[:, at] = g
            gf = g.astype(f32)
            delta_v[:, at] = jnp.sum(gf * o_t[:, at], axis=0, keepdims=True)
            dop[at, :] = (gf * l_v[:, at]).T.astype(bf16)

    def value_grads(at_row, size):
        return dot(p_v[pl.ds(at_row, size), :], dop[...])

    def score_grads(at_row, size, ds, col):
        here = pl.ds(at_row, size)
        vblk = vb[here, :]
        for c in range(ROWS // 256):
            at = pl.ds(c * 256, 256)
            dp = dot(vblk, dot_t[:, at])
            ds[:, pl.ds(col + c * 256, 256)] = (p_v[here, at].astype(f32) * (dp - delta_v[:, at])).astype(bf16)

    def key_grads(ds, col):
        return dot(ds[:, pl.ds(col, ROWS)], qp[...])

    row_terms(0)
    for c in (pair_relay[0], pair_relay[1], last_relay[0], last_relay[1]):
        c.wait_recv()
    project(1, 0)
    for c in (pair_relay[2], pair_relay[3], last_relay[2], last_relay[3]):
        c.wait_recv()
    project(1, 1)
    row_terms(1)

    def own_half(n):
        return pl.ds(pl.multiple_of(n * PAIR + BLK, BLK), BLK)

    z_dest = (z2, zp, zm, z2, zp, zm, yhp)
    extras_of = ((), (), (), (), (), (), (0, 1, 2), (3, 4, 5, 6))

    class Sums:
        def __init__(self, kind, col, out):
            self.kind, self.col, self.out = kind, pl.ds(col, HD), out

        def core(self, n):
            k = self.kind
            return remote(csend.at[k, n], crecv.at[k, n], cs_sem.at[k, n], cr_sem.at[k, n], core)

        def z(self, j):
            k = self.kind
            return remote(zs.at[k, j], zr.at[k, j], zs_sem.at[k, j], zr_sem.at[k, j], z_dest[j])

        def give(self, n, grads):
            csend[self.kind, n] = grads[0:BLK].astype(bf16)
            self.core(n).start()
            s_v[own_half(n), self.col] = grads[BLK:]

        def finish(self, j):
            self.core(j).wait_recv()
            total = s_v[own_half(j), self.col] + crecv[self.kind, j].astype(f32)
            for e in extras_of[j]:
                self.z(e).wait_recv()
                total = total + zr[self.kind, e].astype(f32)
            if j < 7:
                zs[self.kind, j] = total.astype(bf16)
                self.z(j).start()
            else:
                self.out[...] = total.astype(bf16)

        def wait_send(self):
            for n in range(PAIRS):
                self.core(n).wait_send()
            for j in range(7):
                self.z(j).wait_send()

    key_sums = Sums(0, 0, dkp_ref)
    value_sums = Sums(1, HD, dvp_ref)

    VSTEP = 2

    def value_step(i, carry):
        grads = value_grads(pair_at(i * VSTEP), VSTEP * PAIR)
        for j in range(VSTEP):
            value_sums.give(i * VSTEP + j, grads[j * PAIR:(j + 1) * PAIR])
        for j in range(6):
            @pl.when(i == j // VSTEP + 1)
            def _():
                value_sums.finish(j)
        return carry

    lax.fori_loop(0, PAIRS // VSTEP, value_step, 0)

    early = w_v.at[pl.ds(0, PAIR)]

    def late(n):
        return ds_v.at[pl.ds(pl.multiple_of((n - PAIRS // 2) * PAIR, PAIR), PAIR)]

    def early_col(n):
        return pl.multiple_of(n * ROWS, ROWS)

    def send_on(n):
        for j in range(6):
            @pl.when(n == j + 2)
            def _():
                key_sums.finish(j)

    def first_step(n, carry):
        grads = key_grads(early, early_col(n - 1))
        score_grads(pair_at(n), PAIR, early, early_col(n))
        key_sums.give(n - 1, grads)
        send_on(n)
        return carry

    def second_step(n, carry):
        grads = key_grads(late(n - 1), 0)
        score_grads(pair_at(n), PAIR, late(n), 0)
        key_sums.give(n - 1, grads)
        send_on(n)
        return carry

    score_grads(0, PAIR, early, 0)
    lax.fori_loop(1, PAIRS // 2, first_step, 0)
    grads = key_grads(early, (PAIRS // 2 - 1) * ROWS)
    score_grads(PAIRS // 2 * PAIR, PAIR, late(PAIRS // 2), 0)
    key_sums.give(PAIRS // 2 - 1, grads)
    key_sums.finish(2)
    value_sums.finish(6)
    lax.fori_loop(PAIRS // 2 + 1, PAIRS, second_step, 0)
    grads = key_grads(late(PAIRS - 1), 0)
    score_grads(16 * BLK, BLK, ds_v.at[pl.ds(8 * BLK, BLK)], 0)
    key_sums.give(PAIRS - 1, grads)

    dvn_ref[...] = value_grads(16 * BLK, BLK).astype(bf16)
    dk = key_grads(ds_v.at[pl.ds(8 * BLK, BLK)], 0)
    dkn_ref[...] = (dk * cos_v[...] - pltpu.roll(dk, HD // 2, 1) * sin_v[...]).astype(bf16)
    key_sums.finish(6)

    def query_step(c, carry):
        at = pl.ds(pl.multiple_of(c * 256, 256), 256)
        total = dot(kt_v[:, 8 * BLK:], ds_v[:, at])
        for n in range(PAIRS // 2):
            total += dot(
                kt_v[:, n * PAIR:(n + 1) * PAIR], w_v[0:PAIR, pl.ds(pl.multiple_of(n * ROWS + c * 256, 256), 256)]
            )
        dq_t[:, at] = total
        return carry

    lax.fori_loop(0, ROWS // 256, query_step, 0)
    for p in range(2):
        for h in range(HEADS):
            at = pl.ds((p * HEADS + h) * HD, HD)
            g = (dq_t[:, at] * (l_v[:, at] * SCALE)).T
            for j in range(4):
                k = chunks[4 * p + j]
                x = g[j * CHUNK:(j + 1) * CHUNK, :]
                ta = pl.ds(pl.multiple_of(k * CHUNK, CHUNK), CHUNK)
                y = x * cos_v[ta, :] - pltpu.roll(x, HD // 2, 1) * sin_v[ta, :]
                dq_ref[pl.ds(pl.multiple_of(h * SEQ + k * CHUNK, CHUNK), CHUNK), :] = y.astype(bf16)

    value_sums.finish(7)
    key_sums.finish(7)

    keys.wait_send()
    vals.wait_send()
    for c in do_own + do_relay + pair_relay + last_relay:
        c.wait_send()
    key_sums.wait_send()
    value_sums.wait_send()


def hand_over(*refs):
    for source, result in zip(refs[:5], refs[5:]):
        result[...] = source[...]


def local(out_grad, out_weight, queries, keys_new, values_new, keys_prompt, values_prompt, offsets):
    half = HD // 2
    frequency = np.power(np.float32(1000000.0), -(np.arange(half, dtype=np.float32) / half)).astype(np.float32)
    frequency = jnp.asarray(np.concatenate([frequency, frequency])[None, :])
    q = jnp.transpose(queries[0, :, 0], (1, 0, 2)).reshape(ROWS, HD)
    any_spec = pl.BlockSpec(memory_space=pl.ANY)
    vmem = pl.BlockSpec(memory_space=pltpu.VMEM)
    dma = pltpu.SemaphoreType.DMA
    grads = pl.pallas_call(
        kernel,
        out_shape=(
            jax.ShapeDtypeStruct((ROWS, HD), bf16),
            jax.ShapeDtypeStruct((SEQ, HD), bf16),
            jax.ShapeDtypeStruct((SEQ, HD), bf16),
            jax.ShapeDtypeStruct((BLK, HD), bf16),
            jax.ShapeDtypeStruct((BLK, HD), bf16),
        ),
        in_specs=[any_spec] * 7 + [pl.BlockSpec(memory_space=pltpu.SMEM), vmem],
        out_specs=(vmem,) * 5,
        scratch_shapes=[
            pltpu.VMEM((HEADS * HD, WIDTH), bf16),
            pltpu.VMEM((SEQ, WIDTH), bf16),
            pltpu.VMEM((17 * BLK, HD), bf16),
            pltpu.VMEM((17 * BLK, HD), bf16),
            pltpu.VMEM((HD, 17 * BLK), bf16),
            pltpu.VMEM((ROWS, HD), bf16),
            pltpu.VMEM((SEQ, HD), bf16),
            pltpu.VMEM((HD, ROWS), bf16),
            pltpu.VMEM((ROWS, HD), bf16),
            pltpu.VMEM((HD, ROWS), bf16),
            pltpu.VMEM((ROWS, HD), bf16),
            pltpu.VMEM((17 * BLK, ROWS), f32),
            pltpu.VMEM((17 * BLK, ROWS), bf16),
            pltpu.VMEM((HD, ROWS), f32),
            pltpu.VMEM((HD, ROWS), f32),
            pltpu.VMEM((1, ROWS), f32),
            pltpu.VMEM((1, ROWS), f32),
            pltpu.VMEM((1, ROWS), f32),
            pltpu.VMEM((SEQ, HD), f32),
            pltpu.VMEM((SEQ, HD), f32),
            pltpu.VMEM((9 * BLK, ROWS), bf16),
            pltpu.VMEM((2, HEADS * HD, HD), f32),
            pltpu.VMEM((2, PAIRS, BLK, HD), bf16),
            pltpu.VMEM((2, PAIRS, BLK, HD), bf16),
            pltpu.VMEM((2, 7, BLK, HD), bf16),
            pltpu.VMEM((2, 7, BLK, HD), bf16),
            dma((7,)),
            dma((8,)),
            dma((8,)),
            dma((7,)),
            dma((7,)),
            dma((16,)),
            dma((16,)),
            dma((15,)),
            dma((15,)),
            dma((2, 8)),
            dma((2, 8)),
            dma((2, 7)),
            dma((2, 7)),
        ],
        compiler_params=pltpu.CompilerParams(
            collective_id=0, has_side_effects=True, vmem_limit_bytes=60 * 1024 * 1024
        ),
        name="attention_backward",
    )(
        out_grad[0],
        out_weight.reshape(HEADS * HD, WIDTH),
        q,
        keys_new[0, :, 0],
        values_new[0, :, 0],
        keys_prompt[:, 0],
        values_prompt[:, 0],
        offsets,
        frequency,
    )
    dq, dkn, dvn, dkp, dvp = pl.pallas_call(
        hand_over,
        out_shape=tuple(jax.ShapeDtypeStruct(g.shape, g.dtype) for g in grads),
        in_specs=[vmem] * 5,
        out_specs=(vmem,) * 5,
        name="hand_over",
    )(*grads)
    grad_queries = jnp.transpose(dq.reshape(HEADS, SEQ, HD), (1, 0, 2))[None, :, None]
    return (
        grad_queries,
        dkn[None, :, None],
        dvn[None, :, None],
        dkp[:, None],
        dvp[:, None],
    )


def solution(mesh):
    placed = (
        P("roll", "kvh", None),
        P("kvh", None, None, None),
        P("roll", None, "kvh", None, None),
        P("roll", None, "kvh", None),
        P("roll", None, "kvh", None),
        P("roll", "kvh", None),
        P("roll", "kvh", None),
        P("roll"),
    )
    return jax.shard_map(
        local,
        mesh=mesh,
        in_specs=placed,
        out_specs=(
            P("roll", None, "kvh", None, None),
            P("roll", None, "kvh", None),
            P("roll", None, "kvh", None),
            P("roll", "kvh", None),
            P("roll", "kvh", None),
        ),
        check_vma=False,
    )
```

```python
import functools
import math

import jax
import jax.numpy as jnp
import numpy as np
from jax import lax
from jax.experimental import pallas as pl
from jax.experimental.pallas import tpu as pltpu
from jax.sharding import PartitionSpec as P

MESH = pl.DeviceIdType.MESH
f32 = jnp.float32
bf16 = jnp.bfloat16

HEADS = 5
SEQ = 256
HD = 128
ROWS = HEADS * SEQ
HALF = ROWS // 2
BLK = 256
WIDTH = 5120
PROMPT = 4096
CHUNK = 32
SCALE = HD ** -0.5
SCALE2 = SCALE * math.log2(math.e)
PAIRS = 8
PAIR = 2 * BLK
OWN = slice(16 * BLK, 17 * BLK)


def dot(a, b):
    return lax.dot_general(a, b, (((1,), (0,)), ((), ())), preferred_element_type=f32)


def dot_nt(a, b):
    return lax.dot_general(a, b, (((1,), (1,)), ((), ())), preferred_element_type=f32)


def kernel(
    og_hbm, w_hbm, q_hbm, kn_hbm, vn_hbm, kp_hbm, vp_hbm, off_ref, freq_ref,
    dq_ref, dkn_ref, dvn_ref, dkp_ref, dvp_ref,
    w_v, do_v, kb, vb, kt_v, q_v, kn_v, qt, qp, dot_t, dop, s_v, p_v, o_t, dq_t, m_v, l_v, delta_v,
    cos_v, sin_v, ds_v, ag_v, csend, crecv, zs, zr,
    lsem, ksend, vsend, kfw, vfw, krecv, vrecv, dsend, drecv, cs_sem, cr_sem, zs_sem, zr_sem,
):
    roll = lax.axis_index("roll")
    kvh = lax.axis_index("kvh")
    zz, yh, cc = roll // 4, (roll // 2) % 2, roll % 2
    yl, xx = kvh // 4, kvh % 4

    def dev(dz=0, dyh=0, dc=0, dyl=0, dx=0):
        r = (((zz + dz) % 4) * 2 + (yh + dyh) % 2) * 2 + (cc + dc) % 2
        k = ((yl + dyl) % 2) * 4 + (xx + dx) % 4
        return (r, k)

    core, yhp = dev(dc=1), dev(dyh=1)
    zp, zm, z2 = dev(dz=1), dev(dz=3), dev(dz=2)
    ylp, xp, xm = dev(dyl=1), dev(dx=1), dev(dx=3)

    barrier = pltpu.get_barrier_semaphore()
    for d in (core, yhp, zp, zm, z2, ylp, xp, xm):
        pl.semaphore_signal(barrier, 1, device_id=d, device_id_type=MESH)

    local = [
        pltpu.make_async_copy(kp_hbm, kb.at[pl.ds(15 * BLK, BLK)], lsem.at[0]),
        pltpu.make_async_copy(vp_hbm, vb.at[pl.ds(15 * BLK, BLK)], lsem.at[1]),
        pltpu.make_async_copy(q_hbm, q_v, lsem.at[2]),
        pltpu.make_async_copy(kn_hbm, kn_v, lsem.at[3]),
        pltpu.make_async_copy(vn_hbm, vb.at[pl.ds(16 * BLK, BLK)], lsem.at[4]),
        pltpu.make_async_copy(og_hbm, do_v.at[pl.ds(0, CHUNK)], lsem.at[5]),
        pltpu.make_async_copy(w_hbm, w_v, lsem.at[6]),
    ]
    for c in local:
        c.start()

    pos = (off_ref[0] + PROMPT + lax.broadcasted_iota(jnp.int32, (SEQ, HD), 0)).astype(f32)
    angle = pos * freq_ref[...]
    cos_v[...] = jnp.cos(angle)
    lane = lax.broadcasted_iota(jnp.int32, (SEQ, HD), 1)
    sin_a = jnp.sin(angle)
    sin_v[...] = jnp.where(lane < HD // 2, -sin_a, sin_a)

    pl.semaphore_wait(barrier, 8)

    def remote(src, dst, ssem, rsem, d):
        return pltpu.make_async_remote_copy(
            src_ref=src, dst_ref=dst, send_sem=ssem, recv_sem=rsem, device_id=d, device_id_type=MESH
        )

    def blk(buf, slot):
        return buf.at[pl.ds(slot * BLK, BLK)]

    class Spread:
        def __init__(self, src, buf, send, recv, fsend):
            self.buf, self.send, self.recv, self.fsend = buf, send, recv, fsend
            self.own = [
                self.hop(src, s, i, d) for i, (s, d) in enumerate(((13, yhp), (11, zp), (9, zm), (7, z2), (14, core)))
            ]
            self.relay = [
                self.hop(blk(buf, 13), s, 5 + i, d) for i, (s, d) in enumerate(((5, zp), (3, zm), (1, z2)))
            ]

        def hop(self, src, slot, i, d):
            return remote(src, blk(self.buf, slot), self.send.at[i], self.recv.at[slot], d)

        def forward(self, n):
            return remote(
                blk(self.buf, 2 * n + 1), blk(self.buf, 2 * n), self.fsend.at[n], self.recv.at[2 * n], core
            )

        def take(self, n):
            slot = 2 * n + 1
            self.hop(blk(self.buf, slot), slot, 0, core).wait_recv()
            self.forward(n).start()

        def wait_send(self):
            for c in self.own + self.relay:
                c.wait_send()
            for n in range(PAIRS - 1):
                self.forward(n).wait_send()

    keys = Spread(kp_hbm, kb, ksend, krecv, kfw)
    vals = Spread(vp_hbm, vb, vsend, vrecv, vfw)
    for c in keys.own:
        c.start()

    mid = WIDTH // 2

    def rows(slot, lo=0, size=CHUNK, col=0, width=WIDTH):
        return do_v.at[pl.ds(slot * CHUNK + lo, size), pl.ds(col, width)]

    do_own = [
        remote(og_hbm, rows(1), dsend.at[0], drecv.at[0], ylp),
        remote(og_hbm.at[pl.ds(0, 16)], rows(3, 0, 16), dsend.at[1], drecv.at[1], xp),
        remote(og_hbm.at[pl.ds(16, 16)], rows(2, 16, 16), dsend.at[2], drecv.at[2], xm),
        remote(og_hbm.at[pl.ds(16, 16)], rows(3, 16, 16), dsend.at[9], drecv.at[9], xp),
        remote(og_hbm.at[pl.ds(0, 16)], rows(2, 0, 16), dsend.at[10], drecv.at[10], xm),
    ]
    do_relay = [
        remote(rows(3, 0, 16), rows(4, 0, 16), dsend.at[3], drecv.at[3], xp),
        remote(rows(2, 16, 16), rows(4, 16, 16), dsend.at[4], drecv.at[4], xm),
    ]
    pair_relay = [
        remote(rows(1, 0, CHUNK, col, mid), rows(slot, 0, CHUNK, col, mid), dsend.at[i], drecv.at[i], d)
        for i, col, slot, d in ((5, 0, 6, xp), (6, 0, 5, xm), (7, mid, 6, xp), (8, mid, 5, xm))
    ]
    last_relay = [
        remote(rows(4, lo, 16, col, mid), rows(7, lo, 16, col, mid), dsend.at[i], drecv.at[i], ylp)
        for i, col, lo in ((11, 0, 0), (12, 0, 16), (13, mid, 0), (14, mid, 16))
    ]
    for c in do_own[1:]:
        c.start()

    def kof(dyl, dx):
        return ((yl + dyl) % 2) * 4 + (xx + dx) % 4

    chunks = [kof(0, 0), kof(1, 0), kof(0, 1), kof(0, 3), kof(0, 2), kof(1, 1), kof(1, 3), kof(1, 2)]

    for i in (2, 3, 4):
        local[i].wait()
    kn = kn_v[...].astype(f32)
    kb[OWN, :] = (kn * cos_v[...] + pltpu.roll(kn, HD // 2, 1) * sin_v[...]).astype(bf16)
    for p in range(2):
        for h in range(HEADS):
            parts = []
            for j in range(4):
                k = chunks[4 * p + j]
                x = q_v[pl.ds(pl.multiple_of(h * SEQ + k * CHUNK, CHUNK), CHUNK), :].astype(f32)
                at = pl.ds(pl.multiple_of(k * CHUNK, CHUNK), CHUNK)
                parts.append((x * cos_v[at, :] + pltpu.roll(x, HD // 2, 1) * sin_v[at, :]))
            tile = jnp.concatenate(parts, axis=0)
            qt[:, pl.ds((p * HEADS + h) * HD, HD)] = tile.T.astype(bf16)

    for c in do_own[:1] + vals.own:
        c.start()

    tl = lax.broadcasted_iota(jnp.int32, (1, HD), 1)

    def tokens(p):
        which = tl // CHUNK
        base = jnp.where(
            which == 0,
            chunks[4 * p],
            jnp.where(which == 1, chunks[4 * p + 1], jnp.where(which == 2, chunks[4 * p + 2], chunks[4 * p + 3])),
        )
        return base * CHUNK + tl % CHUNK

    key_at = lax.broadcasted_iota(jnp.int32, (BLK, HD), 0)
    kt_v[:, OWN] = kb[OWN, :].T
    for p in range(2):
        allowed = key_at <= tokens(p)
        for h in range(HEADS):
            at = pl.ds((p * HEADS + h) * HD, HD)
            s = jnp.where(allowed, dot(kb[OWN, :], qt[:, at]), -1e30)
            s_v[OWN, at] = s
            m_v[:, at] = jnp.max(s, axis=0, keepdims=True)

    local[0].wait()

    def pair_at(n):
        return pl.multiple_of(n * PAIR, PAIR)

    def scores_of(n):
        here = pl.ds(pair_at(n), PAIR)
        kblk = kb[here, :]
        kt_v[:, here] = kblk.T
        for c in range(ROWS // 256):
            at = pl.ds(c * 256, 256)
            s = dot(kblk, qt[:, at])
            s_v[here, at] = s
            m_v[:, at] = jnp.maximum(m_v[:, at], jnp.max(s, axis=0, keepdims=True))

    def project(p, part):
        tokens_at = slice(p * HD, (p + 1) * HD)

        def step(i, carry):
            at = pl.ds(pl.multiple_of(part * mid + i * 1280, 1280), 1280)
            ag_v[p] += dot_nt(w_v[:, at], do_v[tokens_at, at])
            return carry

        lax.fori_loop(0, mid // 1280, step, 0)

    ag_v[...] = jnp.zeros_like(ag_v)

    def score_step(i, carry):
        n = PAIRS - 1 - i

        @pl.when(i == 1)
        def _():
            keys.take(6)
            for c in keys.relay:
                c.start()
            do_own[1].wait_recv()
            do_relay[0].start()
            do_own[2].wait_recv()
            do_relay[1].start()
            for j in (5, 4, 3):
                keys.take(j)

        @pl.when(i == 3)
        def _():
            vals.take(6)
            for c in vals.relay:
                c.start()

        @pl.when(i == 4)
        def _():
            do_own[0].wait_recv()
            for c in pair_relay:
                c.start()

        @pl.when(i == 5)
        def _():
            for c in do_relay:
                c.wait_recv()
            for c in last_relay:
                c.start()
            do_own[3].wait_recv()
            do_own[4].wait_recv()
            local[5].wait()
            local[6].wait()
            project(0, 0)
            project(0, 1)
            for j in (2, 1, 0):
                keys.take(j)

        @pl.when(i == 7)
        def _():
            for j in (5, 4, 3):
                vals.take(j)

        keys.forward(n).wait_recv()
        scores_of(n)
        return carry

    lax.fori_loop(0, PAIRS, score_step, 0)

    def output_of(at_row, size, first=False):
        here = pl.ds(at_row, size)
        vt = vb[here, :].T
        for c in range(ROWS // 256):
            at = pl.ds(c * 256, 256)
            e = jnp.exp2(s_v[here, at] * SCALE2 - m_v[:, at] * SCALE2)
            total = jnp.sum(e, axis=0, keepdims=True)
            eb = e.astype(bf16)
            p_v[here, at] = eb
            o = dot(vt, eb)
            if first:
                l_v[:, at] = total
                o_t[:, at] = o
            else:
                l_v[:, at] += total
                o_t[:, at] += o

    output_of(16 * BLK, BLK, True)
    local[1].wait()

    def output_step(i, carry):
        n = PAIRS - 1 - i

        for j, ahead in ((3, 2), (4, 1), (5, 0)):
            @pl.when(i == j)
            def _():
                vals.take(ahead)

        vals.forward(n).wait_recv()
        output_of(pair_at(n), PAIR)
        return carry

    lax.fori_loop(0, PAIRS, output_step, 0)

    for t in range(ROWS // HD):
        at = pl.ds(t * HD, HD)
        inv = 1.0 / l_v[:, at]
        l_v[:, at] = inv
        o_t[:, at] *= inv
        qp[at, :] = (qt[:, at].astype(f32) * (inv * SCALE)).T.astype(bf16)

    def row_terms(p):
        for h in range(HEADS):
            at = pl.ds((p * HEADS + h) * HD, HD)
            g = ag_v[p, h * HD:(h + 1) * HD, :].astype(bf16)
            dot_t[:, at] = g
            gf = g.astype(f32)
            delta_v[:, at] = jnp.sum(gf * o_t[:, at], axis=0, keepdims=True)
            dop[at, :] = (gf * l_v[:, at]).T.astype(bf16)

    def value_grads(at_row, size):
        here = pl.ds(at_row, size)
        return dot(p_v[here, HALF:], dop[HALF:, :]) + s_v[here, HD:2 * HD]

    def score_grads(at_row, size, ds, col):
        here = pl.ds(at_row, size)
        vblk = vb[here, :]
        for c in range(ROWS // 256):
            at = pl.ds(c * 256, 256)
            dp = dot(vblk, dot_t[:, at])
            ds[:, pl.ds(col + c * 256, 256)] = (p_v[here, at].astype(f32) * (dp - delta_v[:, at])).astype(bf16)

    def key_grads(ds, col):
        return dot(ds[:, pl.ds(col, ROWS)], qp[...])

    row_terms(0)

    def first_value_step(i, carry):
        here = pl.ds(pl.multiple_of(i * 2 * PAIR, 2 * PAIR), 2 * PAIR)
        s_v[here, HD:2 * HD] = dot(p_v[here, 0:HALF], dop[0:HALF, :])
        return carry

    lax.fori_loop(0, PAIRS // 2, first_value_step, 0)
    s_v[OWN, HD:2 * HD] = dot(p_v[OWN, 0:HALF], dop[0:HALF, :])
    for c in (pair_relay[0], pair_relay[1], last_relay[0], last_relay[1]):
        c.wait_recv()
    project(1, 0)
    for c in (pair_relay[2], pair_relay[3], last_relay[2], last_relay[3]):
        c.wait_recv()
    project(1, 1)
    row_terms(1)

    def own_half(n):
        return pl.ds(pl.multiple_of(n * PAIR + BLK, BLK), BLK)

    z_dest = (z2, zp, zm, z2, zp, zm, yhp)
    extras_of = ((), (), (), (), (), (), (0, 1, 2), (3, 4, 5, 6))

    class Sums:
        def __init__(self, kind, col, out):
            self.kind, self.col, self.out = kind, pl.ds(col, HD), out

        def core(self, n):
            k = self.kind
            return remote(csend.at[k, n], crecv.at[k, n], cs_sem.at[k, n], cr_sem.at[k, n], core)

        def z(self, j):
            k = self.kind
            return remote(zs.at[k, j], zr.at[k, j], zs_sem.at[k, j], zr_sem.at[k, j], z_dest[j])

        def give(self, n, grads):
            csend[self.kind, n] = grads[0:BLK].astype(bf16)
            self.core(n).start()
            s_v[own_half(n), self.col] = grads[BLK:]

        def finish(self, j):
            self.core(j).wait_recv()
            total = s_v[own_half(j), self.col] + crecv[self.kind, j].astype(f32)
            for e in extras_of[j]:
                self.z(e).wait_recv()
                total = total + zr[self.kind, e].astype(f32)
            if j < 7:
                zs[self.kind, j] = total.astype(bf16)
                self.z(j).start()
            else:
                self.out[...] = total.astype(bf16)

        def wait_send(self):
            for n in range(PAIRS):
                self.core(n).wait_send()
            for j in range(7):
                self.z(j).wait_send()

    key_sums = Sums(0, 0, dkp_ref)
    value_sums = Sums(1, HD, dvp_ref)

    VSTEP = 2

    def value_step(i, carry):
        grads = value_grads(pair_at(i * VSTEP), VSTEP * PAIR)
        for j in range(VSTEP):
            value_sums.give(i * VSTEP + j, grads[j * PAIR:(j + 1) * PAIR])
        for j in range(6):
            @pl.when(i == j // VSTEP + 1)
            def _():
                value_sums.finish(j)
        return carry

    lax.fori_loop(0, PAIRS // VSTEP, value_step, 0)

    early = w_v.at[pl.ds(0, PAIR)]

    def late(n):
        return ds_v.at[pl.ds(pl.multiple_of((n - PAIRS // 2) * PAIR, PAIR), PAIR)]

    def early_col(n):
        return pl.multiple_of(n * ROWS, ROWS)

    def send_on(n):
        for j in range(6):
            @pl.when(n == j + 2)
            def _():
                key_sums.finish(j)

    def first_step(n, carry):
        grads = key_grads(early, early_col(n - 1))
        score_grads(pair_at(n), PAIR, early, early_col(n))
        key_sums.give(n - 1, grads)
        send_on(n)
        return carry

    def second_step(n, carry):
        grads = key_grads(late(n - 1), 0)
        score_grads(pair_at(n), PAIR, late(n), 0)
        key_sums.give(n - 1, grads)
        send_on(n)
        return carry

    score_grads(0, PAIR, early, 0)
    lax.fori_loop(1, PAIRS // 2, first_step, 0)
    grads = key_grads(early, (PAIRS // 2 - 1) * ROWS)
    score_grads(PAIRS // 2 * PAIR, PAIR, late(PAIRS // 2), 0)
    key_sums.give(PAIRS // 2 - 1, grads)
    key_sums.finish(2)
    value_sums.finish(6)
    lax.fori_loop(PAIRS // 2 + 1, PAIRS, second_step, 0)
    grads = key_grads(late(PAIRS - 1), 0)
    score_grads(16 * BLK, BLK, ds_v.at[pl.ds(8 * BLK, BLK)], 0)
    key_sums.give(PAIRS - 1, grads)

    dvn_ref[...] = value_grads(16 * BLK, BLK).astype(bf16)
    dk = key_grads(ds_v.at[pl.ds(8 * BLK, BLK)], 0)
    dkn_ref[...] = (dk * cos_v[...] - pltpu.roll(dk, HD // 2, 1) * sin_v[...]).astype(bf16)
    key_sums.finish(6)

    def query_step(c, carry):
        at = pl.ds(pl.multiple_of(c * 256, 256), 256)
        total = dot(kt_v[:, 8 * BLK:], ds_v[:, at])
        for n in range(PAIRS // 2):
            total += dot(
                kt_v[:, n * PAIR:(n + 1) * PAIR], w_v[0:PAIR, pl.ds(pl.multiple_of(n * ROWS + c * 256, 256), 256)]
            )
        dq_t[:, at] = total
        return carry

    lax.fori_loop(0, ROWS // 256, query_step, 0)
    for p in range(2):
        for h in range(HEADS):
            at = pl.ds((p * HEADS + h) * HD, HD)
            g = (dq_t[:, at] * (l_v[:, at] * SCALE)).T
            for j in range(4):
                k = chunks[4 * p + j]
                x = g[j * CHUNK:(j + 1) * CHUNK, :]
                ta = pl.ds(pl.multiple_of(k * CHUNK, CHUNK), CHUNK)
                y = x * cos_v[ta, :] - pltpu.roll(x, HD // 2, 1) * sin_v[ta, :]
                dq_ref[pl.ds(pl.multiple_of(h * SEQ + k * CHUNK, CHUNK), CHUNK), :] = y.astype(bf16)

    value_sums.finish(7)
    key_sums.finish(7)

    keys.wait_send()
    vals.wait_send()
    for c in do_own + do_relay + pair_relay + last_relay:
        c.wait_send()
    key_sums.wait_send()
    value_sums.wait_send()


def hand_over(*refs):
    for source, result in zip(refs[:5], refs[5:]):
        result[...] = source[...]


def local(out_grad, out_weight, queries, keys_new, values_new, keys_prompt, values_prompt, offsets):
    half = HD // 2
    frequency = np.power(np.float32(1000000.0), -(np.arange(half, dtype=np.float32) / half)).astype(np.float32)
    frequency = jnp.asarray(np.concatenate([frequency, frequency])[None, :])
    q = jnp.transpose(queries[0, :, 0], (1, 0, 2)).reshape(ROWS, HD)
    any_spec = pl.BlockSpec(memory_space=pl.ANY)
    vmem = pl.BlockSpec(memory_space=pltpu.VMEM)
    dma = pltpu.SemaphoreType.DMA
    grads = pl.pallas_call(
        kernel,
        out_shape=(
            jax.ShapeDtypeStruct((ROWS, HD), bf16),
            jax.ShapeDtypeStruct((SEQ, HD), bf16),
            jax.ShapeDtypeStruct((SEQ, HD), bf16),
            jax.ShapeDtypeStruct((BLK, HD), bf16),
            jax.ShapeDtypeStruct((BLK, HD), bf16),
        ),
        in_specs=[any_spec] * 7 + [pl.BlockSpec(memory_space=pltpu.SMEM), vmem],
        out_specs=(vmem,) * 5,
        scratch_shapes=[
            pltpu.VMEM((HEADS * HD, WIDTH), bf16),
            pltpu.VMEM((SEQ, WIDTH), bf16),
            pltpu.VMEM((17 * BLK, HD), bf16),
            pltpu.VMEM((17 * BLK, HD), bf16),
            pltpu.VMEM((HD, 17 * BLK), bf16),
            pltpu.VMEM((ROWS, HD), bf16),
            pltpu.VMEM((SEQ, HD), bf16),
            pltpu.VMEM((HD, ROWS), bf16),
            pltpu.VMEM((ROWS, HD), bf16),
            pltpu.VMEM((HD, ROWS), bf16),
            pltpu.VMEM((ROWS, HD), bf16),
            pltpu.VMEM((17 * BLK, ROWS), f32),
            pltpu.VMEM((17 * BLK, ROWS), bf16),
            pltpu.VMEM((HD, ROWS), f32),
            pltpu.VMEM((HD, ROWS), f32),
            pltpu.VMEM((1, ROWS), f32),
            pltpu.VMEM((1, ROWS), f32),
            pltpu.VMEM((1, ROWS), f32),
            pltpu.VMEM((SEQ, HD), f32),
            pltpu.VMEM((SEQ, HD), f32),
            pltpu.VMEM((9 * BLK, ROWS), bf16),
            pltpu.VMEM((2, HEADS * HD, HD), f32),
            pltpu.VMEM((2, PAIRS, BLK, HD), bf16),
            pltpu.VMEM((2, PAIRS, BLK, HD), bf16),
            pltpu.VMEM((2, 7, BLK, HD), bf16),
            pltpu.VMEM((2, 7, BLK, HD), bf16),
            dma((7,)),
            dma((8,)),
            dma((8,)),
            dma((7,)),
            dma((7,)),
            dma((16,)),
            dma((16,)),
            dma((15,)),
            dma((15,)),
            dma((2, 8)),
            dma((2, 8)),
            dma((2, 7)),
            dma((2, 7)),
        ],
        compiler_params=pltpu.CompilerParams(
            collective_id=0, has_side_effects=True, vmem_limit_bytes=60 * 1024 * 1024
        ),
        name="attention_backward",
    )(
        out_grad[0],
        out_weight.reshape(HEADS * HD, WIDTH),
        q,
        keys_new[0, :, 0],
        values_new[0, :, 0],
        keys_prompt[:, 0],
        values_prompt[:, 0],
        offsets,
        frequency,
    )
    dq, dkn, dvn, dkp, dvp = pl.pallas_call(
        hand_over,
        out_shape=tuple(jax.ShapeDtypeStruct(g.shape, g.dtype) for g in grads),
        in_specs=[vmem] * 5,
        out_specs=(vmem,) * 5,
        name="hand_over",
    )(*grads)
    grad_queries = jnp.transpose(dq.reshape(HEADS, SEQ, HD), (1, 0, 2))[None, :, None]
    return (
        grad_queries,
        dkn[None, :, None],
        dvn[None, :, None],
        dkp[:, None],
        dvp[:, None],
    )


def solution(mesh):
    placed = (
        P("roll", "kvh", None),
        P("kvh", None, None, None),
        P("roll", None, "kvh", None, None),
        P("roll", None, "kvh", None),
        P("roll", None, "kvh", None),
        P("roll", "kvh", None),
        P("roll", "kvh", None),
        P("roll"),
    )
    return jax.shard_map(
        local,
        mesh=mesh,
        in_specs=placed,
        out_specs=(
            P("roll", None, "kvh", None, None),
            P("roll", None, "kvh", None),
            P("roll", None, "kvh", None),
            P("roll", "kvh", None),
            P("roll", "kvh", None),
        ),
        check_vma=False,
    )
```

```python
import functools
import math

import jax
import jax.numpy as jnp
import numpy as np
from jax import lax
from jax.experimental import pallas as pl
from jax.experimental.pallas import tpu as pltpu
from jax.sharding import PartitionSpec as P

MESH = pl.DeviceIdType.MESH
f32 = jnp.float32
bf16 = jnp.bfloat16

HEADS = 5
SEQ = 256
HD = 128
ROWS = HEADS * SEQ
BLK = 256
WIDTH = 5120
PROMPT = 4096
CHUNK = 32
SCALE = HD ** -0.5
SCALE2 = SCALE * math.log2(math.e)
PAIRS = 8
PAIR = 2 * BLK
OWN = slice(16 * BLK, 17 * BLK)


def dot(a, b):
    return lax.dot_general(a, b, (((1,), (0,)), ((), ())), preferred_element_type=f32)


def dot_nt(a, b):
    return lax.dot_general(a, b, (((1,), (1,)), ((), ())), preferred_element_type=f32)


def kernel(
    og_hbm, w_hbm, q_hbm, kn_hbm, vn_hbm, kp_hbm, vp_hbm, off_ref, freq_ref,
    dq_ref, dkn_ref, dvn_ref, dkp_ref, dvp_ref,
    w_v, do_v, kb, vb, kt_v, q_v, kn_v, qt, qp, dot_t, dop, s_v, p_v, o_t, dq_t, m_v, l_v, delta_v,
    cos_v, sin_v, ds_v, ag_v, csend, crecv, zs, zr,
    lsem, ksend, vsend, kfw, vfw, krecv, vrecv, dsend, drecv, cs_sem, cr_sem, zs_sem, zr_sem,
):
    roll = lax.axis_index("roll")
    kvh = lax.axis_index("kvh")
    zz, yh, cc = roll // 4, (roll // 2) % 2, roll % 2
    yl, xx = kvh // 4, kvh % 4

    def dev(dz=0, dyh=0, dc=0, dyl=0, dx=0):
        r = (((zz + dz) % 4) * 2 + (yh + dyh) % 2) * 2 + (cc + dc) % 2
        k = ((yl + dyl) % 2) * 4 + (xx + dx) % 4
        return (r, k)

    core, yhp = dev(dc=1), dev(dyh=1)
    zp, zm, z2 = dev(dz=1), dev(dz=3), dev(dz=2)
    ylp, xp, xm = dev(dyl=1), dev(dx=1), dev(dx=3)

    barrier = pltpu.get_barrier_semaphore()
    for d in (core, yhp, zp, zm, z2, ylp, xp, xm):
        pl.semaphore_signal(barrier, 1, device_id=d, device_id_type=MESH)

    local = [
        pltpu.make_async_copy(kp_hbm, kb.at[pl.ds(15 * BLK, BLK)], lsem.at[0]),
        pltpu.make_async_copy(vp_hbm, vb.at[pl.ds(15 * BLK, BLK)], lsem.at[1]),
        pltpu.make_async_copy(q_hbm, q_v, lsem.at[2]),
        pltpu.make_async_copy(kn_hbm, kn_v, lsem.at[3]),
        pltpu.make_async_copy(vn_hbm, vb.at[pl.ds(16 * BLK, BLK)], lsem.at[4]),
        pltpu.make_async_copy(og_hbm, do_v.at[pl.ds(0, CHUNK)], lsem.at[5]),
        pltpu.make_async_copy(w_hbm, w_v, lsem.at[6]),
    ]
    for c in local:
        c.start()

    pos = (off_ref[0] + PROMPT + lax.broadcasted_iota(jnp.int32, (SEQ, HD), 0)).astype(f32)
    angle = pos * freq_ref[...]
    cos_v[...] = jnp.cos(angle)
    lane = lax.broadcasted_iota(jnp.int32, (SEQ, HD), 1)
    sin_a = jnp.sin(angle)
    sin_v[...] = jnp.where(lane < HD // 2, -sin_a, sin_a)

    pl.semaphore_wait(barrier, 8)

    def remote(src, dst, ssem, rsem, d):
        return pltpu.make_async_remote_copy(
            src_ref=src, dst_ref=dst, send_sem=ssem, recv_sem=rsem, device_id=d, device_id_type=MESH
        )

    def blk(buf, slot):
        return buf.at[pl.ds(slot * BLK, BLK)]

    class Spread:
        def __init__(self, src, buf, send, recv, fsend):
            self.buf, self.send, self.recv, self.fsend = buf, send, recv, fsend
            self.own = [
                self.hop(src, s, i, d) for i, (s, d) in enumerate(((13, yhp), (11, zp), (9, zm), (7, z2), (14, core)))
            ]
            self.relay = [
                self.hop(blk(buf, 13), s, 5 + i, d) for i, (s, d) in enumerate(((5, zp), (3, zm), (1, z2)))
            ]

        def hop(self, src, slot, i, d):
            return remote(src, blk(self.buf, slot), self.send.at[i], self.recv.at[slot], d)

        def forward(self, n):
            return remote(
                blk(self.buf, 2 * n + 1), blk(self.buf, 2 * n), self.fsend.at[n], self.recv.at[2 * n], core
            )

        def take(self, n):
            slot = 2 * n + 1
            self.hop(blk(self.buf, slot), slot, 0, core).wait_recv()
            self.forward(n).start()

        def wait_send(self):
            for c in self.own + self.relay:
                c.wait_send()
            for n in range(PAIRS - 1):
                self.forward(n).wait_send()

    keys = Spread(kp_hbm, kb, ksend, krecv, kfw)
    vals = Spread(vp_hbm, vb, vsend, vrecv, vfw)
    for c in keys.own:
        c.start()

    mid = WIDTH // 2

    def rows(slot, lo=0, size=CHUNK, col=0, width=WIDTH):
        return do_v.at[pl.ds(slot * CHUNK + lo, size), pl.ds(col, width)]

    do_own = [
        remote(og_hbm, rows(1), dsend.at[0], drecv.at[0], ylp),
        remote(og_hbm.at[pl.ds(0, 16)], rows(3, 0, 16), dsend.at[1], drecv.at[1], xp),
        remote(og_hbm.at[pl.ds(16, 16)], rows(2, 16, 16), dsend.at[2], drecv.at[2], xm),
        remote(og_hbm.at[pl.ds(16, 16)], rows(3, 16, 16), dsend.at[9], drecv.at[9], xp),
        remote(og_hbm.at[pl.ds(0, 16)], rows(2, 0, 16), dsend.at[10], drecv.at[10], xm),
    ]
    do_relay = [
        remote(rows(3, 0, 16), rows(4, 0, 16), dsend.at[3], drecv.at[3], xp),
        remote(rows(2, 16, 16), rows(4, 16, 16), dsend.at[4], drecv.at[4], xm),
    ]
    pair_relay = [
        remote(rows(1, 0, CHUNK, col, mid), rows(slot, 0, CHUNK, col, mid), dsend.at[i], drecv.at[i], d)
        for i, col, slot, d in ((5, 0, 6, xp), (6, 0, 5, xm), (7, mid, 6, xp), (8, mid, 5, xm))
    ]
    last_relay = [
        remote(rows(4, lo, 16, col, mid), rows(7, lo, 16, col, mid), dsend.at[i], drecv.at[i], ylp)
        for i, col, lo in ((11, 0, 0), (12, 0, 16), (13, mid, 0), (14, mid, 16))
    ]
    for c in do_own[1:]:
        c.start()

    def kof(dyl, dx):
        return ((yl + dyl) % 2) * 4 + (xx + dx) % 4

    chunks = [kof(0, 0), kof(1, 0), kof(0, 1), kof(0, 3), kof(0, 2), kof(1, 1), kof(1, 3), kof(1, 2)]

    for i in (2, 3, 4):
        local[i].wait()
    kn = kn_v[...].astype(f32)
    kb[OWN, :] = (kn * cos_v[...] + pltpu.roll(kn, HD // 2, 1) * sin_v[...]).astype(bf16)
    for p in range(2):
        for h in range(HEADS):
            parts = []
            for j in range(4):
                k = chunks[4 * p + j]
                x = q_v[pl.ds(pl.multiple_of(h * SEQ + k * CHUNK, CHUNK), CHUNK), :].astype(f32)
                at = pl.ds(pl.multiple_of(k * CHUNK, CHUNK), CHUNK)
                parts.append((x * cos_v[at, :] + pltpu.roll(x, HD // 2, 1) * sin_v[at, :]))
            tile = jnp.concatenate(parts, axis=0)
            qt[:, pl.ds((p * HEADS + h) * HD, HD)] = tile.T.astype(bf16)

    for c in do_own[:1] + vals.own:
        c.start()

    tl = lax.broadcasted_iota(jnp.int32, (1, HD), 1)

    def tokens(p):
        which = tl // CHUNK
        base = jnp.where(
            which == 0,
            chunks[4 * p],
            jnp.where(which == 1, chunks[4 * p + 1], jnp.where(which == 2, chunks[4 * p + 2], chunks[4 * p + 3])),
        )
        return base * CHUNK + tl % CHUNK

    key_at = lax.broadcasted_iota(jnp.int32, (BLK, HD), 0)
    kt_v[:, OWN] = kb[OWN, :].T
    for p in range(2):
        allowed = key_at <= tokens(p)
        for h in range(HEADS):
            at = pl.ds((p * HEADS + h) * HD, HD)
            s = jnp.where(allowed, dot(kb[OWN, :], qt[:, at]), -1e30)
            s_v[OWN, at] = s
            m_v[:, at] = jnp.max(s, axis=0, keepdims=True)

    local[0].wait()

    def pair_at(n):
        return pl.multiple_of(n * PAIR, PAIR)

    def scores_of(n):
        here = pl.ds(pair_at(n), PAIR)
        kblk = kb[here, :]
        kt_v[:, here] = kblk.T
        for c in range(ROWS // 256):
            at = pl.ds(c * 256, 256)
            s = dot(kblk, qt[:, at])
            s_v[here, at] = s
            m_v[:, at] = jnp.maximum(m_v[:, at], jnp.max(s, axis=0, keepdims=True))

    def project(p, part):
        tokens_at = slice(p * HD, (p + 1) * HD)

        def step(i, carry):
            at = pl.ds(pl.multiple_of(part * mid + i * 1280, 1280), 1280)
            ag_v[p] += dot_nt(w_v[:, at], do_v[tokens_at, at])
            return carry

        lax.fori_loop(0, mid // 1280, step, 0)

    ag_v[...] = jnp.zeros_like(ag_v)

    def score_step(i, carry):
        n = PAIRS - 1 - i

        @pl.when(i == 1)
        def _():
            keys.take(6)
            for c in keys.relay:
                c.start()
            do_own[1].wait_recv()
            do_relay[0].start()
            do_own[2].wait_recv()
            do_relay[1].start()
            for j in (5, 4, 3):
                keys.take(j)

        @pl.when(i == 4)
        def _():
            vals.take(6)
            for c in vals.relay:
                c.start()

        @pl.when(i == 5)
        def _():
            do_own[0].wait_recv()
            for c in pair_relay:
                c.start()
            do_own[3].wait_recv()
            do_own[4].wait_recv()
            local[5].wait()
            local[6].wait()
            project(0, 0)
            project(0, 1)
            for c in do_relay:
                c.wait_recv()
            for c in last_relay:
                c.start()
            for j in (2, 1, 0):
                keys.take(j)

        @pl.when(i == 7)
        def _():
            for j in (5, 4, 3):
                vals.take(j)

        keys.forward(n).wait_recv()
        scores_of(n)
        return carry

    lax.fori_loop(0, PAIRS, score_step, 0)

    def output_of(at_row, size, first=False):
        here = pl.ds(at_row, size)
        vt = vb[here, :].T
        for c in range(ROWS // 256):
            at = pl.ds(c * 256, 256)
            e = jnp.exp2(s_v[here, at] * SCALE2 - m_v[:, at] * SCALE2)
            total = jnp.sum(e, axis=0, keepdims=True)
            eb = e.astype(bf16)
            p_v[here, at] = eb
            o = dot(vt, eb)
            if first:
                l_v[:, at] = total
                o_t[:, at] = o
            else:
                l_v[:, at] += total
                o_t[:, at] += o

    output_of(16 * BLK, BLK, True)
    local[1].wait()

    def output_step(i, carry):
        n = PAIRS - 1 - i

        for j, ahead in ((3, 2), (4, 1), (5, 0)):
            @pl.when(i == j)
            def _():
                vals.take(ahead)

        vals.forward(n).wait_recv()
        output_of(pair_at(n), PAIR)
        return carry

    lax.fori_loop(0, PAIRS, output_step, 0)

    for t in range(ROWS // HD):
        at = pl.ds(t * HD, HD)
        inv = 1.0 / l_v[:, at]
        l_v[:, at] = inv
        o_t[:, at] *= inv
        qp[at, :] = (qt[:, at].astype(f32) * (inv * SCALE)).T.astype(bf16)

    def row_terms(p):
        for h in range(HEADS):
            at = pl.ds((p * HEADS + h) * HD, HD)
            g = ag_v[p, h * HD:(h + 1) * HD, :].astype(bf16)
            dot_t[:, at] = g
            gf = g.astype(f32)
            delta_v[:, at] = jnp.sum(gf * o_t[:, at], axis=0, keepdims=True)
            dop[at, :] = (gf * l_v[:, at]).T.astype(bf16)

    def value_grads(at_row, size):
        return dot(p_v[pl.ds(at_row, size), :], dop[...])

    def score_grads(at_row, size, ds, col):
        here = pl.ds(at_row, size)
        vblk = vb[here, :]
        for c in range(ROWS // 256):
            at = pl.ds(c * 256, 256)
            dp = dot(vblk, dot_t[:, at])
            ds[:, pl.ds(col + c * 256, 256)] = (p_v[here, at].astype(f32) * (dp - delta_v[:, at])).astype(bf16)

    def key_grads(ds, col):
        return dot(ds[:, pl.ds(col, ROWS)], qp[...])

    row_terms(0)
    for c in (pair_relay[0], pair_relay[1], last_relay[0], last_relay[1]):
        c.wait_recv()
    project(1, 0)
    for c in (pair_relay[2], pair_relay[3], last_relay[2], last_relay[3]):
        c.wait_recv()
    project(1, 1)
    row_terms(1)

    def own_half(n):
        return pl.ds(pl.multiple_of(n * PAIR + BLK, BLK), BLK)

    z_dest = (z2, zp, zm, z2, zp, zm, yhp)
    extras_of = ((), (), (), (), (), (), (0, 1, 2), (3, 4, 5, 6))

    class Sums:
        def __init__(self, kind, col, out):
            self.kind, self.col, self.out = kind, pl.ds(col, HD), out

        def core(self, n):
            k = self.kind
            return remote(csend.at[k, n], crecv.at[k, n], cs_sem.at[k, n], cr_sem.at[k, n], core)

        def z(self, j):
            k = self.kind
            return remote(zs.at[k, j], zr.at[k, j], zs_sem.at[k, j], zr_sem.at[k, j], z_dest[j])

        def give(self, n, grads):
            csend[self.kind, n] = grads[0:BLK].astype(bf16)
            self.core(n).start()
            s_v[own_half(n), self.col] = grads[BLK:]

        def finish(self, j):
            self.core(j).wait_recv()
            total = s_v[own_half(j), self.col] + crecv[self.kind, j].astype(f32)
            for e in extras_of[j]:
                self.z(e).wait_recv()
                total = total + zr[self.kind, e].astype(f32)
            if j < 7:
                zs[self.kind, j] = total.astype(bf16)
                self.z(j).start()
            else:
                self.out[...] = total.astype(bf16)

        def wait_send(self):
            for n in range(PAIRS):
                self.core(n).wait_send()
            for j in range(7):
                self.z(j).wait_send()

    key_sums = Sums(0, 0, dkp_ref)
    value_sums = Sums(1, HD, dvp_ref)

    VSTEP = 2

    def value_step(i, carry):
        grads = value_grads(pair_at(i * VSTEP), VSTEP * PAIR)
        for j in range(VSTEP):
            value_sums.give(i * VSTEP + j, grads[j * PAIR:(j + 1) * PAIR])
        for j in range(6):
            @pl.when(i == j // VSTEP + 1)
            def _():
                value_sums.finish(j)
        return carry

    lax.fori_loop(0, PAIRS // VSTEP, value_step, 0)

    early = w_v.at[pl.ds(0, PAIR)]

    def late(n):
        return ds_v.at[pl.ds(pl.multiple_of((n - PAIRS // 2) * PAIR, PAIR), PAIR)]

    def early_col(n):
        return pl.multiple_of(n * ROWS, ROWS)

    def send_on(n):
        for j in range(6):
            @pl.when(n == j + 2)
            def _():
                key_sums.finish(j)

    def first_step(n, carry):
        grads = key_grads(early, early_col(n - 1))
        score_grads(pair_at(n), PAIR, early, early_col(n))
        key_sums.give(n - 1, grads)
        send_on(n)
        return carry

    def second_step(n, carry):
        grads = key_grads(late(n - 1), 0)
        score_grads(pair_at(n), PAIR, late(n), 0)
        key_sums.give(n - 1, grads)
        send_on(n)
        return carry

    score_grads(0, PAIR, early, 0)
    lax.fori_loop(1, PAIRS // 2, first_step, 0)
    grads = key_grads(early, (PAIRS // 2 - 1) * ROWS)
    score_grads(PAIRS // 2 * PAIR, PAIR, late(PAIRS // 2), 0)
    key_sums.give(PAIRS // 2 - 1, grads)
    key_sums.finish(2)
    value_sums.finish(6)
    lax.fori_loop(PAIRS // 2 + 1, PAIRS, second_step, 0)
    grads = key_grads(late(PAIRS - 1), 0)
    score_grads(16 * BLK, BLK, ds_v.at[pl.ds(8 * BLK, BLK)], 0)
    key_sums.give(PAIRS - 1, grads)

    dvn_ref[...] = value_grads(16 * BLK, BLK).astype(bf16)
    dk = key_grads(ds_v.at[pl.ds(8 * BLK, BLK)], 0)
    dkn_ref[...] = (dk * cos_v[...] - pltpu.roll(dk, HD // 2, 1) * sin_v[...]).astype(bf16)
    key_sums.finish(6)

    def query_step(c, carry):
        at = pl.ds(pl.multiple_of(c * 256, 256), 256)
        total = dot(kt_v[:, 8 * BLK:], ds_v[:, at])
        for n in range(PAIRS // 2):
            total += dot(
                kt_v[:, n * PAIR:(n + 1) * PAIR], w_v[0:PAIR, pl.ds(pl.multiple_of(n * ROWS + c * 256, 256), 256)]
            )
        dq_t[:, at] = total
        return carry

    lax.fori_loop(0, ROWS // 256, query_step, 0)
    for p in range(2):
        for h in range(HEADS):
            at = pl.ds((p * HEADS + h) * HD, HD)
            g = (dq_t[:, at] * (l_v[:, at] * SCALE)).T
            for j in range(4):
                k = chunks[4 * p + j]
                x = g[j * CHUNK:(j + 1) * CHUNK, :]
                ta = pl.ds(pl.multiple_of(k * CHUNK, CHUNK), CHUNK)
                y = x * cos_v[ta, :] - pltpu.roll(x, HD // 2, 1) * sin_v[ta, :]
                dq_ref[pl.ds(pl.multiple_of(h * SEQ + k * CHUNK, CHUNK), CHUNK), :] = y.astype(bf16)

    value_sums.finish(7)
    key_sums.finish(7)

    keys.wait_send()
    vals.wait_send()
    for c in do_own + do_relay + pair_relay + last_relay:
        c.wait_send()
    key_sums.wait_send()
    value_sums.wait_send()


def hand_over(*refs):
    for source, result in zip(refs[:5], refs[5:]):
        result[...] = source[...]


def local(out_grad, out_weight, queries, keys_new, values_new, keys_prompt, values_prompt, offsets):
    half = HD // 2
    frequency = np.power(np.float32(1000000.0), -(np.arange(half, dtype=np.float32) / half)).astype(np.float32)
    frequency = jnp.asarray(np.concatenate([frequency, frequency])[None, :])
    q = jnp.transpose(queries[0, :, 0], (1, 0, 2)).reshape(ROWS, HD)
    any_spec = pl.BlockSpec(memory_space=pl.ANY)
    vmem = pl.BlockSpec(memory_space=pltpu.VMEM)
    dma = pltpu.SemaphoreType.DMA
    grads = pl.pallas_call(
        kernel,
        out_shape=(
            jax.ShapeDtypeStruct((ROWS, HD), bf16),
            jax.ShapeDtypeStruct((SEQ, HD), bf16),
            jax.ShapeDtypeStruct((SEQ, HD), bf16),
            jax.ShapeDtypeStruct((BLK, HD), bf16),
            jax.ShapeDtypeStruct((BLK, HD), bf16),
        ),
        in_specs=[any_spec] * 7 + [pl.BlockSpec(memory_space=pltpu.SMEM), vmem],
        out_specs=(vmem,) * 5,
        scratch_shapes=[
            pltpu.VMEM((HEADS * HD, WIDTH), bf16),
            pltpu.VMEM((SEQ, WIDTH), bf16),
            pltpu.VMEM((17 * BLK, HD), bf16),
            pltpu.VMEM((17 * BLK, HD), bf16),
            pltpu.VMEM((HD, 17 * BLK), bf16),
            pltpu.VMEM((ROWS, HD), bf16),
            pltpu.VMEM((SEQ, HD), bf16),
            pltpu.VMEM((HD, ROWS), bf16),
            pltpu.VMEM((ROWS, HD), bf16),
            pltpu.VMEM((HD, ROWS), bf16),
            pltpu.VMEM((ROWS, HD), bf16),
            pltpu.VMEM((17 * BLK, ROWS), f32),
            pltpu.VMEM((17 * BLK, ROWS), bf16),
            pltpu.VMEM((HD, ROWS), f32),
            pltpu.VMEM((HD, ROWS), f32),
            pltpu.VMEM((1, ROWS), f32),
            pltpu.VMEM((1, ROWS), f32),
            pltpu.VMEM((1, ROWS), f32),
            pltpu.VMEM((SEQ, HD), f32),
            pltpu.VMEM((SEQ, HD), f32),
            pltpu.VMEM((9 * BLK, ROWS), bf16),
            pltpu.VMEM((2, HEADS * HD, HD), f32),
            pltpu.VMEM((2, PAIRS, BLK, HD), bf16),
            pltpu.VMEM((2, PAIRS, BLK, HD), bf16),
            pltpu.VMEM((2, 7, BLK, HD), bf16),
            pltpu.VMEM((2, 7, BLK, HD), bf16),
            dma((7,)),
            dma((8,)),
            dma((8,)),
            dma((7,)),
            dma((7,)),
            dma((16,)),
            dma((16,)),
            dma((15,)),
            dma((15,)),
            dma((2, 8)),
            dma((2, 8)),
            dma((2, 7)),
            dma((2, 7)),
        ],
        compiler_params=pltpu.CompilerParams(
            collective_id=0, has_side_effects=True, vmem_limit_bytes=60 * 1024 * 1024
        ),
        name="attention_backward",
    )(
        out_grad[0],
        out_weight.reshape(HEADS * HD, WIDTH),
        q,
        keys_new[0, :, 0],
        values_new[0, :, 0],
        keys_prompt[:, 0],
        values_prompt[:, 0],
        offsets,
        frequency,
    )
    dq, dkn, dvn, dkp, dvp = pl.pallas_call(
        hand_over,
        out_shape=tuple(jax.ShapeDtypeStruct(g.shape, g.dtype) for g in grads),
        in_specs=[vmem] * 5,
        out_specs=(vmem,) * 5,
        name="hand_over",
    )(*grads)
    grad_queries = jnp.transpose(dq.reshape(HEADS, SEQ, HD), (1, 0, 2))[None, :, None]
    return (
        grad_queries,
        dkn[None, :, None],
        dvn[None, :, None],
        dkp[:, None],
        dvp[:, None],
    )


def solution(mesh):
    placed = (
        P("roll", "kvh", None),
        P("kvh", None, None, None),
        P("roll", None, "kvh", None, None),
        P("roll", None, "kvh", None),
        P("roll", None, "kvh", None),
        P("roll", "kvh", None),
        P("roll", "kvh", None),
        P("roll"),
    )
    return jax.shard_map(
        local,
        mesh=mesh,
        in_specs=placed,
        out_specs=(
            P("roll", None, "kvh", None, None),
            P("roll", None, "kvh", None),
            P("roll", None, "kvh", None),
            P("roll", "kvh", None),
            P("roll", "kvh", None),
        ),
        check_vma=False,
    )
```
